128 devices in a mesh: seq: 8 (over z, y_hi), shard: 16 (over x, y_lo, core).
Axes of the slice: x: 4, y: 4 (y_hi: 2, y_lo: 2; y = y_hi * 2 + y_lo), z: 4, core: 2. Of those that a mesh axis runs over, the one named last changes fastest.
Arguments:
- images: bfloat16 [32, 56, 14, 512], P('shard', 'seq'), may hold values from -6 to 6
- norm_gain: bfloat16 [2, 2, 512], P(None, None, 'shard'), may hold values from 0.099609375 to 1.8984375
- norm_shift: bfloat16 [2, 2, 512], P(None, None, 'shard'), may hold values from -3 to 3
- qkv_weight: bfloat16 [2, 512, 1536], P(None, 'shard'), may hold values from -0.25 to 0.25
- qkv_bias: bfloat16 [2, 2, 512], P(None, None, 'shard'), may hold values from -3 to 3
- rel_table: bfloat16 [2, 16, 169], P(None, 'shard'), may hold values from -4 to 4
- proj_weight: bfloat16 [2, 512, 512], P(None, 'shard'), may hold values from -1 to 1
- out_bias: bfloat16 [2, 2, 512], P(None, None, 'shard'), may hold values from -3 to 3
- fc1_weight: bfloat16 [2, 512, 2048], P(None, 'shard'), may hold values from -0.25 to 0.25
- fc1_bias: bfloat16 [2, 2048], P(None, 'shard'), may hold values from -3 to 3
- fc2_weight: bfloat16 [2, 2048, 512], P(None, 'shard'), may hold values from -0.125 to 0.125
- cotangent: bfloat16 [32, 56, 14, 512], P('shard', 'seq'), may hold values from -6 to 6
Outputs:
- outputs: float32 [32, 56, 14, 512], P('shard', 'seq')
- input_grad: float32 [32, 56, 14, 512], P('shard', 'seq')
- norm_gain_grad: float32 [2, 2, 512], P(None, None, 'shard')
- norm_shift_grad: float32 [2, 2, 512], P(None, None, 'shard')
- qkv_weight_grad: float32 [2, 512, 1536], P(None, 'shard')
- qkv_bias_grad: float32 [2, 2, 512], P(None, None, 'shard')
- rel_table_grad: float32 [2, 16, 169], P(None, 'shard')
- proj_weight_grad: float32 [2, 512, 512], P(None, 'shard')
- out_bias_grad: float32 [2, 2, 512], P(None, None, 'shard')
- fc1_weight_grad: float32 [2, 512, 2048], P(None, 'shard')
- fc1_bias_grad: float32 [2, 2048], P(None, 'shard')
- fc2_weight_grad: float32 [2, 2048, 512], P(None, 'shard')
The draws below stay inside these ranges and needn't reach their ends.
All inputs are finite; a program needn't handle non-finite values.
Results may differ from the reference program's by a relative error of at most 0.025.
Values may be sent and summed in bfloat16 or wider, within the bound.
No kernel may reach another device: no remote copies, remote signals or barrier semaphores. Data moves between devices by JAX's collectives and lax.ppermute only.
A program may use at most 128 MiB of HBM per device.

```python
import jax
import jax.numpy as jnp
from jax import lax

C = 512
HEADS = 16
HD = 32
MLP = 2048
WIN = 7
SHIFT = 3
RELS = 169
LAYERS = 2
GRID_ROWS = 56
COLS = 14
IMAGES = 32


def steps_of(key, shape, split, low, high):
    def one(position, blocks):
        draws = jax.random.uniform(jax.random.fold_in(jax.random.fold_in(key, 6), position), (blocks,), jnp.float32, low / len(split), high / len(split))
        return jnp.repeat(jnp.exp(draws), shape[position] // blocks).reshape((-1,) + (1,) * (len(shape) - position - 1))

    loudness = one(*split[0])
    for cut in split[1:]:
        loudness = loudness * one(*cut)
    return loudness


def gaussian(own_key, dims, scale, bound, cuts=(), held_as=jnp.bfloat16):
    drawn = jax.random.normal(own_key, dims, jnp.float32) * scale
    if len(cuts) > 0:
        drawn = steps_of(own_key, dims, cuts, -0.22, 0.18) * drawn
    return jnp.clip(drawn, min=-bound, max=bound).astype(held_as)


def setup_inputs(seed: int = 0) -> dict:
    key_list = jax.random.split(jax.random.key(seed), 13)
    return {
        "images": gaussian(key_list[0], (IMAGES, GRID_ROWS, COLS, C), 1.0, 6.0, ((0, 16), (1, 8))),
        "norm_gain": jnp.clip(1.0 + 0.18 * jax.random.normal(key_list[1], (LAYERS, 2, C), jnp.float32), 0.099609375, 1.8984375).astype(jnp.bfloat16),
        "norm_shift": gaussian(key_list[2], (LAYERS, 2, C), 0.5, 3.0, ((2, 16),)),
        "qkv_weight": gaussian(key_list[3], (LAYERS, C, 3 * C), C ** -0.5, 0.25, ((1, 16),)),
        "qkv_bias": gaussian(key_list[4], (LAYERS, 2, C), 0.5, 3.0, ((2, 16),)),
        "rel_table": gaussian(key_list[5], (LAYERS, HEADS, RELS), 1.0, 4.0, ((1, 16),)),
        "proj_weight": gaussian(key_list[6], (LAYERS, C, C), (C // 16) ** -0.5, 1.0, ((1, 16),)),
        "out_bias": gaussian(key_list[7], (LAYERS, 2, C), 0.5, 3.0, ((2, 16),)),
        "fc1_weight": gaussian(key_list[8], (LAYERS, C, MLP), C ** -0.5, 0.25, ((1, 16),)),
        "fc1_bias": gaussian(key_list[9], (LAYERS, MLP), 0.5, 3.0, ((1, 16),)),
        "fc2_weight": gaussian(key_list[10], (LAYERS, MLP, C), MLP ** -0.5, 0.125, ((1, 16),)),
        "cotangent": gaussian(key_list[11], (IMAGES, GRID_ROWS, COLS, C), 1.0, 6.0, ((0, 16), (1, 8))),
    }


epsilon = 1e-05
highest = lax.Precision.HIGHEST

@jax.custom_vjp
def low(v):
    return lax.optimization_barrier(v.astype(jnp.bfloat16)).astype(jnp.float32)

@jax.custom_vjp
def low_back(v):
    return v

def low_keep(v):
    return (low(v), None)

def low_pass(kept, grad):
    return (grad,)

def back_keep(v):
    return (v, None)

def back_low(kept, grad):
    return (low(grad),)
low.defvjp(low_keep, low_pass)
low_back.defvjp(back_keep, back_low)

def normalize(values, gain_row, shift_row):
    center = values - lax.optimization_barrier(jnp.mean(values, axis=-1, keepdims=True))
    spread = lax.optimization_barrier(jnp.mean(center * center, axis=-1, keepdims=True))
    return center * lax.rsqrt(spread + epsilon) * gain_row + shift_row

def to_windows(field, height, width):
    depth = field.shape[-1]
    blocks = field.reshape(height // WIN, WIN, width // WIN, WIN, depth)
    return blocks.transpose(0, 2, 1, 3, 4).reshape(-1, WIN * WIN, depth)

def from_windows(blocks, height, width):
    depth = blocks.shape[-1]
    field = blocks.reshape(height // WIN, width // WIN, WIN, WIN, depth)
    return field.transpose(0, 2, 1, 3, 4).reshape(height, width, depth)

def relative_index():
    places = jnp.arange(WIN * WIN)
    row_of = places // WIN
    col_of = places % WIN
    offsets = (row_of[:, None] - row_of[None, :] + WIN - 1) * (2 * WIN - 1) + col_of[:, None] - col_of[None, :] + WIN - 1
    return offsets.astype(jnp.int32)

def region_mask(first_row, height, width, total_rows):
    row_ids = first_row + jnp.arange(height)
    col_ids = jnp.arange(width)
    row_region = jnp.where(row_ids < total_rows - WIN, 0, jnp.where(row_ids < total_rows - SHIFT, 1, 2))
    col_region = jnp.where(col_ids < width - WIN, 0, jnp.where(col_ids < width - SHIFT, 1, 2))
    labels = (row_region[:, None] * 3 + col_region[None, :]).astype(jnp.float32)
    label_win = to_windows(labels[:, :, None], height, width)[:, :, 0]
    return jnp.where(label_win[:, :, None] == label_win[:, None, :], 0.0, -100.0).astype(jnp.float32)

def layer(field, weights, mask):
    gain_pair, shift_pair, qkv_w, qkv_b, table, proj_w, out_b, fc1_w, fc1_b, fc2_w = weights
    height = field.shape[0]
    width = field.shape[1]
    tokens = field.reshape(-1, C)
    normed = low(normalize(tokens, gain_pair[0], shift_pair[0]))
    projected = jnp.dot(normed, qkv_w, precision=highest)
    query = low_back(low(projected[:, :C] + qkv_b[0]))
    key_all = low_back(low(projected[:, C:2 * C]))
    value_all = low_back(low(projected[:, 2 * C:] + qkv_b[1]))

    def as_heads(part):
        return to_windows(part.reshape(height, width, C), height, width).reshape(-1, WIN * WIN, HEADS, HD)
    scores = jnp.einsum('wqhd,wkhd->whqk', as_heads(query), as_heads(key_all), precision=highest) * HD ** (-0.5)
    scores = scores + table[:, relative_index()][None]
    if mask is not None:
        scores = scores + mask[:, None]
    scores = low_back(scores)
    soft = low(jax.nn.softmax(scores, axis=-1))
    mixed = jnp.einsum('whqk,wkhd->wqhd', soft, as_heads(value_all), precision=highest)
    mixed = from_windows(mixed.reshape(-1, WIN * WIN, C), height, width).reshape(-1, C)
    mixed = low_back(low(mixed))
    branch = low_back(jnp.dot(mixed, proj_w, precision=highest) + out_b[0])
    middle = tokens + branch
    normed_two = low(normalize(middle, gain_pair[1], shift_pair[1]))
    hidden = low_back(jnp.dot(normed_two, fc1_w, precision=highest) + fc1_b)
    active = low(jax.nn.gelu(hidden, approximate=False))
    second = low_back(jnp.dot(active, fc2_w, precision=highest) + out_b[1])
    return (middle + second).reshape(height, width, C)

def image_pass(field, params):
    first = layer(field, tuple((member[0] for member in params)), None)
    rolled = jnp.roll(first, (-SHIFT, -SHIFT), (0, 1))
    shifted_mask = region_mask(0, GRID_ROWS, COLS, GRID_ROWS)
    second = layer(rolled, tuple((member[1] for member in params)), shifted_mask)
    return jnp.roll(second, (SHIFT, SHIFT), (0, 1))

def forward(fields, params):
    return lax.map(lambda single: jax.checkpoint(image_pass)(single, params), fields)

def reference(images, norm_gain, norm_shift, qkv_weight, qkv_bias, rel_table, proj_weight, out_bias, fc1_weight, fc1_bias, fc2_weight, cotangent):
    params = tuple((member.astype(jnp.float32) for member in (norm_gain, norm_shift, qkv_weight, qkv_bias, rel_table, proj_weight, out_bias, fc1_weight, fc1_bias, fc2_weight)))
    fields = images.astype(jnp.float32)
    result, backward = jax.vjp(forward, fields, params)
    grad_fields, grads = backward(cotangent.astype(jnp.float32))
    return (result, grad_fields, grads[0], grads[1], grads[2], grads[3], grads[4], grads[5], grads[6], grads[7], grads[8], grads[9])
```

```python
import functools

import jax
import jax.numpy as jnp
import numpy as np
from jax import lax
from jax.experimental import pallas as pl
from jax.experimental.pallas import tpu as pltpu
from jax.sharding import PartitionSpec as P

C = 512
HEADS = 16
HD = 32
MLP = 2048
WIN = 7
SHIFT = 3
SPOT = 64
WINDOWS = 4
TOK = WINDOWS * SPOT
GROUPS = 4
NAT = 2 * 7 * 16
HALO = 2 * 3 * 16
SMALL = 128
ATTN = 2048
SPLIT = 3072
SHARE = 3200
ATTN_IN = ATTN + SMALL
ATTN_OUT = ATTN + 2 * SMALL
FF = 4096
TOTAL = 6656
QUARTER = TOTAL // 4
SCALE = HD ** (-0.5)
EPS = 1e-05
BF = jnp.bfloat16
F32 = jnp.float32
VM = pl.BlockSpec(memory_space=pltpu.VMEM)
HB = pl.BlockSpec(memory_space=pl.ANY)


def _places():
    nat = lambda m, r, c: (m * 7 + r) * 16 + c
    halo = lambda m, r, c: (m * 3 + r) * 16 + c
    plain = np.zeros((TOK, NAT), np.float32)
    rolled = np.zeros((TOK, NAT), np.float32)
    rolled_halo = np.zeros((TOK, HALO), np.float32)
    first_rows = np.zeros((HALO, TOK), np.float32)
    last_rows = np.zeros((HALO, TOK), np.float32)
    for m in range(2):
        for w in range(2):
            for y in range(7):
                for x in range(7):
                    t = (m * 2 + w) * SPOT + y * 7 + x
                    col = w * 7 + x
                    plain[t, nat(m, y, col)] = 1
                    if y < SHIFT:
                        first_rows[halo(m, y, col), t] = 1
                    col = (col + SHIFT) % 14
                    if y + SHIFT < 7:
                        rolled[t, nat(m, y + SHIFT, col)] = 1
                    else:
                        rolled_halo[t, halo(m, y + SHIFT - 7, col)] = 1
                        last_rows[halo(m, y + SHIFT - 7, col), t] = 1
    return plain, rolled, rolled_halo, first_rows, last_rows


PLAIN, ROLLED, ROLLED_HALO, FIRST_ROWS, LAST_ROWS = _places()
ROLL = ROLLED @ PLAIN.T
PLAIN_HALO = np.zeros((TOK, HALO), np.float32)
for _r, _t in zip(*np.nonzero(FIRST_ROWS)):
    PLAIN_HALO[_t, _r] = 1


def _pairs():
    rel = np.full((SPOT, SPOT), -1)
    rows = np.zeros((SPOT, GROUPS * SPOT), np.float32)
    cols = np.zeros((SPOT, GROUPS * SPOT), np.float32)
    for a in range(49):
        for b in range(49):
            rel[a, b] = (a // 7 - b // 7 + 6) * 13 + a % 7 - b % 7 + 6
            for h in range(GROUPS):
                if (a // 7 >= 4) != (b // 7 >= 4):
                    rows[a, h * SPOT + b] = -100.0
                if (a % 7 >= 4) != (b % 7 >= 4):
                    cols[a, h * SPOT + b] = -100.0
    return rel, rows, cols


REL, MASK_ROWS, MASK_COLS = _pairs()
REL_HOT = (REL[None] == np.arange(192)[:, None, None]).astype(np.float32)
PACKED_REL = np.concatenate([REL[:32], REL[32:]], axis=1)
PACKED_HOT = (PACKED_REL.reshape(-1, 1) == np.arange(256)[None]).astype(np.float32)
EDGE = np.where(np.tile(np.arange(SPOT), GROUPS) < 49, 0.0, -1e30).astype(np.float32)
HEAD_LANES = np.repeat(np.kron(np.eye(GROUPS), np.ones((1, HD))), SPOT, axis=0).astype(np.float32)
SEGMENT = np.kron(np.eye(2), np.ones((SPOT, SPOT))).astype(np.float32)


def const(x):
    return jnp.asarray(x, BF)


def dot(a, b):
    return lax.dot_general(a, b, (((1,), (0,)), ((), ())), preferred_element_type=F32)


def dot_nt(a, b):
    return lax.dot_general(a, b, (((1,), (1,)), ((), ())), preferred_element_type=F32)


def dot_tn(a, b):
    return lax.dot_general(a, b, (((0,), (0,)), ((), ())), preferred_element_type=F32)


def halves(x):
    high = x.astype(BF)
    return high, (x - high.astype(F32)).astype(BF)


def place(hot, x):
    high = x.astype(BF)
    rest = x - high.astype(F32)
    mid = rest.astype(BF)
    low = (rest - mid.astype(F32)).astype(BF)
    return dot(hot, high) + dot(hot, mid) + dot(hot, low)


def segment_sum(x, seg):
    high, low = halves(x)
    parts = [
        dot(high[:, k : k + 128], seg) + dot(low[:, k : k + 128], seg) for k in (0, 128)
    ]
    return jnp.concatenate(parts, axis=1)


def segment_max(s):
    lane = lax.broadcasted_iota(jnp.int32, (SPOT, 128), 1)
    left = lane < SPOT
    parts = []
    for k in (0, 128):
        part = s[:, k : k + 128]
        one = jnp.max(jnp.where(left, part, -3e38), axis=1, keepdims=True)
        two = jnp.max(jnp.where(left, -3e38, part), axis=1, keepdims=True)
        parts.append(jnp.where(left, one, two))
    return jnp.concatenate(parts, axis=1)


def norm_parts(x):
    center = x - jnp.mean(x, axis=-1, keepdims=True)
    r = lax.rsqrt(jnp.mean(center * center, axis=-1, keepdims=True) + EPS)
    return center * r, r


def norm_back(dh, xhat, r, gain):
    e = dh * gain
    return r * (
        e
        - jnp.mean(e, axis=-1, keepdims=True)
        - xhat * jnp.mean(e * xhat, axis=-1, keepdims=True)
    )


def four(x, lanes):
    return jnp.concatenate([x] * GROUPS, axis=0) * lanes


def fold(x, lanes):
    x = x * lanes
    return x[:64] + x[64:128] + x[128:192] + x[192:]


def column_sum(x):
    return jnp.sum(x, axis=0, keepdims=True)


def me_shard():
    return lax.axis_index("shard")


def row_at(i, rows):
    return pl.ds(pl.multiple_of(i * rows, 32), 32)


def gathered(blocks):
    left, right = [], []
    for core in range(2):
        for m in range(4):
            for y in range(2):
                whose = 4 * m + 2 * y + core
                left.append((blocks[4 * core + m], 32 * y, whose))
                right.append((blocks[8 + 2 * core + y], 32 * m, whose))
    return left, right


def attn_copies(blocks, offset, w, sem):
    if len(blocks) == 1:
        return [pltpu.make_async_copy(blocks[0].at[:, offset : offset + ATTN], w, sem.at[0])]
    me = me_shard()
    return [
        pltpu.make_async_copy(
            ref.at[row : row + 32, :ATTN],
            w.at[row_at(lax.bitwise_xor(me, whose), 32), :],
            sem.at[n],
        )
        for n, (ref, row, whose) in enumerate(gathered(blocks)[0])
    ]


def ff_copies(blocks, offset, w1, w2, sem):
    out = []
    if len(blocks) == 1:
        whole = blocks[0]
        out.append(pltpu.make_async_copy(whole.at[:, offset : offset + MLP], w1, sem.at[0, 0]))
        for i in range(16):
            for j in range(4):
                at = offset + MLP + 512 * j
                to = 128 * i + 32 * j
                out.append(
                    pltpu.make_async_copy(
                        whole.at[32 * i : 32 * i + 32, at : at + 512],
                        w2.at[to : to + 32, :],
                        sem.at[i, 1 + j],
                    )
                )
        return out
    me = me_shard()
    left, right = gathered(blocks)
    first = SPLIT - ATTN
    for n, (ref, row, whose) in enumerate(left):
        rows = row_at(lax.bitwise_xor(me, whose), 32)
        out.append(
            pltpu.make_async_copy(
                ref.at[row : row + 32, ATTN:], w1.at[rows, :first], sem.at[n, 0]
            )
        )
    for n, (ref, row, whose) in enumerate(right):
        i = lax.bitwise_xor(me, whose)
        out.append(
            pltpu.make_async_copy(
                ref.at[row : row + 32, : MLP - first],
                w1.at[row_at(i, 32), first:],
                sem.at[n, 1],
            )
        )
        for j in range(4):
            at = MLP - first + 512 * j
            out.append(
                pltpu.make_async_copy(
                    ref.at[row : row + 32, at : at + 512],
                    w2.at[row_at(4 * i + j, 32), :],
                    sem.at[n, 2 + j],
                )
            )
    return out


def share_copies(grads, mine, theirs, sem):
    core = lax.rem(me_shard(), 2)
    out = []
    for q in range(8):
        for n, (target, bit) in enumerate(((mine, core), (theirs, 1 - core))):
            at = pl.multiple_of((2 * q + bit) * 32, 32)
            out.append(
                pltpu.make_async_copy(
                    grads.at[pl.ds(at, 32), :],
                    target.at[32 * q : 32 * q + 32, :],
                    sem.at[q, n],
                )
            )
    return out


def params_kernel(small, out, scratch):
    me = me_shard()
    for t in range(16):
        scratch[row_at(lax.bitwise_xor(me, t), 32), :] = small[32 * t : 32 * t + 32, :].astype(F32)
    out[...] = scratch[...].T


def attn_forward_kernel(level, *refs):
    if level == 0:
        img, spread = refs[:2]
        refs = refs[2:]
    else:
        own, halo, spread, spread_halo, mask_rows, mask_cols = refs[:6]
        refs = refs[6:]
    params, bias, lanes_ref, seg_ref = refs[:4]
    blocks, refs = refs[4:-8], refs[-8:]
    x_out, x1_out, h_out, qkv, a_out, o_out, w, sem = refs
    copies = attn_copies(blocks, 0, w, sem)
    for c in copies:
        c.start()
    if level == 0:
        x = dot(spread[...], img[...])
    else:
        x = place(spread[...], own[...]) + dot(spread_halo[...], halo[...])
    x_out[...] = x
    row = 8 * level
    xhat, _ = norm_parts(x)
    h = (xhat * params[row : row + 1, :] + params[row + 2 : row + 3, :]).astype(BF)
    h_out[...] = h
    for c in copies:
        c.wait()
    qkv[:, :C] = (dot(h, w[:, :C]) + params[row + 4 : row + 5, :]).astype(BF)
    qkv[:, C : 2 * C] = dot(h, w[:, C : 2 * C]).astype(BF)
    qkv[:, 2 * C :] = (dot(h, w[:, 2 * C : 3 * C]) + params[row + 5 : row + 6, :]).astype(BF)
    lanes = lanes_ref[...]
    seg = seg_ref[...]
    if level == 1:
        last = (lax.axis_index("seq") == 7).astype(F32)
        row_mask = mask_rows[...] * last
        both_mask = jnp.minimum(row_mask, mask_cols[...])
    for window in range(WINDOWS):
        rows = slice(window * SPOT, (window + 1) * SPOT)
        for g in range(GROUPS):
            at = 128 * g
            q = qkv[rows, at : at + 128]
            k = qkv[rows, C + at : C + at + 128]
            v = qkv[rows, 2 * C + at : 2 * C + at + 128]
            s = dot_nt(q, four(k, lanes)) * SCALE + bias[g]
            if level == 1:
                s = s + (both_mask if window % 2 else row_mask)
            e = jnp.exp(s - segment_max(s))
            a = e / segment_sum(e, seg)
            a_out[window * GROUPS + g] = a
            o_out[rows, at : at + 128] = dot(a.astype(BF), four(v, lanes)).astype(BF)
    x1_out[...] = x + (dot(o_out[...], w[:, 3 * C :]) + params[row + 6 : row + 7, :])


def ff_forward_kernel(level, offset, *refs):
    x1_ref, params, fc1_b, send_hot = refs[:4]
    refs = refs[4:]
    if level == 1:
        out_hot = refs[0]
        refs = refs[1:]
    blocks, refs = refs[:-8], refs[-8:]
    result, send, h2_out, g_out, gp_out, w1, w2, sem = refs
    copies = ff_copies(blocks, offset, w1, w2, sem)
    for c in copies:
        c.start()
    row = 8 * level
    x1 = x1_ref[...]
    xhat, _ = norm_parts(x1)
    h2 = (xhat * params[row + 1 : row + 2, :] + params[row + 3 : row + 4, :]).astype(BF)
    h2_out[...] = h2
    for c in copies:
        c.wait()
    total = x1 + params[row + 7 : row + 8, :]
    for n in range(4):
        cols = slice(512 * n, 512 * n + 512)
        f = dot(h2, w1[:, cols]) + fc1_b[:, cols]
        phi = 0.5 * (1.0 + lax.erf(f * (0.5**0.5)))
        g = (f * phi).astype(BF)
        g_out[:, cols] = g
        gp_out[:, cols] = (phi + f * (jnp.exp(f * f * -0.5) * 0.3989422804014327)).astype(BF)
        total = total + dot(g, w2[cols, :])
    send[...] = dot(send_hot[...], total.astype(BF)).astype(BF)
    if level == 0:
        result[...] = total
    else:
        result[...] = place(out_hot[...], total)


def ff_backward_kernel(level, offset, *refs):
    if level == 1:
        cot, halo, spread, spread_halo = refs[:4]
        refs = refs[4:]
    else:
        own, halo, spread_halo = refs[:3]
        refs = refs[3:]
    x1_ref, h2_ref, g_ref, gp_ref, params, pick = refs[:6]
    blocks, refs = refs[6:-10], refs[-10:]
    g1_out, rows_out, col_out, mine, theirs, w1, w2, grads, sem, share_sem = refs
    copies = ff_copies(blocks, offset, w1, w2, sem)
    for c in copies:
        c.start()
    if level == 1:
        g2 = dot(spread[...], cot[...]) + dot(spread_halo[...], halo[...])
    else:
        g2 = own[...] + dot(spread_halo[...], halo[...])
    dz = g2.astype(BF)
    row = 8 * level
    xhat, r = norm_parts(x1_ref[...])
    h2 = h2_ref[...]
    ones = jnp.ones((TOK, 128), BF)
    for c in copies:
        c.wait()
    dh2 = jnp.zeros((TOK, C), F32)
    col_out[...] = jnp.zeros((C, SMALL), F32)
    lane = lax.broadcasted_iota(jnp.int32, (32, SMALL), 1)
    for n in range(4):
        cols = slice(512 * n, 512 * n + 512)
        d = dot_tn(g_ref[:, cols], dz).astype(BF)
        for i in range(4):
            for j in range(4):
                at = 128 * i + 32 * j
                to = 32 * (4 * n + i)
                grads[to : to + 32, MLP + 512 * j : MLP + 512 * j + 512] = d[at : at + 32, :]
        df = (dot_nt(dz, w2[cols, :]) * gp_ref[:, cols].astype(F32)).astype(BF)
        grads[:, cols] = dot_tn(h2, df).astype(BF)
        sums = dot_tn(df, ones)
        for i in range(4):
            to = 32 * (4 * n + i)
            picked = jnp.zeros((32, SMALL), F32)
            for j in range(4):
                at = 128 * i + 32 * j
                picked = picked + jnp.where(lane == 8 + j, sums[at : at + 32, :], 0.0)
            col_out[to : to + 32, :] = picked
        dh2 = dh2 + dot_nt(df, w1[:, cols])
    shares = share_copies(grads, mine, theirs, share_sem)
    for c in shares:
        c.start()
    g1_out[...] = g2 + norm_back(dh2, xhat, r, params[row + 1 : row + 2, :])
    rows_out[...] = jnp.zeros((8, C), F32)
    rows_out[1:2, :] = column_sum(dh2 * xhat)
    rows_out[3:4, :] = column_sum(dh2)
    rows_out[7:8, :] = column_sum(dz.astype(F32))
    for c in shares:
        c.wait()


def attn_backward_kernel(level, *refs):
    g1_ref, x_ref, h_ref, qkv, a_ref, o_ref, params, rows_ref, col_ref = refs[:9]
    lanes_ref, seg_ref, back_hot = refs[9:12]
    refs = refs[12:]
    if level == 1:
        send_hot = refs[0]
        refs = refs[1:]
    count = 12 if level == 0 else 1
    blocks, refs = refs[:count], refs[count:]
    if level == 1:
        send = refs[0]
        refs = refs[1:]
    back, mine, theirs, w, grads, d_qkv, stack, sem, share_sem = refs
    copies = attn_copies(blocks, 0, w, sem)
    for c in copies:
        c.start()
    row = 8 * level
    g1 = g1_ref[...]
    dy = g1.astype(BF)
    grads[:, 3 * C : 4 * C] = dot_tn(o_ref[...], dy).astype(BF)
    stack[...] = jnp.zeros((SMALL, C), F32)
    stack[0:8, :] = rows_ref[...]
    stack[6:7, :] = column_sum(dy.astype(F32))
    xhat, r = norm_parts(x_ref[...])
    lanes = lanes_ref[...]
    lanes_f = lanes.astype(F32)
    seg = seg_ref[...]
    for c in copies:
        c.wait()
    do_all = dot_nt(dy, w[:, 3 * C :]).astype(BF)
    lane = lax.broadcasted_iota(jnp.int32, (32, 128), 1)
    for g in range(GROUPS):
        at = 128 * g
        ds_sum = jnp.zeros((SPOT, GROUPS * SPOT), F32)
        for window in range(WINDOWS):
            rows = slice(window * SPOT, (window + 1) * SPOT)
            q = qkv[rows, at : at + 128]
            k = qkv[rows, C + at : C + at + 128]
            v = qkv[rows, 2 * C + at : 2 * C + at + 128]
            do = do_all[rows, at : at + 128]
            a = a_ref[window * GROUPS + g]
            da = dot_nt(do, four(v, lanes))
            ds = (a * (da - segment_sum(a * da, seg))).astype(BF)
            ds_sum = ds_sum + ds.astype(F32)
            dv = fold(dot_tn(a.astype(BF), do), lanes_f)
            dq = dot(ds, four(k, lanes)) * SCALE
            dk = fold(dot_tn(ds, q), lanes_f) * SCALE
            d_qkv[rows, at : at + 128] = dq.astype(BF)
            d_qkv[rows, C + at : C + at + 128] = dk.astype(BF)
            d_qkv[rows, 2 * C + at : 2 * C + at + 128] = dv.astype(BF)
        for pair in range(2):
            top = ds_sum[:32, 128 * pair : 128 * pair + 128]
            low = ds_sum[32:, 128 * pair : 128 * pair + 128]
            even = jnp.where(lane < 64, top, pltpu.roll(low, 64, 1))
            odd = jnp.where(lane < 64, pltpu.roll(top, 64, 1), low)
            head = 4 * g + 2 * pair
            grads[32 * head : 32 * head + 32, ATTN_IN:] = even.astype(BF)
            grads[32 * head + 32 : 32 * head + 64, ATTN_IN:] = odd.astype(BF)
    h = h_ref[...]
    for n in range(3):
        cols = slice(C * n, C * n + C)
        grads[:, cols] = dot_tn(h, d_qkv[:, cols]).astype(BF)
    stack[4:5, :] = column_sum(d_qkv[:, :C].astype(F32))
    stack[5:6, :] = column_sum(d_qkv[:, 2 * C :].astype(F32))
    dh = dot_nt(d_qkv[...], w[:, : 3 * C])
    stack[0:1, :] = column_sum(dh * xhat)
    stack[2:3, :] = column_sum(dh)
    grads[:, ATTN:ATTN_IN] = (stack[...].T + col_ref[...]).astype(BF)
    shares = share_copies(grads, mine, theirs, share_sem)
    for c in shares:
        c.start()
    total = g1 + norm_back(dh, xhat, r, params[row : row + 1, :])
    if level == 1:
        send[...] = dot(send_hot[...], total.astype(BF)).astype(BF)
    back[...] = place(back_hot[...], total)
    for c in shares:
        c.wait()


def pair_kernel(*refs):
    shares, outs = refs[:4], refs[4:]
    chip = lax.div(me_shard(), 2)
    for m in range(4):
        for y in range(2):
            rows = row_at(lax.bitwise_xor(chip, 2 * m + y), 32)
            left, right = outs[m], outs[4 + y]
            for mine, other, start, width in (
                (shares[0], shares[1], 0, FF),
                (shares[2], shares[3], FF, ATTN_OUT),
            ):
                total = (mine[rows, :].astype(F32) + other[rows, :].astype(F32)).astype(BF)
                cut = max(0, min(width, SHARE - start))
                if cut:
                    left[32 * y : 32 * y + 32, start : start + cut] = total[:, :cut]
                if cut < width:
                    at = start + cut - SHARE
                    right[32 * m : 32 * m + 32, at : at + width - cut] = total[:, cut:]


def added(refs):
    return functools.reduce(jnp.add, [r[...].astype(F32) for r in refs])


def middle_kernel(*refs):
    outs = refs[6:]
    left = added(refs[:4]).astype(BF)
    for y in range(2):
        outs[y][...] = left[32 * y : 32 * y + 32, :]
    right = added(refs[4:6]).astype(BF)
    for m in range(4):
        outs[2 + m][...] = right[32 * m : 32 * m + 32, :]


def z_part(ref, k):
    p = lax.bitwise_xor(lax.div(lax.axis_index("seq"), 2), k)
    return ref.at[:, pl.ds(pl.multiple_of(p * QUARTER, 128), QUARTER)]


def split_kernel(*refs):
    pieces, outs = refs[:6], refs[6:10]
    total, sem = refs[10:]
    total[:, :SHARE] = added(pieces[:2]).astype(BF)
    total[:, SHARE : 2 * SHARE] = added(pieces[2:]).astype(BF)
    total[:, 2 * SHARE :] = jnp.zeros((32, TOTAL - 2 * SHARE), BF)
    copies = [pltpu.make_async_copy(z_part(total, k), outs[k], sem.at[k]) for k in range(4)]
    for c in copies:
        c.start()
    for c in copies:
        c.wait()


def finish_kernel(*refs):
    pieces, hot = refs[:8], refs[8]
    gain, shift, qkv_w, qkv_b, table, proj, out_b, fc1, fc1_b, fc2 = refs[9:19]
    scratch, sem = refs[19:]
    copies = [
        pltpu.make_async_copy(
            pieces[4 * level + k], z_part(scratch.at[level], k), sem.at[level, k]
        )
        for level in range(2)
        for k in range(4)
    ]
    for c in copies:
        c.start()
    for c in copies:
        c.wait()
    total = scratch[...]
    for level in range(2):
        fc1[level] = total[level, :, :MLP].astype(F32)
        for j in range(4):
            fc2[level, 32 * j : 32 * j + 32, :] = total[
                level, :, MLP + 512 * j : MLP + 512 * j + 512
            ].astype(F32)
        qkv_w[level] = total[level, :, FF : FF + 3 * C].astype(F32)
        proj[level] = total[level, :, FF + 3 * C : FF + 4 * C].astype(F32)
        small = total[level, :, FF + ATTN : FF + ATTN_IN].astype(F32).T
        gain[level] = small[0:2, :]
        shift[level] = small[2:4, :]
        qkv_b[level] = small[4:6, :]
        out_b[level] = small[6:8, :]
        fc1_b[level : level + 1, :] = jnp.concatenate(
            [small[8 + j : 9 + j, :] for j in range(4)], axis=1
        )
        ds = total[level, :, FF + ATTN_IN : FF + ATTN_OUT]
        flat = jnp.concatenate([ds[r : r + 1, :] for r in range(32)], axis=1)
        sums = dot(jnp.broadcast_to(flat.astype(F32), (16, 4096)).astype(BF), hot[...])
        table[level] = sums[0:1, :169]


def sds(shape, dtype):
    return jax.ShapeDtypeStruct(shape, dtype)


def call(kernel, ins, outs, scratch, args, flops=0):
    return pl.pallas_call(
        kernel,
        out_shape=tuple(s for s, _ in outs),
        in_specs=ins,
        out_specs=tuple(m for _, m in outs),
        scratch_shapes=scratch,
        compiler_params=pltpu.CompilerParams(vmem_limit_bytes=48 * 1024 * 1024),
        cost_estimate=pl.CostEstimate(flops=8 * flops, bytes_accessed=8000000, transcendentals=0),
    )(*args)


def shard_permute(x, k):
    return lax.ppermute(x, "shard", [(i, i ^ k) for i in range(16)])


def core_permute(x):
    return shard_permute(x, 1)


def y_permute(x):
    return shard_permute(x, 2)


def x_permutes(pieces):
    return [shard_permute(p, 4 * k) for k, p in enumerate(pieces, 1)]


def seq_permute(x, k):
    return lax.ppermute(x, "seq", [(i, i ^ k) for i in range(8)])


def z_permutes(pieces):
    return [seq_permute(p, 2 * k) for k, p in enumerate(pieces, 1)]


def passed_along(x, by):
    return lax.ppermute(x, "seq", [(i, (i + by) % 8) for i in range(8)])


def gather_blocks(left, right):
    left_pair = jnp.concatenate([left, y_permute(left)], axis=0)
    right_row = jnp.concatenate([right] + x_permutes([right] * 3), axis=0)
    left_all = [left_pair] + x_permutes([left_pair] * 3)
    right_all = [right_row, y_permute(right_row)]
    return (
        left_all
        + [core_permute(b) for b in left_all]
        + right_all
        + [core_permute(b) for b in right_all]
    )


def pair_sums(shares):
    ff_mine, ff_theirs, attn_mine, attn_theirs = shares
    return call(
        pair_kernel,
        [VM] * 4,
        [(sds((64, SHARE), BF), VM)] * 4 + [(sds((128, SHARE), BF), VM)] * 2,
        [],
        (ff_mine, core_permute(ff_theirs), attn_mine, core_permute(attn_theirs)),
    )


def middle_sums(pieces):
    left, right = list(pieces[:4]), list(pieces[4:])
    arrived = left[:1] + x_permutes(left[1:]) + right[:1] + [y_permute(right[1])]
    return call(middle_kernel, [VM] * 6, [(sds((32, SHARE), BF), VM)] * 6, [], arrived)


def end_sums(pieces):
    left, right = list(pieces[:2]), list(pieces[2:])
    arrived = left[:1] + [y_permute(left[1])] + right[:1] + x_permutes(right[1:])
    return call(
        split_kernel,
        [VM] * 6,
        [(sds((32, QUARTER), BF), HB)] * 4,
        [pltpu.VMEM((32, TOTAL), BF), pltpu.SemaphoreType.DMA((4,))],
        arrived,
    )


def total_of(parts):
    return functools.reduce(jnp.add, [p.astype(F32) for p in parts]).astype(BF)


def seq_sum(pieces):
    own = total_of([pieces[0]] + z_permutes(pieces[1:]))
    own = total_of([own, seq_permute(own, 1)])
    return [own] + z_permutes([own] * 3)


def on_device(
    images,
    norm_gain,
    norm_shift,
    qkv_weight,
    qkv_bias,
    rel_table,
    proj_weight,
    out_bias,
    fc1_weight,
    fc1_bias,
    fc2_weight,
    cotangent,
):
    small = jnp.concatenate(
        [
            jnp.stack([norm_gain, norm_shift, qkv_bias, out_bias], axis=1).reshape(16, 32),
            fc1_bias.reshape(8, 32),
            jnp.pad(rel_table[:, 0], ((0, 0), (0, 23))).reshape(12, 32),
        ],
        axis=0,
    ).T
    small = jnp.pad(small, ((0, 0), (0, SMALL - 36)))

    def packed(level):
        tall = fc2_weight[level]
        wide = [qkv_weight[level], proj_weight[level], fc1_weight[level]]
        return jnp.concatenate(
            wide + [tall[32 * j : 32 * j + 32] for j in range(4)], axis=1
        )

    block = packed(0)
    all_one = gather_blocks(block[:, :SPLIT], block[:, SPLIT:])
    for k in (1, 2, 4, 8):
        small = jnp.concatenate([small, shard_permute(small, k)], axis=0)
    all_two = [lax.all_gather(packed(1), "shard", axis=0, tiled=True)]

    def natural(x):
        return jnp.pad(x, ((0, 0), (0, 0), (0, 2), (0, 0))).reshape(-1, C)

    img = natural(images)
    cot = natural(cotangent)
    cot_halo = passed_along(natural(cotangent[:, :SHIFT]), -1)

    (params,) = call(params_kernel, [VM], [(sds((SMALL, C), F32), VM)], [pltpu.VMEM((C, SMALL), F32)], (small,))
    tables = params[24:36].reshape(2, 6, HEADS, 32).transpose(0, 2, 1, 3).reshape(32, 192)
    bias_all = lax.dot_general(
        tables.astype(BF),
        const(REL_HOT),
        (((1,), (0,)), ((), ())),
        preferred_element_type=F32,
    )
    bias_all = bias_all.reshape(2, GROUPS, 4, SPOT, SPOT).transpose(0, 1, 3, 2, 4)
    bias_all = bias_all.reshape(2, GROUPS, SPOT, 256) + jnp.asarray(EDGE)
    fc1_b = params[16:24].reshape(2, 4, 16, 32).transpose(0, 2, 1, 3).reshape(2, 1, MLP)

    lanes = const(HEAD_LANES)
    seg = const(SEGMENT)
    tokens = sds((TOK, C), F32)
    tokens_low = sds((TOK, C), BF)
    hidden_low = sds((TOK, MLP), BF)
    halo_low = sds((HALO, C), BF)

    def attn_forward(level, lead, blocks):
        outs = [
            (tokens, VM),
            (tokens, VM),
            (tokens_low, VM),
            (sds((TOK, 3 * C), BF), VM),
            (sds((16, SPOT, 256), F32), VM),
            (tokens_low, VM),
        ]
        return call(
            functools.partial(attn_forward_kernel, level),
            [VM] * (len(lead) + 4) + [HB] * len(blocks),
            outs,
            [pltpu.VMEM((C, ATTN), BF), pltpu.SemaphoreType.DMA((16,))],
            tuple(lead) + (params, bias_all[level], lanes, seg) + tuple(blocks),
            flops=2 * TOK * C * ATTN,
        )

    def ff_scratch():
        return [pltpu.VMEM((C, MLP), BF), pltpu.VMEM((MLP, C), BF)]

    def ff_forward(level, x1, blocks):
        lead = (x1, params, fc1_b[level])
        if level == 0:
            lead += (const(FIRST_ROWS),)
            out, offset = tokens, 0
        else:
            lead += (const(LAST_ROWS), const(ROLLED.T))
            out, offset = sds((NAT, C), F32), ATTN
        return call(
            functools.partial(ff_forward_kernel, level, offset),
            [VM] * len(lead) + [HB] * len(blocks),
            [(out, VM), (halo_low, VM), (tokens_low, VM), (hidden_low, VM), (hidden_low, VM)],
            ff_scratch() + [pltpu.SemaphoreType.DMA((16, 6))],
            lead + tuple(blocks),
            flops=4 * TOK * C * MLP,
        )

    def ff_backward(level, lead, saved, blocks):
        shares = sds((256, FF), BF)
        return call(
            functools.partial(ff_backward_kernel, level, ATTN * level),
            [VM] * (len(lead) + 6) + [HB] * len(blocks),
            [
                (tokens, VM),
                (sds((8, C), F32), VM),
                (sds((C, SMALL), F32), VM),
                (shares, HB),
                (shares, HB),
            ],
            ff_scratch()
            + [
                pltpu.VMEM((C, FF), BF),
                pltpu.SemaphoreType.DMA((16, 6)),
                pltpu.SemaphoreType.DMA((8, 2)),
            ],
            tuple(lead) + tuple(saved) + (params, lanes) + tuple(blocks),
            flops=8 * TOK * C * MLP,
        )

    def attn_backward(level, g1, saved, rows, cols, hots, blocks):
        shares = sds((256, ATTN_OUT), BF)
        outs = [(halo_low, VM)] if level == 1 else []
        outs.append((tokens if level == 1 else sds((NAT, C), F32), VM))
        return call(
            functools.partial(attn_backward_kernel, level),
            [VM] * (11 + len(hots)) + [HB] * len(blocks),
            outs + [(shares, HB), (shares, HB)],
            [
                pltpu.VMEM((C, ATTN), BF),
                pltpu.VMEM((C, ATTN_OUT), BF),
                pltpu.VMEM((TOK, 3 * C), BF),
                pltpu.VMEM((SMALL, C), F32),
                pltpu.SemaphoreType.DMA((16,)),
                pltpu.SemaphoreType.DMA((8, 2)),
            ],
            (g1,) + tuple(saved) + (params, rows, cols, lanes, seg) + tuple(hots) + tuple(blocks),
            flops=4 * TOK * C * ATTN,
        )

    x_one, x1_one, *attn_saved_one = attn_forward(0, (img, const(PLAIN)), all_one)
    mid, send, *ff_saved_one = ff_forward(0, x1_one, all_one)
    lead = (
        mid,
        passed_along(send, -1),
        const(ROLL),
        const(ROLLED_HALO),
        jnp.asarray(MASK_ROWS),
        jnp.asarray(MASK_COLS),
    )
    x_two, x1_two, *attn_saved_two = attn_forward(1, lead, all_two)
    own_rows, send, *ff_saved_two = ff_forward(1, x1_two, all_two)
    returned = passed_along(send, 1).astype(F32).reshape(2, SHIFT, 16, C)
    outputs = jnp.concatenate(
        [returned, own_rows.reshape(2, 7, 16, C)[:, SHIFT:]], axis=1
    )[:, :, :14]

    g1, rows, cols, mine, theirs = ff_backward(
        1,
        (cot, cot_halo, const(ROLLED), const(ROLLED_HALO)),
        (x1_two, *ff_saved_two),
        all_two,
    )
    shares_two = (mine, theirs)
    send, own, mine, theirs = attn_backward(
        1,
        g1,
        (x_two, *attn_saved_two),
        rows,
        cols,
        (const(ROLL.T), const(LAST_ROWS)),
        all_two,
    )
    pieces_two = pair_sums(shares_two + (mine, theirs))
    own, pieces_two, outputs = lax.optimization_barrier((own, pieces_two, outputs))
    g1, rows, cols, mine, theirs = ff_backward(
        0,
        (own, passed_along(send, 1), const(PLAIN_HALO)),
        (x1_one, *ff_saved_one),
        all_one,
    )
    pieces_two = middle_sums(pieces_two)
    g1, pieces_two, shares_one = lax.optimization_barrier((g1, pieces_two, (mine, theirs)))
    input_grad, mine, theirs = attn_backward(
        0, g1, (x_one, *attn_saved_one), rows, cols, (const(PLAIN.T),), all_one
    )
    pieces_two = end_sums(pieces_two)
    shares_one, pieces_two = lax.optimization_barrier(
        (shares_one + (mine, theirs), pieces_two)
    )
    pieces_one = end_sums(middle_sums(pair_sums(shares_one)))
    sums_two = seq_sum(pieces_two)
    sums_one = seq_sum(pieces_one)
    shapes = [
        (2, 2, 32),
        (2, 2, 32),
        (2, 32, 3 * C),
        (2, 2, 32),
        (2, 1, 169),
        (2, 32, C),
        (2, 2, 32),
        (2, 32, MLP),
        (2, 128),
        (2, 128, C),
    ]
    grads = call(
        finish_kernel,
        [HB] * 8 + [VM],
        [(sds(shape, F32), VM) for shape in shapes],
        [pltpu.VMEM((2, 32, TOTAL), BF), pltpu.SemaphoreType.DMA((2, 4))],
        tuple(sums_one) + tuple(sums_two) + (const(PACKED_HOT),),
    )
    input_grad = input_grad.reshape(2, 7, 16, C)[:, :, :14]
    return (outputs, input_grad) + tuple(grads)


def solution(mesh):
    return jax.shard_map(
        on_device,
        mesh=mesh,
        in_specs=(
            P("shard", "seq", None, None),
            P(None, None, "shard"),
            P(None, None, "shard"),
            P(None, "shard", None),
            P(None, None, "shard"),
            P(None, "shard", None),
            P(None, "shard", None),
            P(None, None, "shard"),
            P(None, "shard", None),
            P(None, "shard"),
            P(None, "shard", None),
            P("shard", "seq", None, None),
        ),
        out_specs=(
            P("shard", "seq", None, None),
            P("shard", "seq", None, None),
            P(None, None, "shard"),
            P(None, None, "shard"),
            P(None, "shard", None),
            P(None, None, "shard"),
            P(None, "shard", None),
            P(None, "shard", None),
            P(None, None, "shard"),
            P(None, "shard", None),
            P(None, "shard"),
            P(None, "shard", None),
        ),
        check_vma=False,
    )
```

```python
import functools

import jax
import jax.numpy as jnp
import numpy as np
from jax import lax
from jax.experimental import pallas as pl
from jax.experimental.pallas import tpu as pltpu
from jax.sharding import PartitionSpec as P

C = 512
HEADS = 16
HD = 32
MLP = 2048
WIN = 7
SHIFT = 3
SPOT = 64
WINDOWS = 4
TOK = WINDOWS * SPOT
GROUPS = 4
NAT = 2 * 7 * 16
HALO = 2 * 3 * 16
SMALL = 128
ATTN = 2048
SPLIT = 3072
SHARE = 3200
ATTN_IN = ATTN + SMALL
ATTN_OUT = ATTN + 2 * SMALL
FF = 4096
TOTAL = 6656
QUARTER = TOTAL // 4
SCALE = HD ** (-0.5)
EPS = 1e-05
BF = jnp.bfloat16
F32 = jnp.float32
VM = pl.BlockSpec(memory_space=pltpu.VMEM)
HB = pl.BlockSpec(memory_space=pl.ANY)
FAR = pl.BlockSpec(memory_space=pltpu.HBM)


def _places():
    nat = lambda m, r, c: (m * 7 + r) * 16 + c
    halo = lambda m, r, c: (m * 3 + r) * 16 + c
    plain = np.zeros((TOK, NAT), np.float32)
    rolled = np.zeros((TOK, NAT), np.float32)
    rolled_halo = np.zeros((TOK, HALO), np.float32)
    first_rows = np.zeros((HALO, TOK), np.float32)
    last_rows = np.zeros((HALO, TOK), np.float32)
    for m in range(2):
        for w in range(2):
            for y in range(7):
                for x in range(7):
                    t = (m * 2 + w) * SPOT + y * 7 + x
                    col = w * 7 + x
                    plain[t, nat(m, y, col)] = 1
                    if y < SHIFT:
                        first_rows[halo(m, y, col), t] = 1
                    col = (col + SHIFT) % 14
                    if y + SHIFT < 7:
                        rolled[t, nat(m, y + SHIFT, col)] = 1
                    else:
                        rolled_halo[t, halo(m, y + SHIFT - 7, col)] = 1
                        last_rows[halo(m, y + SHIFT - 7, col), t] = 1
    return plain, rolled, rolled_halo, first_rows, last_rows


PLAIN, ROLLED, ROLLED_HALO, FIRST_ROWS, LAST_ROWS = _places()
ROLL = ROLLED @ PLAIN.T
PLAIN_HALO = np.zeros((TOK, HALO), np.float32)
for _r, _t in zip(*np.nonzero(FIRST_ROWS)):
    PLAIN_HALO[_t, _r] = 1


def _pairs():
    rel = np.full((SPOT, SPOT), -1)
    rows = np.zeros((SPOT, GROUPS * SPOT), np.float32)
    cols = np.zeros((SPOT, GROUPS * SPOT), np.float32)
    for a in range(49):
        for b in range(49):
            rel[a, b] = (a // 7 - b // 7 + 6) * 13 + a % 7 - b % 7 + 6
            for h in range(GROUPS):
                if (a // 7 >= 4) != (b // 7 >= 4):
                    rows[a, h * SPOT + b] = -100.0
                if (a % 7 >= 4) != (b % 7 >= 4):
                    cols[a, h * SPOT + b] = -100.0
    return rel, rows, cols


REL, MASK_ROWS, MASK_COLS = _pairs()
REL_HOT = (REL[None] == np.arange(192)[:, None, None]).astype(np.float32)
PACKED_REL = np.concatenate([REL[:32], REL[32:]], axis=1)
PACKED_HOT = (PACKED_REL.reshape(-1, 1) == np.arange(256)[None]).astype(np.float32)
EDGE = np.where(np.tile(np.arange(SPOT), GROUPS) < 49, 0.0, -1e30).astype(np.float32)
HEAD_LANES = np.repeat(np.kron(np.eye(GROUPS), np.ones((1, HD))), SPOT, axis=0).astype(np.float32)
SEGMENT = np.kron(np.eye(2), np.ones((SPOT, SPOT))).astype(np.float32)


def const(x):
    return jnp.asarray(x, BF)


def dot(a, b):
    return lax.dot_general(a, b, (((1,), (0,)), ((), ())), preferred_element_type=F32)


def dot_nt(a, b):
    return lax.dot_general(a, b, (((1,), (1,)), ((), ())), preferred_element_type=F32)


def dot_tn(a, b):
    return lax.dot_general(a, b, (((0,), (0,)), ((), ())), preferred_element_type=F32)


def halves(x):
    high = x.astype(BF)
    return high, (x - high.astype(F32)).astype(BF)


def place(hot, x):
    high = x.astype(BF)
    rest = x - high.astype(F32)
    mid = rest.astype(BF)
    low = (rest - mid.astype(F32)).astype(BF)
    return dot(hot, high) + dot(hot, mid) + dot(hot, low)


def segment_sum(x, seg):
    high, low = halves(x)
    parts = [
        dot(high[:, k : k + 128], seg) + dot(low[:, k : k + 128], seg) for k in (0, 128)
    ]
    return jnp.concatenate(parts, axis=1)


def segment_max(s):
    lane = lax.broadcasted_iota(jnp.int32, (SPOT, 128), 1)
    left = lane < SPOT
    parts = []
    for k in (0, 128):
        part = s[:, k : k + 128]
        one = jnp.max(jnp.where(left, part, -3e38), axis=1, keepdims=True)
        two = jnp.max(jnp.where(left, -3e38, part), axis=1, keepdims=True)
        parts.append(jnp.where(left, one, two))
    return jnp.concatenate(parts, axis=1)


def norm_parts(x):
    center = x - jnp.mean(x, axis=-1, keepdims=True)
    r = lax.rsqrt(jnp.mean(center * center, axis=-1, keepdims=True) + EPS)
    return center * r, r


def norm_back(dh, xhat, r, gain):
    e = dh * gain
    return r * (
        e
        - jnp.mean(e, axis=-1, keepdims=True)
        - xhat * jnp.mean(e * xhat, axis=-1, keepdims=True)
    )


def four(x, lanes):
    return jnp.concatenate([x] * GROUPS, axis=0) * lanes


def fold(x, lanes):
    x = x * lanes
    return x[:64] + x[64:128] + x[128:192] + x[192:]


def column_sum(x):
    return jnp.sum(x, axis=0, keepdims=True)


def me_shard():
    return lax.axis_index("shard")


def row_at(i, rows):
    return pl.ds(pl.multiple_of(i * rows, 32), 32)


def gathered(blocks):
    left, right = [], []
    for core in range(2):
        for m in range(4):
            for y in range(2):
                whose = 4 * m + 2 * y + core
                left.append((blocks[4 * core + m], 32 * y, whose))
                right.append((blocks[8 + 2 * core + y], 32 * m, whose))
    return left, right


def attn_copies(blocks, w, sem):
    me = me_shard()
    return [
        pltpu.make_async_copy(
            ref.at[row : row + 32, :ATTN],
            w.at[row_at(lax.bitwise_xor(me, whose), 32), :],
            sem.at[n],
        )
        for n, (ref, row, whose) in enumerate(gathered(blocks)[0])
    ]


def ff_copies(blocks, w1, w2, sem):
    out = []
    me = me_shard()
    left, right = gathered(blocks)
    first = SPLIT - ATTN
    for n, (ref, row, whose) in enumerate(left):
        rows = row_at(lax.bitwise_xor(me, whose), 32)
        out.append(
            pltpu.make_async_copy(
                ref.at[row : row + 32, ATTN:], w1.at[rows, :first], sem.at[n, 0]
            )
        )
    for n, (ref, row, whose) in enumerate(right):
        i = lax.bitwise_xor(me, whose)
        out.append(
            pltpu.make_async_copy(
                ref.at[row : row + 32, : MLP - first],
                w1.at[row_at(i, 32), first:],
                sem.at[n, 1],
            )
        )
        for j in range(4):
            at = MLP - first + 512 * j
            out.append(
                pltpu.make_async_copy(
                    ref.at[row : row + 32, at : at + 512],
                    w2.at[row_at(4 * i + j, 32), :],
                    sem.at[n, 2 + j],
                )
            )
    return out


def share_copies(grads, mine, theirs, sem):
    core = lax.rem(me_shard(), 2)
    out = []
    for q in range(8):
        for n, (target, bit) in enumerate(((mine, core), (theirs, 1 - core))):
            at = pl.multiple_of((2 * q + bit) * 32, 32)
            out.append(
                pltpu.make_async_copy(
                    grads.at[pl.ds(at, 32), :],
                    target.at[32 * q : 32 * q + 32, :],
                    sem.at[q, n],
                )
            )
    return out


def pack_kernel(*refs):
    qkv_w, proj, fc1, fc2, gain, shift, qkv_b, out_b, fc1_b, table = refs[:10]
    left, right, stack, sem = refs[10:]
    first = SPLIT - ATTN
    copies = []
    for level in range(2):
        base = SPLIT * level
        pairs = [
            (qkv_w.at[level], left.at[:, base : base + 3 * C]),
            (proj.at[level], left.at[:, base + 3 * C : base + ATTN]),
            (fc1.at[level, :, :first], left.at[:, base + ATTN : base + SPLIT]),
            (fc1.at[level, :, first:], right.at[:, base : base + MLP - first]),
        ]
        for j in range(4):
            at = base + MLP - first + 512 * j
            pairs.append((fc2.at[level, 32 * j : 32 * j + 32, :], right.at[:, at : at + 512]))
        copies += [
            pltpu.make_async_copy(a, b, sem.at[level, n]) for n, (a, b) in enumerate(pairs)
        ]
    for c in copies:
        c.start()
    stack[...] = jnp.zeros((SMALL, SMALL), F32)
    for level in range(2):
        for n, ref in enumerate((gain, shift, qkv_b, out_b)):
            at = 8 * level + 2 * n
            stack[at : at + 2, :32] = ref[level].astype(F32)
        for j in range(4):
            at = 16 + 4 * level + j
            stack[at : at + 1, :32] = fc1_b[level : level + 1, 32 * j : 32 * j + 32].astype(F32)
        for j in range(6):
            at = 24 + 6 * level + j
            width = min(32, 169 - 32 * j)
            stack[at : at + 1, :width] = table[level, :, 32 * j : 32 * j + width].astype(F32)
    right[:, 2 * SPLIT :] = stack[...].T[:32, :].astype(BF)
    for c in copies:
        c.wait()


def params_kernel(small, out, scratch):
    me = me_shard()
    for t in range(16):
        at = 128 * (t // 2 % 2) + 256 * (t % 2) + 32 * (t // 4)
        scratch[row_at(lax.bitwise_xor(me, t), 32), :] = small[at : at + 32, :].astype(F32)
    out[...] = scratch[...].T


def attn_forward_kernel(level, *refs):
    if level == 0:
        img, spread = refs[:2]
        refs = refs[2:]
    else:
        own, halo, spread_halo, mask_rows, mask_cols = refs[:5]
        refs = refs[5:]
    params, bias, lanes_ref, seg_ref = refs[:4]
    blocks, refs = refs[4:-8], refs[-8:]
    x_out, x1_out, h_out, qkv, a_out, o_out, w, sem = refs
    copies = attn_copies(blocks, w, sem)
    for c in copies:
        c.start()
    if level == 0:
        x = dot(spread[...], img[...])
    else:
        x = own[...] + dot(spread_halo[...], halo[...])
    x_out[...] = x
    row = 8 * level
    xhat, _ = norm_parts(x)
    h = (xhat * params[row : row + 1, :] + params[row + 2 : row + 3, :]).astype(BF)
    h_out[...] = h
    for c in copies:
        c.wait()
    qkv[:, :C] = (dot(h, w[:, :C]) + params[row + 4 : row + 5, :]).astype(BF)
    qkv[:, C : 2 * C] = dot(h, w[:, C : 2 * C]).astype(BF)
    qkv[:, 2 * C :] = (dot(h, w[:, 2 * C : 3 * C]) + params[row + 5 : row + 6, :]).astype(BF)
    lanes = lanes_ref[...]
    seg = seg_ref[...]
    if level == 1:
        last = (lax.axis_index("seq") == 7).astype(F32)
        row_mask = mask_rows[...] * last
        both_mask = jnp.minimum(row_mask, mask_cols[...])
    groups = range(GROUPS)
    for window in range(WINDOWS):
        rows = slice(window * SPOT, (window + 1) * SPOT)
        q, k, v = (
            [qkv[rows, C * n + 128 * g : C * n + 128 * g + 128] for g in groups] for n in range(3)
        )
        s = [dot_nt(q[g], four(k[g], lanes)) * SCALE + bias[g] for g in groups]
        if level == 1:
            mask = both_mask if window % 2 else row_mask
            s = [t + mask for t in s]
        top = [segment_max(t) for t in s]
        e = [jnp.exp(s[g] - top[g]) for g in groups]
        total = [segment_sum(t, seg) for t in e]
        a = [e[g] / total[g] for g in groups]
        o = [dot(a[g].astype(BF), four(v[g], lanes)).astype(BF) for g in groups]
        for g in groups:
            a_out[window * GROUPS + g] = a[g]
            o_out[rows, 128 * g : 128 * g + 128] = o[g]
    x1_out[...] = x + (dot(o_out[...], w[:, 3 * C :]) + params[row + 6 : row + 7, :])


def ff_forward_kernel(level, *refs):
    x1_ref, params, fc1_b, send_hot, out_hot = refs[:5]
    refs = refs[5:]
    blocks, refs = refs[:-8], refs[-8:]
    result, send, h2_out, g_out, gp_out, w1, w2, sem = refs
    copies = ff_copies(blocks, w1, w2, sem)
    for c in copies:
        c.start()
    row = 8 * level
    x1 = x1_ref[...]
    xhat, _ = norm_parts(x1)
    h2 = (xhat * params[row + 1 : row + 2, :] + params[row + 3 : row + 4, :]).astype(BF)
    h2_out[...] = h2
    for c in copies:
        c.wait()
    total = x1 + params[row + 7 : row + 8, :]
    for n in range(4):
        cols = slice(512 * n, 512 * n + 512)
        f = dot(h2, w1[:, cols]) + fc1_b[:, cols]
        phi = 0.5 * (1.0 + lax.erf(f * (0.5**0.5)))
        g = (f * phi).astype(BF)
        g_out[:, cols] = g
        gp_out[:, cols] = (phi + f * (jnp.exp(f * f * -0.5) * 0.3989422804014327)).astype(BF)
        total = total + dot(g, w2[cols, :])
    send[...] = dot(send_hot[...], total.astype(BF)).astype(BF)
    result[...] = place(out_hot[...], total)


def ff_backward_kernel(level, *refs):
    if level == 1:
        cot, halo, spread, spread_halo = refs[:4]
        refs = refs[4:]
    else:
        own, halo, spread_halo = refs[:3]
        refs = refs[3:]
    x1_ref, h2_ref, g_ref, gp_ref, params, pick = refs[:6]
    blocks, refs = refs[6:-10], refs[-10:]
    g1_out, rows_out, col_out, mine, theirs, w1, w2, grads, sem, share_sem = refs
    copies = ff_copies(blocks, w1, w2, sem)
    for c in copies:
        c.start()
    if level == 1:
        g2 = dot(spread[...], cot[...]) + dot(spread_halo[...], halo[...])
    else:
        g2 = own[...] + dot(spread_halo[...], halo[...])
    dz = g2.astype(BF)
    row = 8 * level
    xhat, r = norm_parts(x1_ref[...])
    h2 = h2_ref[...]
    ones = jnp.ones((TOK, 128), BF)
    for c in copies:
        c.wait()
    dh2 = jnp.zeros((TOK, C), F32)
    col_out[...] = jnp.zeros((C, SMALL), F32)
    lane = lax.broadcasted_iota(jnp.int32, (32, SMALL), 1)
    for n in range(4):
        cols = slice(512 * n, 512 * n + 512)
        d = dot_tn(g_ref[:, cols], dz).astype(BF)
        for i in range(4):
            for j in range(4):
                at = 128 * i + 32 * j
                to = 32 * (4 * n + i)
                grads[to : to + 32, MLP + 512 * j : MLP + 512 * j + 512] = d[at : at + 32, :]
        df = (dot_nt(dz, w2[cols, :]) * gp_ref[:, cols].astype(F32)).astype(BF)
        grads[:, cols] = dot_tn(h2, df).astype(BF)
        sums = dot_tn(df, ones)
        for i in range(4):
            to = 32 * (4 * n + i)
            picked = jnp.zeros((32, SMALL), F32)
            for j in range(4):
                at = 128 * i + 32 * j
                picked = picked + jnp.where(lane == 8 + j, sums[at : at + 32, :], 0.0)
            col_out[to : to + 32, :] = picked
        dh2 = dh2 + dot_nt(df, w1[:, cols])
    shares = share_copies(grads, mine, theirs, share_sem)
    for c in shares:
        c.start()
    g1_out[...] = g2 + norm_back(dh2, xhat, r, params[row + 1 : row + 2, :])
    rows_out[...] = jnp.zeros((8, C), F32)
    rows_out[1:2, :] = column_sum(dh2 * xhat)
    rows_out[3:4, :] = column_sum(dh2)
    rows_out[7:8, :] = column_sum(dz.astype(F32))
    for c in shares:
        c.wait()


def attn_backward_kernel(level, *refs):
    g1_ref, x_ref, h_ref, qkv, a_ref, o_ref, params, rows_ref, col_ref = refs[:9]
    lanes_ref, seg_ref, back_hot = refs[9:12]
    refs = refs[12:]
    if level == 1:
        send_hot = refs[0]
        refs = refs[1:]
    blocks, refs = refs[:12], refs[12:]
    others = None
    if level == 1:
        send = refs[0]
        refs = refs[1:]
    else:
        others = refs[0]
        refs = refs[1:]
    back, mine, theirs, w, grads, d_qkv, stack, ds_all, sem, share_sem = refs
    passed = []
    if others is not None:
        passed.append(
            pltpu.make_async_copy(others, theirs.at[:, :FF], share_sem.at[8, 0])
        )
        passed[0].start()
        theirs = theirs.at[:, FF:]
    copies = attn_copies(blocks, w, sem)
    for c in copies:
        c.start()
    row = 8 * level
    g1 = g1_ref[...]
    dy = g1.astype(BF)
    grads[:, 3 * C : 4 * C] = dot_tn(o_ref[...], dy).astype(BF)
    stack[...] = jnp.zeros((SMALL, C), F32)
    stack[0:8, :] = rows_ref[...]
    stack[6:7, :] = column_sum(dy.astype(F32))
    xhat, r = norm_parts(x_ref[...])
    lanes = lanes_ref[...]
    lanes_f = lanes.astype(F32)
    seg = seg_ref[...]
    for c in copies:
        c.wait()
    do_all = dot_nt(dy, w[:, 3 * C :]).astype(BF)
    lane = lax.broadcasted_iota(jnp.int32, (32, 128), 1)
    groups = range(GROUPS)
    for window in range(WINDOWS):
        rows = slice(window * SPOT, (window + 1) * SPOT)
        q, k, v = (
            [qkv[rows, C * n + 128 * g : C * n + 128 * g + 128] for g in groups] for n in range(3)
        )
        do = [do_all[rows, 128 * g : 128 * g + 128] for g in groups]
        a = [a_ref[window * GROUPS + g] for g in groups]
        da = [dot_nt(do[g], four(v[g], lanes)) for g in groups]
        total = [segment_sum(a[g] * da[g], seg) for g in groups]
        dv = [fold(dot_tn(a[g].astype(BF), do[g]), lanes_f) for g in groups]
        ds = [(a[g] * (da[g] - total[g])).astype(BF) for g in groups]
        dq = [dot(ds[g], four(k[g], lanes)) * SCALE for g in groups]
        dk = [fold(dot_tn(ds[g], q[g]), lanes_f) * SCALE for g in groups]
        for g in groups:
            at = 128 * g
            d_qkv[rows, at : at + 128] = dq[g].astype(BF)
            d_qkv[rows, C + at : C + at + 128] = dk[g].astype(BF)
            d_qkv[rows, 2 * C + at : 2 * C + at + 128] = dv[g].astype(BF)
            if window == 0:
                ds_all[g] = ds[g].astype(F32)
            else:
                ds_all[g] = ds_all[g] + ds[g].astype(F32)
    for g in groups:
        ds_sum = ds_all[g]
        for pair in range(2):
            top = ds_sum[:32, 128 * pair : 128 * pair + 128]
            low = ds_sum[32:, 128 * pair : 128 * pair + 128]
            even = jnp.where(lane < 64, top, pltpu.roll(low, 64, 1))
            odd = jnp.where(lane < 64, pltpu.roll(top, 64, 1), low)
            head = 4 * g + 2 * pair
            grads[32 * head : 32 * head + 32, ATTN_IN:] = even.astype(BF)
            grads[32 * head + 32 : 32 * head + 64, ATTN_IN:] = odd.astype(BF)
    h = h_ref[...]
    for n in range(3):
        cols = slice(C * n, C * n + C)
        grads[:, cols] = dot_tn(h, d_qkv[:, cols]).astype(BF)
    stack[4:5, :] = column_sum(d_qkv[:, :C].astype(F32))
    stack[5:6, :] = column_sum(d_qkv[:, 2 * C :].astype(F32))
    dh = dot_nt(d_qkv[...], w[:, : 3 * C])
    stack[0:1, :] = column_sum(dh * xhat)
    stack[2:3, :] = column_sum(dh)
    grads[:, ATTN:ATTN_IN] = (stack[...].T + col_ref[...]).astype(BF)
    shares = share_copies(grads, mine, theirs, share_sem)
    for c in shares:
        c.start()
    total = g1 + norm_back(dh, xhat, r, params[row : row + 1, :])
    if level == 1:
        send[...] = dot(send_hot[...], total.astype(BF)).astype(BF)
    back[...] = place(back_hot[...], total)
    for c in shares + passed:
        c.wait()


def pair_kernel(*refs):
    shares, outs = list(refs[:-6]), refs[-6:]
    if len(shares) == 3:
        whole = shares[2]
        shares = [shares[0], whole.at[:, :FF], shares[1], whole.at[:, FF:]]
    chip = lax.div(me_shard(), 2)
    for m in range(4):
        for y in range(2):
            rows = row_at(lax.bitwise_xor(chip, 2 * m + y), 32)
            left, right = outs[m], outs[4 + y]
            for mine, other, start, width in (
                (shares[0], shares[1], 0, FF),
                (shares[2], shares[3], FF, ATTN_OUT),
            ):
                total = (mine[rows, :].astype(F32) + other[rows, :].astype(F32)).astype(BF)
                cut = max(0, min(width, SHARE - start))
                if cut:
                    left[32 * y : 32 * y + 32, start : start + cut] = total[:, :cut]
                if cut < width:
                    at = start + cut - SHARE
                    right[32 * m : 32 * m + 32, at : at + width - cut] = total[:, cut:]


def added(refs):
    return functools.reduce(jnp.add, [r[...].astype(F32) for r in refs])


def middle_kernel(*refs):
    outs = refs[6:]
    left = added(refs[:4]).astype(BF)
    for y in range(2):
        outs[y][...] = left[32 * y : 32 * y + 32, :]
    right = added(refs[4:6]).astype(BF)
    for m in range(4):
        outs[2 + m][...] = right[32 * m : 32 * m + 32, :]


def z_part(ref, k):
    p = lax.bitwise_xor(lax.div(lax.axis_index("seq"), 2), k)
    return ref.at[:, pl.ds(pl.multiple_of(p * QUARTER, 128), QUARTER)]


def split_kernel(*refs):
    pieces, outs = refs[:6], refs[6:10]
    total, sem = refs[10:]
    total[:, :SHARE] = added(pieces[:2]).astype(BF)
    total[:, SHARE : 2 * SHARE] = added(pieces[2:]).astype(BF)
    total[:, 2 * SHARE :] = jnp.zeros((32, TOTAL - 2 * SHARE), BF)
    copies = [pltpu.make_async_copy(z_part(total, k), outs[k], sem.at[k]) for k in range(4)]
    for c in copies:
        c.start()
    for c in copies:
        c.wait()


def finish_kernel(*refs):
    pieces, hot = refs[:8], refs[8]
    gain, shift, qkv_w, qkv_b, table, proj, out_b, fc1, fc1_b, fc2 = refs[9:19]
    scratch, sem = refs[19:]
    copies = [
        pltpu.make_async_copy(
            pieces[4 * level + k], z_part(scratch.at[level], k), sem.at[level, k]
        )
        for level in range(2)
        for k in range(4)
    ]
    for c in copies:
        c.start()
    for c in copies:
        c.wait()
    total = scratch[...]
    for level in range(2):
        fc1[level] = total[level, :, :MLP].astype(F32)
        for j in range(4):
            fc2[level, 32 * j : 32 * j + 32, :] = total[
                level, :, MLP + 512 * j : MLP + 512 * j + 512
            ].astype(F32)
        qkv_w[level] = total[level, :, FF : FF + 3 * C].astype(F32)
        proj[level] = total[level, :, FF + 3 * C : FF + 4 * C].astype(F32)
        small = total[level, :, FF + ATTN : FF + ATTN_IN].astype(F32).T
        gain[level] = small[0:2, :]
        shift[level] = small[2:4, :]
        qkv_b[level] = small[4:6, :]
        out_b[level] = small[6:8, :]
        fc1_b[level : level + 1, :] = jnp.concatenate(
            [small[8 + j : 9 + j, :] for j in range(4)], axis=1
        )
        ds = total[level, :, FF + ATTN_IN : FF + ATTN_OUT]
        flat = jnp.concatenate([ds[r : r + 1, :] for r in range(32)], axis=1)
        sums = dot(jnp.broadcast_to(flat.astype(F32), (16, 4096)).astype(BF), hot[...])
        table[level] = sums[0:1, :169]


def sds(shape, dtype):
    return jax.ShapeDtypeStruct(shape, dtype)


def call(kernel, ins, outs, scratch, args, flops=0, room=32):
    return pl.pallas_call(
        kernel,
        out_shape=tuple(s for s, _ in outs),
        in_specs=ins,
        out_specs=tuple(m for _, m in outs),
        scratch_shapes=scratch,
        compiler_params=pltpu.CompilerParams(vmem_limit_bytes=room * 1024 * 1024),
        cost_estimate=pl.CostEstimate(flops=8 * flops, bytes_accessed=8000000, transcendentals=0),
    )(*args)


def shard_permute(x, k):
    return lax.ppermute(x, "shard", [(i, i ^ k) for i in range(16)])


def core_permute(x):
    return shard_permute(x, 1)


def y_permute(x):
    return shard_permute(x, 2)


def x_permutes(pieces):
    return [shard_permute(p, 4 * k) for k, p in enumerate(pieces, 1)]


def seq_permute(x, k):
    return lax.ppermute(x, "seq", [(i, i ^ k) for i in range(8)])


def z_permutes(pieces):
    return [seq_permute(p, 2 * k) for k, p in enumerate(pieces, 1)]


def passed_along(x, by):
    return lax.ppermute(x, "seq", [(i, (i + by) % 8) for i in range(8)])


def gather_second(left_pair, right_row):
    return [left_pair] + x_permutes([left_pair] * 3), [right_row, y_permute(right_row)]


def with_other_core(blocks):
    return blocks + [core_permute(b) for b in blocks]


def pair_sums(shares):
    return call(
        pair_kernel,
        [VM] * len(shares),
        [(sds((64, SHARE), BF), VM)] * 4 + [(sds((128, SHARE), BF), VM)] * 2,
        [],
        shares,
    )


def x_first(pieces):
    left, right = list(pieces[:4]), list(pieces[4:])
    return left[:1] + x_permutes(left[1:]) + right[:1] + [y_permute(right[1])]


def middle_sums(arrived):
    return call(middle_kernel, [VM] * 6, [(sds((32, SHARE), BF), VM)] * 6, [], arrived)


def end_sums(pieces):
    left, right = list(pieces[:2]), list(pieces[2:])
    arrived = left[:1] + [y_permute(left[1])] + right[:1] + x_permutes(right[1:])
    return call(
        split_kernel,
        [VM] * 6,
        [(sds((32, QUARTER), BF), HB)] * 4,
        [pltpu.VMEM((32, TOTAL), BF), pltpu.SemaphoreType.DMA((4,))],
        arrived,
    )


def total_of(parts):
    return functools.reduce(jnp.add, [p.astype(F32) for p in parts]).astype(BF)


def seq_sum(pieces):
    own = total_of([pieces[0]] + z_permutes(pieces[1:]))
    own = total_of([own, seq_permute(own, 1)])
    return [own] + z_permutes([own] * 3)


def on_device(
    images,
    norm_gain,
    norm_shift,
    qkv_weight,
    qkv_bias,
    rel_table,
    proj_weight,
    out_bias,
    fc1_weight,
    fc1_bias,
    fc2_weight,
    cotangent,
):
    left, right = call(
        pack_kernel,
        [FAR] * 4 + [VM] * 6,
        [(sds((32, 2 * SPLIT), BF), VM), (sds((32, 2 * SPLIT + SMALL), BF), VM)],
        [pltpu.VMEM((SMALL, SMALL), F32), pltpu.SemaphoreType.DMA((2, 8))],
        (
            qkv_weight,
            proj_weight,
            fc1_weight,
            fc2_weight,
            norm_gain,
            norm_shift,
            qkv_bias,
            out_bias,
            fc1_bias,
            rel_table,
        ),
        room=60,
    )
    lefts, rights = [left, y_permute(left)], [right] + x_permutes([right] * 3)
    lefts, rights = lax.optimization_barrier((lefts, rights))
    small = jnp.concatenate([b[:, 2 * SPLIT :] for b in rights], axis=0)
    for permute in (y_permute, core_permute):
        small = jnp.concatenate([small, permute(small)], axis=0)

    def joined(level):
        cols = slice(SPLIT * level, SPLIT * level + SPLIT)
        return tuple(jnp.concatenate([b[:, cols] for b in bs], axis=0) for bs in (lefts, rights))

    pair_two, row_two = joined(1)
    left_one, right_one = gather_second(*joined(0))
    left_one, right_one, pair_two, row_two = lax.optimization_barrier(
        (left_one, right_one, pair_two, row_two)
    )
    left_two, right_two = gather_second(pair_two, row_two)

    def natural(x):
        return jnp.pad(x, ((0, 0), (0, 0), (0, 2), (0, 0))).reshape(-1, C)

    img = natural(images)
    cot = natural(cotangent)
    cot_halo = passed_along(natural(cotangent[:, :SHIFT]), -1)

    (params,) = call(params_kernel, [VM], [(sds((SMALL, C), F32), VM)], [pltpu.VMEM((C, SMALL), F32)], (small,))
    tables = params[24:36].reshape(2, 6, HEADS, 32).transpose(0, 2, 1, 3).reshape(32, 192)
    bias_all = lax.dot_general(
        tables.astype(BF),
        const(REL_HOT),
        (((1,), (0,)), ((), ())),
        preferred_element_type=F32,
    )
    bias_all = bias_all.reshape(2, GROUPS, 4, SPOT, SPOT).transpose(0, 1, 3, 2, 4)
    bias_all = bias_all.reshape(2, GROUPS, SPOT, 256) + jnp.asarray(EDGE)
    fc1_b = params[16:24].reshape(2, 4, 16, 32).transpose(0, 2, 1, 3).reshape(2, 1, MLP)

    lanes = const(HEAD_LANES)
    seg = const(SEGMENT)
    tokens = sds((TOK, C), F32)
    tokens_low = sds((TOK, C), BF)
    hidden_low = sds((TOK, MLP), BF)
    halo_low = sds((HALO, C), BF)

    def attn_forward(level, lead, blocks):
        outs = [
            (tokens, VM),
            (tokens, VM),
            (tokens_low, VM),
            (sds((TOK, 3 * C), BF), VM),
            (sds((16, SPOT, 256), F32), VM),
            (tokens_low, VM),
        ]
        return call(
            functools.partial(attn_forward_kernel, level),
            [VM] * (len(lead) + 4) + [HB] * len(blocks),
            outs,
            [pltpu.VMEM((C, ATTN), BF), pltpu.SemaphoreType.DMA((16,))],
            tuple(lead) + (params, bias_all[level], lanes, seg) + tuple(blocks),
            flops=2 * TOK * C * ATTN,
        )

    def ff_scratch():
        return [pltpu.VMEM((C, MLP), BF), pltpu.VMEM((MLP, C), BF)]

    def ff_forward(level, x1, blocks):
        lead = (x1, params, fc1_b[level])
        if level == 0:
            lead += (const(FIRST_ROWS), const(ROLL))
            out = tokens
        else:
            lead += (const(LAST_ROWS), const(ROLLED.T))
            out = sds((NAT, C), F32)
        return call(
            functools.partial(ff_forward_kernel, level),
            [VM] * len(lead) + [HB] * len(blocks),
            [(out, VM), (halo_low, VM), (tokens_low, VM), (hidden_low, VM), (hidden_low, VM)],
            ff_scratch() + [pltpu.SemaphoreType.DMA((16, 6))],
            lead + tuple(blocks),
            flops=4 * TOK * C * MLP,
        )

    def ff_backward(level, lead, saved, blocks):
        shares = sds((256, FF), BF)
        return call(
            functools.partial(ff_backward_kernel, level),
            [VM] * (len(lead) + 6) + [HB] * len(blocks),
            [
                (tokens, VM),
                (sds((8, C), F32), VM),
                (sds((C, SMALL), F32), VM),
                (shares, HB),
                (shares, HB),
            ],
            ff_scratch()
            + [
                pltpu.VMEM((C, FF), BF),
                pltpu.SemaphoreType.DMA((16, 6)),
                pltpu.SemaphoreType.DMA((8, 2)),
            ],
            tuple(lead) + tuple(saved) + (params, lanes) + tuple(blocks),
            flops=8 * TOK * C * MLP,
        )

    def attn_backward(level, g1, saved, rows, cols, hots, blocks, others=()):
        shares = sds((256, ATTN_OUT), BF)
        sent = shares if level == 1 else sds((256, FF + ATTN_OUT), BF)
        outs = [(halo_low, VM)] if level == 1 else []
        outs.append((tokens if level == 1 else sds((NAT, C), F32), VM))
        return call(
            functools.partial(attn_backward_kernel, level),
            [VM] * (11 + len(hots)) + [HB] * (len(blocks) + len(others)),
            outs + [(shares, HB), (sent, HB)],
            [
                pltpu.VMEM((C, ATTN), BF),
                pltpu.VMEM((C, ATTN_OUT), BF),
                pltpu.VMEM((TOK, 3 * C), BF),
                pltpu.VMEM((SMALL, C), F32),
                pltpu.VMEM((GROUPS, SPOT, 256), F32),
                pltpu.SemaphoreType.DMA((16,)),
                pltpu.SemaphoreType.DMA((9, 2)),
            ],
            (g1,) + tuple(saved) + (params, rows, cols, lanes, seg) + tuple(hots) + tuple(blocks) + others,
            flops=4 * TOK * C * ATTN,
        )

    left_one, right_one, bias_all, fc1_b, img = lax.optimization_barrier(
        (left_one, right_one, bias_all, fc1_b, img)
    )
    all_one = with_other_core(left_one) + with_other_core(right_one)
    x_one, x1_one, *attn_saved_one = attn_forward(0, (img, const(PLAIN)), all_one)
    mid, send, *ff_saved_one = ff_forward(0, x1_one, all_one)
    mid, left_two, right_two = lax.optimization_barrier((mid, left_two, right_two))
    all_two = with_other_core(left_two) + with_other_core(right_two)
    lead = (
        mid,
        passed_along(send, -1),
        const(ROLLED_HALO),
        jnp.asarray(MASK_ROWS),
        jnp.asarray(MASK_COLS),
    )
    x_two, x1_two, *attn_saved_two = attn_forward(1, lead, all_two)
    own_rows, send, *ff_saved_two = ff_forward(1, x1_two, all_two)
    returned = passed_along(send, 1).astype(F32).reshape(2, SHIFT, 16, C)
    outputs = jnp.concatenate(
        [returned, own_rows.reshape(2, 7, 16, C)[:, SHIFT:]], axis=1
    )[:, :, :14]

    g1, rows, cols, mine, theirs = ff_backward(
        1,
        (cot, cot_halo, const(ROLLED), const(ROLLED_HALO)),
        (x1_two, *ff_saved_two),
        all_two,
    )
    shares_two = (mine, core_permute(theirs))
    g1, outputs = lax.optimization_barrier((g1, outputs))
    send, own, mine, theirs = attn_backward(
        1,
        g1,
        (x_two, *attn_saved_two),
        rows,
        cols,
        (const(ROLL.T), const(LAST_ROWS)),
        all_two,
    )
    pieces_two = pair_sums(shares_two + (mine, core_permute(theirs)))
    own, pieces_two = lax.optimization_barrier((own, pieces_two))
    g1, rows, cols, mine, theirs = ff_backward(
        0,
        (own, passed_along(send, 1), const(PLAIN_HALO)),
        (x1_one, *ff_saved_one),
        all_one,
    )
    input_grad, mine_attn, theirs = attn_backward(
        0, g1, (x_one, *attn_saved_one), rows, cols, (const(PLAIN.T),), all_one, (theirs,)
    )
    arrived, mine, mine_attn, theirs = lax.optimization_barrier(
        (x_first(pieces_two), mine, mine_attn, theirs)
    )
    pieces_two = middle_sums(arrived)
    pieces_one, pieces_two = lax.optimization_barrier(
        (pair_sums((mine, mine_attn, core_permute(theirs))), end_sums(pieces_two))
    )
    pieces_one = end_sums(middle_sums(x_first(pieces_one)))
    sums_two = seq_sum(pieces_two)
    sums_one = seq_sum(pieces_one)
    shapes = [
        (2, 2, 32),
        (2, 2, 32),
        (2, 32, 3 * C),
        (2, 2, 32),
        (2, 1, 169),
        (2, 32, C),
        (2, 2, 32),
        (2, 32, MLP),
        (2, 128),
        (2, 128, C),
    ]
    grads = call(
        finish_kernel,
        [HB] * 8 + [VM],
        [(sds(shape, F32), VM) for shape in shapes],
        [pltpu.VMEM((2, 32, TOTAL), BF), pltpu.SemaphoreType.DMA((2, 4))],
        tuple(sums_one) + tuple(sums_two) + (const(PACKED_HOT),),
    )
    input_grad = input_grad.reshape(2, 7, 16, C)[:, :, :14]
    return (outputs, input_grad) + tuple(grads)


def solution(mesh):
    return jax.shard_map(
        on_device,
        mesh=mesh,
        in_specs=(
            P("shard", "seq", None, None),
            P(None, None, "shard"),
            P(None, None, "shard"),
            P(None, "shard", None),
            P(None, None, "shard"),
            P(None, "shard", None),
            P(None, "shard", None),
            P(None, None, "shard"),
            P(None, "shard", None),
            P(None, "shard"),
            P(None, "shard", None),
            P("shard", "seq", None, None),
        ),
        out_specs=(
            P("shard", "seq", None, None),
            P("shard", "seq", None, None),
            P(None, None, "shard"),
            P(None, None, "shard"),
            P(None, "shard", None),
            P(None, None, "shard"),
            P(None, "shard", None),
            P(None, "shard", None),
            P(None, None, "shard"),
            P(None, "shard", None),
            P(None, "shard"),
            P(None, "shard", None),
        ),
        check_vma=False,
    )
```

```python
import functools

import jax
import jax.numpy as jnp
import numpy as np
from jax import lax
from jax.experimental import pallas as pl
from jax.experimental.pallas import tpu as pltpu
from jax.sharding import PartitionSpec as P

C = 512
HEADS = 16
HD = 32
MLP = 2048
WIN = 7
SHIFT = 3
SPOT = 64
WINDOWS = 4
TOK = WINDOWS * SPOT
GROUPS = 4
NAT = 2 * 7 * 16
HALO = 2 * 3 * 16
SMALL = 128
ATTN = 2048
SPLIT = 3072
SHARE = 3200
ATTN_IN = ATTN + SMALL
ATTN_OUT = ATTN + 2 * SMALL
FF = 4096
TOTAL = 6656
QUARTER = TOTAL // 4
SCALE = HD ** (-0.5)
EPS = 1e-05
BF = jnp.bfloat16
F32 = jnp.float32
VM = pl.BlockSpec(memory_space=pltpu.VMEM)
HB = pl.BlockSpec(memory_space=pl.ANY)
FAR = pl.BlockSpec(memory_space=pltpu.HBM)


def _places():
    nat = lambda m, r, c: (m * 7 + r) * 16 + c
    halo = lambda m, r, c: (m * 3 + r) * 16 + c
    plain = np.zeros((TOK, NAT), np.float32)
    rolled = np.zeros((TOK, NAT), np.float32)
    rolled_halo = np.zeros((TOK, HALO), np.float32)
    first_rows = np.zeros((HALO, TOK), np.float32)
    last_rows = np.zeros((HALO, TOK), np.float32)
    for m in range(2):
        for w in range(2):
            for y in range(7):
                for x in range(7):
                    t = (m * 2 + w) * SPOT + y * 7 + x
                    col = w * 7 + x
                    plain[t, nat(m, y, col)] = 1
                    if y < SHIFT:
                        first_rows[halo(m, y, col), t] = 1
                    col = (col + SHIFT) % 14
                    if y + SHIFT < 7:
                        rolled[t, nat(m, y + SHIFT, col)] = 1
                    else:
                        rolled_halo[t, halo(m, y + SHIFT - 7, col)] = 1
                        last_rows[halo(m, y + SHIFT - 7, col), t] = 1
    return plain, rolled, rolled_halo, first_rows, last_rows


PLAIN, ROLLED, ROLLED_HALO, FIRST_ROWS, LAST_ROWS = _places()
ROLL = ROLLED @ PLAIN.T
PLAIN_HALO = np.zeros((TOK, HALO), np.float32)
for _r, _t in zip(*np.nonzero(FIRST_ROWS)):
    PLAIN_HALO[_t, _r] = 1


def _pairs():
    rel = np.full((SPOT, SPOT), -1)
    rows = np.zeros((SPOT, GROUPS * SPOT), np.float32)
    cols = np.zeros((SPOT, GROUPS * SPOT), np.float32)
    for a in range(49):
        for b in range(49):
            rel[a, b] = (a // 7 - b // 7 + 6) * 13 + a % 7 - b % 7 + 6
            for h in range(GROUPS):
                if (a // 7 >= 4) != (b // 7 >= 4):
                    rows[a, h * SPOT + b] = -100.0
                if (a % 7 >= 4) != (b % 7 >= 4):
                    cols[a, h * SPOT + b] = -100.0
    return rel, rows, cols


REL, MASK_ROWS, MASK_COLS = _pairs()
REL_HOT = (REL[None] == np.arange(192)[:, None, None]).astype(np.float32)
PACKED_REL = np.concatenate([REL[:32], REL[32:]], axis=1)
PACKED_HOT = (PACKED_REL.reshape(-1, 1) == np.arange(256)[None]).astype(np.float32)
EDGE = np.where(np.tile(np.arange(SPOT), GROUPS) < 49, 0.0, -1e30).astype(np.float32)
HEAD_LANES = np.repeat(np.kron(np.eye(GROUPS), np.ones((1, HD))), SPOT, axis=0).astype(np.float32)
SEGMENT = np.kron(np.eye(2), np.ones((SPOT, SPOT))).astype(np.float32)


def const(x):
    return jnp.asarray(x, BF)


def dot(a, b):
    return lax.dot_general(a, b, (((1,), (0,)), ((), ())), preferred_element_type=F32)


def dot_nt(a, b):
    return lax.dot_general(a, b, (((1,), (1,)), ((), ())), preferred_element_type=F32)


def dot_tn(a, b):
    return lax.dot_general(a, b, (((0,), (0,)), ((), ())), preferred_element_type=F32)


def halves(x):
    high = x.astype(BF)
    return high, (x - high.astype(F32)).astype(BF)


def place(hot, x):
    high = x.astype(BF)
    rest = x - high.astype(F32)
    mid = rest.astype(BF)
    low = (rest - mid.astype(F32)).astype(BF)
    return dot(hot, high) + dot(hot, mid) + dot(hot, low)


def segment_sum(x, seg):
    high, low = halves(x)
    parts = [
        dot(high[:, k : k + 128], seg) + dot(low[:, k : k + 128], seg) for k in (0, 128)
    ]
    return jnp.concatenate(parts, axis=1)


def segment_max(s):
    lane = lax.broadcasted_iota(jnp.int32, (SPOT, 128), 1)
    left = lane < SPOT
    parts = []
    for k in (0, 128):
        part = s[:, k : k + 128]
        one = jnp.max(jnp.where(left, part, -3e38), axis=1, keepdims=True)
        two = jnp.max(jnp.where(left, -3e38, part), axis=1, keepdims=True)
        parts.append(jnp.where(left, one, two))
    return jnp.concatenate(parts, axis=1)


def norm_parts(x):
    center = x - jnp.mean(x, axis=-1, keepdims=True)
    r = lax.rsqrt(jnp.mean(center * center, axis=-1, keepdims=True) + EPS)
    return center * r, r


def norm_back(dh, xhat, r, gain):
    e = dh * gain
    return r * (
        e
        - jnp.mean(e, axis=-1, keepdims=True)
        - xhat * jnp.mean(e * xhat, axis=-1, keepdims=True)
    )


def four(x, lanes):
    return jnp.concatenate([x] * GROUPS, axis=0) * lanes


def fold(x, lanes):
    x = x * lanes
    return x[:64] + x[64:128] + x[128:192] + x[192:]


def column_sum(x):
    return jnp.sum(x, axis=0, keepdims=True)


def me_shard():
    return lax.axis_index("shard")


def row_at(i, rows):
    return pl.ds(pl.multiple_of(i * rows, 32), 32)


def gathered(blocks):
    return [
        [
            (half[2 * core + y], 32 * m, 4 * m + 2 * y + core)
            for core in range(2)
            for y in range(2)
            for m in range(4)
        ]
        for half in (blocks[:4], blocks[4:])
    ]


def attn_copies(blocks, w, sem):
    me = me_shard()
    return [
        pltpu.make_async_copy(
            ref.at[row : row + 32, :ATTN],
            w.at[row_at(lax.bitwise_xor(me, whose), 32), :],
            sem.at[n],
        )
        for n, (ref, row, whose) in enumerate(gathered(blocks)[0])
    ]


def ff_copies(blocks, w1, w2, sem):
    first_copies, second_copies = [], []
    me = me_shard()
    left, right = gathered(blocks)
    first = SPLIT - ATTN
    for n, (ref, row, whose) in enumerate(left):
        rows = row_at(lax.bitwise_xor(me, whose), 32)
        first_copies.append(
            pltpu.make_async_copy(
                ref.at[row : row + 32, ATTN:], w1.at[rows, :first], sem.at[n, 0]
            )
        )
    for n, (ref, row, whose) in enumerate(right):
        i = lax.bitwise_xor(me, whose)
        first_copies.append(
            pltpu.make_async_copy(
                ref.at[row : row + 32, : MLP - first],
                w1.at[row_at(i, 32), first:],
                sem.at[n, 1],
            )
        )
        for j in range(4):
            at = MLP - first + 512 * j
            second_copies.append(
                pltpu.make_async_copy(
                    ref.at[row : row + 32, at : at + 512],
                    w2.at[row_at(4 * i + j, 32), :],
                    sem.at[n, 2 + j],
                )
            )
    return first_copies, second_copies


def share_copies(grads, mine, theirs, sem):
    core = lax.rem(me_shard(), 2)
    out = []
    for q in range(8):
        for n, (target, bit) in enumerate(((mine, core), (theirs, 1 - core))):
            at = pl.multiple_of((2 * q + bit) * 32, 32)
            out.append(
                pltpu.make_async_copy(
                    grads.at[pl.ds(at, 32), :],
                    target.at[32 * q : 32 * q + 32, :],
                    sem.at[q, n],
                )
            )
    return out


def pack_kernel(*refs):
    qkv_w, proj, fc1, fc2, gain, shift, qkv_b, out_b, fc1_b, table = refs[:10]
    outs, stack, sem = refs[10:12], refs[12], refs[13]
    copies = []
    for level in range(2):
        out = outs[level]
        pairs = [
            (qkv_w.at[level], out.at[:, : 3 * C]),
            (proj.at[level], out.at[:, 3 * C : ATTN]),
            (fc1.at[level], out.at[:, ATTN : ATTN + MLP]),
        ]
        for j in range(4):
            at = ATTN + MLP + 512 * j
            pairs.append((fc2.at[level, 32 * j : 32 * j + 32, :], out.at[:, at : at + 512]))
        copies += [
            pltpu.make_async_copy(a, b, sem.at[level, n]) for n, (a, b) in enumerate(pairs)
        ]
    for c in copies:
        c.start()
    stack[...] = jnp.zeros((SMALL, SMALL), F32)
    for level in range(2):
        for n, ref in enumerate((gain, shift, qkv_b, out_b)):
            at = 8 * level + 2 * n
            stack[at : at + 2, :32] = ref[level].astype(F32)
        for j in range(4):
            at = 16 + 4 * level + j
            stack[at : at + 1, :32] = fc1_b[level : level + 1, 32 * j : 32 * j + 32].astype(F32)
        for j in range(6):
            at = 24 + 6 * level + j
            width = min(32, 169 - 32 * j)
            stack[at : at + 1, :width] = table[level : level + 1, 32 * j : 32 * j + width].astype(F32)
    outs[0][:, 2 * SPLIT :] = stack[...].T[:32, :].astype(BF)
    for c in copies:
        c.wait()


def join_kernel(*refs):
    blocks, outs = refs[:4], refs[4:]
    for m in range(4):
        for n, out in enumerate(outs):
            cols = slice(SPLIT * n, SPLIT * n + out.shape[1])
            out[32 * m : 32 * m + 32, :] = blocks[m][:, cols]


def params_kernel(small, out, scratch):
    me = me_shard()
    for t in range(16):
        at = 128 * (t // 2 % 2) + 256 * (t % 2) + 32 * (t // 4)
        scratch[row_at(lax.bitwise_xor(me, t), 32), :] = small[at : at + 32, :].astype(F32)
    out[...] = scratch[...].T


def attn_forward_kernel(level, *refs):
    if level == 0:
        img, spread = refs[:2]
        refs = refs[2:]
    else:
        own, halo, spread_halo, mask_rows, mask_cols = refs[:5]
        refs = refs[5:]
    params, bias, lanes_ref, seg_ref = refs[:4]
    blocks, refs = refs[4:-8], refs[-8:]
    x_out, x1_out, h_out, qkv, a_out, o_out, w, sem = refs
    copies = attn_copies(blocks, w, sem)
    for c in copies:
        c.start()
    if level == 0:
        x = dot(spread[...], img[...])
    else:
        x = own[...] + dot(spread_halo[...], halo[...])
    x_out[...] = x
    row = 8 * level
    xhat, _ = norm_parts(x)
    h = (xhat * params[row : row + 1, :] + params[row + 2 : row + 3, :]).astype(BF)
    h_out[...] = h
    for c in copies:
        c.wait()
    qkv[:, :C] = (dot(h, w[:, :C]) + params[row + 4 : row + 5, :]).astype(BF)
    qkv[:, C : 2 * C] = dot(h, w[:, C : 2 * C]).astype(BF)
    qkv[:, 2 * C :] = (dot(h, w[:, 2 * C : 3 * C]) + params[row + 5 : row + 6, :]).astype(BF)
    lanes = lanes_ref[...]
    seg = seg_ref[...]
    if level == 1:
        last = (lax.axis_index("seq") == 7).astype(F32)
        row_mask = mask_rows[...] * last
        both_mask = jnp.minimum(row_mask, mask_cols[...])
    groups = range(GROUPS)
    for window in range(WINDOWS):
        rows = slice(window * SPOT, (window + 1) * SPOT)
        q, k, v = (
            [qkv[rows, C * n + 128 * g : C * n + 128 * g + 128] for g in groups] for n in range(3)
        )
        s = [dot_nt(q[g], four(k[g], lanes)) * SCALE + bias[g] for g in groups]
        if level == 1:
            mask = both_mask if window % 2 else row_mask
            s = [t + mask for t in s]
        top = [segment_max(t) for t in s]
        e = [jnp.exp(s[g] - top[g]) for g in groups]
        total = [segment_sum(t, seg) for t in e]
        a = [e[g] / total[g] for g in groups]
        o = [dot(a[g].astype(BF), four(v[g], lanes)).astype(BF) for g in groups]
        for g in groups:
            a_out[window * GROUPS + g] = a[g]
            o_out[rows, 128 * g : 128 * g + 128] = o[g]
    x1_out[...] = x + (dot(o_out[...], w[:, 3 * C :]) + params[row + 6 : row + 7, :])


def ff_forward_kernel(level, *refs):
    x1_ref, params, fc1_b, send_hot, out_hot = refs[:5]
    refs = refs[5:]
    blocks, refs = refs[:-8], refs[-8:]
    result, send, h2_out, g_out, gp_out, w1, w2, sem = refs
    first_copies, second_copies = ff_copies(blocks, w1, w2, sem)
    for c in first_copies + second_copies:
        c.start()
    row = 8 * level
    x1 = x1_ref[...]
    xhat, _ = norm_parts(x1)
    h2 = (xhat * params[row + 1 : row + 2, :] + params[row + 3 : row + 4, :]).astype(BF)
    h2_out[...] = h2
    for c in first_copies:
        c.wait()
    total = x1 + params[row + 7 : row + 8, :]
    for n in range(4):
        cols = slice(512 * n, 512 * n + 512)
        f = dot(h2, w1[:, cols]) + fc1_b[:, cols]
        phi = 0.5 * (1.0 + lax.erf(f * (0.5**0.5)))
        g = (f * phi).astype(BF)
        g_out[:, cols] = g
        gp_out[:, cols] = (phi + f * (jnp.exp(f * f * -0.5) * 0.3989422804014327)).astype(BF)
    for c in second_copies:
        c.wait()
    total = total + dot(g_out[...], w2[...])
    send[...] = dot(send_hot[...], total.astype(BF)).astype(BF)
    result[...] = place(out_hot[...], total)


def ff_backward_kernel(level, *refs):
    if level == 1:
        cot, halo, spread, spread_halo = refs[:4]
        refs = refs[4:]
    else:
        own, halo, spread_halo = refs[:3]
        refs = refs[3:]
    x1_ref, h2_ref, g_ref, gp_ref, params, pick = refs[:6]
    blocks, refs = refs[6:-10], refs[-10:]
    g1_out, rows_out, col_out, mine, theirs, w1, w2, grads, sem, share_sem = refs
    first_copies, second_copies = ff_copies(blocks, w1, w2, sem)
    for c in second_copies + first_copies:
        c.start()
    if level == 1:
        g2 = dot(spread[...], cot[...]) + dot(spread_halo[...], halo[...])
    else:
        g2 = own[...] + dot(spread_halo[...], halo[...])
    dz = g2.astype(BF)
    row = 8 * level
    xhat, r = norm_parts(x1_ref[...])
    h2 = h2_ref[...]
    ones = jnp.ones((TOK, 128), BF)
    dh2 = jnp.zeros((TOK, C), F32)
    col_out[...] = jnp.zeros((C, SMALL), F32)
    lane = lax.broadcasted_iota(jnp.int32, (32, SMALL), 1)
    for n in range(4):
        cols = slice(512 * n, 512 * n + 512)
        d = dot_tn(g_ref[:, cols], dz).astype(BF)
        for i in range(4):
            for j in range(4):
                at = 128 * i + 32 * j
                to = 32 * (4 * n + i)
                grads[to : to + 32, MLP + 512 * j : MLP + 512 * j + 512] = d[at : at + 32, :]
    for c in second_copies + first_copies:
        c.wait()
    for n in range(4):
        cols = slice(512 * n, 512 * n + 512)
        df = (dot_nt(dz, w2[cols, :]) * gp_ref[:, cols].astype(F32)).astype(BF)
        grads[:, cols] = dot_tn(h2, df).astype(BF)
        sums = dot_tn(df, ones)
        for i in range(4):
            to = 32 * (4 * n + i)
            picked = jnp.zeros((32, SMALL), F32)
            for j in range(4):
                at = 128 * i + 32 * j
                picked = picked + jnp.where(lane == 8 + j, sums[at : at + 32, :], 0.0)
            col_out[to : to + 32, :] = picked
        dh2 = dh2 + dot_nt(df, w1[:, cols])
    shares = share_copies(grads, mine, theirs, share_sem)
    for c in shares:
        c.start()
    g1_out[...] = g2 + norm_back(dh2, xhat, r, params[row + 1 : row + 2, :])
    rows_out[...] = jnp.zeros((8, C), F32)
    rows_out[1:2, :] = column_sum(dh2 * xhat)
    rows_out[3:4, :] = column_sum(dh2)
    rows_out[7:8, :] = column_sum(dz.astype(F32))
    for c in shares:
        c.wait()


def attn_backward_kernel(level, *refs):
    g1_ref, x_ref, h_ref, qkv, a_ref, o_ref, params, rows_ref, col_ref = refs[:9]
    lanes_ref, seg_ref, back_hot = refs[9:12]
    refs = refs[12:]
    if level == 1:
        send_hot = refs[0]
        refs = refs[1:]
    blocks, refs = refs[:8], refs[8:]
    if level == 1:
        send = refs[0]
        refs = refs[1:]
    back, mine, theirs, w, grads, d_qkv, stack, ds_all, sem, share_sem = refs
    copies = attn_copies(blocks, w, sem)
    for c in copies:
        c.start()
    row = 8 * level
    g1 = g1_ref[...]
    dy = g1.astype(BF)
    grads[:, 3 * C : 4 * C] = dot_tn(o_ref[...], dy).astype(BF)
    stack[...] = jnp.zeros((SMALL, C), F32)
    stack[0:8, :] = rows_ref[...]
    stack[6:7, :] = column_sum(dy.astype(F32))
    xhat, r = norm_parts(x_ref[...])
    lanes = lanes_ref[...]
    lanes_f = lanes.astype(F32)
    seg = seg_ref[...]
    for c in copies:
        c.wait()
    do_all = dot_nt(dy, w[:, 3 * C :]).astype(BF)
    lane = lax.broadcasted_iota(jnp.int32, (32, 128), 1)
    groups = range(GROUPS)
    for window in range(WINDOWS):
        rows = slice(window * SPOT, (window + 1) * SPOT)
        q, k, v = (
            [qkv[rows, C * n + 128 * g : C * n + 128 * g + 128] for g in groups] for n in range(3)
        )
        do = [do_all[rows, 128 * g : 128 * g + 128] for g in groups]
        a = [a_ref[window * GROUPS + g] for g in groups]
        da = [dot_nt(do[g], four(v[g], lanes)) for g in groups]
        total = [segment_sum(a[g] * da[g], seg) for g in groups]
        dv = [fold(dot_tn(a[g].astype(BF), do[g]), lanes_f) for g in groups]
        ds = [(a[g] * (da[g] - total[g])).astype(BF) for g in groups]
        dq = [dot(ds[g], four(k[g], lanes)) * SCALE for g in groups]
        dk = [fold(dot_tn(ds[g], q[g]), lanes_f) * SCALE for g in groups]
        for g in groups:
            at = 128 * g
            d_qkv[rows, at : at + 128] = dq[g].astype(BF)
            d_qkv[rows, C + at : C + at + 128] = dk[g].astype(BF)
            d_qkv[rows, 2 * C + at : 2 * C + at + 128] = dv[g].astype(BF)
            if window == 0:
                ds_all[g] = ds[g].astype(F32)
            else:
                ds_all[g] = ds_all[g] + ds[g].astype(F32)
    for g in groups:
        ds_sum = ds_all[g]
        for pair in range(2):
            top = ds_sum[:32, 128 * pair : 128 * pair + 128]
            low = ds_sum[32:, 128 * pair : 128 * pair + 128]
            even = jnp.where(lane < 64, top, pltpu.roll(low, 64, 1))
            odd = jnp.where(lane < 64, pltpu.roll(top, 64, 1), low)
            head = 4 * g + 2 * pair
            grads[32 * head : 32 * head + 32, ATTN_IN:] = even.astype(BF)
            grads[32 * head + 32 : 32 * head + 64, ATTN_IN:] = odd.astype(BF)
    h = h_ref[...]
    for n in range(3):
        cols = slice(C * n, C * n + C)
        grads[:, cols] = dot_tn(h, d_qkv[:, cols]).astype(BF)
    stack[4:5, :] = column_sum(d_qkv[:, :C].astype(F32))
    stack[5:6, :] = column_sum(d_qkv[:, 2 * C :].astype(F32))
    dh = dot_nt(d_qkv[...], w[:, : 3 * C])
    stack[0:1, :] = column_sum(dh * xhat)
    stack[2:3, :] = column_sum(dh)
    grads[:, ATTN:ATTN_IN] = (stack[...].T + col_ref[...]).astype(BF)
    shares = share_copies(grads, mine, theirs, share_sem)
    for c in shares:
        c.start()
    total = g1 + norm_back(dh, xhat, r, params[row : row + 1, :])
    if level == 1:
        send[...] = dot(send_hot[...], total.astype(BF)).astype(BF)
    back[...] = place(back_hot[...], total)
    for c in shares:
        c.wait()


def pair_kernel(*refs):
    shares, outs = refs[:4], refs[4:]
    chip = lax.div(me_shard(), 2)
    for m in range(4):
        to = slice(32 * m, 32 * m + 32)
        for y in range(2):
            rows = row_at(lax.bitwise_xor(chip, 2 * m + y), 32)
            for mine, other, start, width in (
                (shares[0], shares[1], 0, FF),
                (shares[2], shares[3], FF, ATTN_OUT),
            ):
                total = (mine[rows, :].astype(F32) + other[rows, :].astype(F32)).astype(BF)
                if y == 0:
                    outs[0][to, start : start + width] = total
                    continue
                cut = max(0, min(width, SHARE - start))
                if cut:
                    outs[1][to, start : start + cut] = total[:, :cut]
                if cut < width:
                    at = start + cut - SHARE
                    outs[2][to, at : at + width - cut] = total[:, cut:]


def added(refs):
    return functools.reduce(jnp.add, [r[...].astype(F32) for r in refs])


def middle_kernel(own, left, right, *outs):
    for m in range(4):
        rows = slice(32 * m, 32 * m + 32)
        for part, cols in ((left, slice(0, SHARE)), (right, slice(SHARE, 2 * SHARE))):
            total = own[rows, cols].astype(F32) + part[rows, :].astype(F32)
            outs[m][:, cols] = total.astype(BF)


def z_part(ref, k):
    p = lax.bitwise_xor(lax.div(lax.axis_index("seq"), 2), k)
    return ref.at[:, pl.ds(pl.multiple_of(p * QUARTER, 128), QUARTER)]


def split_kernel(*refs):
    pieces, outs = refs[:4], refs[4:8]
    total, sem = refs[8:]
    total[:, : 2 * SHARE] = added(pieces).astype(BF)
    total[:, 2 * SHARE :] = jnp.zeros((32, TOTAL - 2 * SHARE), BF)
    copies = [pltpu.make_async_copy(z_part(total, k), outs[k], sem.at[k]) for k in range(4)]
    for c in copies:
        c.start()
    for c in copies:
        c.wait()


def finish_kernel(*refs):
    pieces, hot = refs[:8], refs[8]
    gain, shift, qkv_w, qkv_b, table, proj, out_b, fc1, fc1_b, fc2 = refs[9:19]
    scratch, sem = refs[19:]
    copies = [
        pltpu.make_async_copy(
            pieces[4 * level + k], z_part(scratch.at[level], k), sem.at[level, k]
        )
        for level in range(2)
        for k in range(4)
    ]
    for c in copies:
        c.start()
    for c in copies:
        c.wait()
    total = scratch[...]
    for level in range(2):
        fc1[level] = total[level, :, :MLP].astype(F32)
        for j in range(4):
            fc2[level, 32 * j : 32 * j + 32, :] = total[
                level, :, MLP + 512 * j : MLP + 512 * j + 512
            ].astype(F32)
        qkv_w[level] = total[level, :, FF : FF + 3 * C].astype(F32)
        proj[level] = total[level, :, FF + 3 * C : FF + 4 * C].astype(F32)
        small = total[level, :, FF + ATTN : FF + ATTN_IN].astype(F32).T
        gain[level] = small[0:2, :]
        shift[level] = small[2:4, :]
        qkv_b[level] = small[4:6, :]
        out_b[level] = small[6:8, :]
        fc1_b[level : level + 1, :] = jnp.concatenate(
            [small[8 + j : 9 + j, :] for j in range(4)], axis=1
        )
        ds = total[level, :, FF + ATTN_IN : FF + ATTN_OUT]
        flat = jnp.concatenate([ds[r : r + 1, :] for r in range(32)], axis=1)
        sums = dot(jnp.broadcast_to(flat.astype(F32), (16, 4096)).astype(BF), hot[...])
        table[level] = sums[0:1, :169]


def sds(shape, dtype):
    return jax.ShapeDtypeStruct(shape, dtype)


def call(kernel, ins, outs, scratch, args, flops=0, room=24):
    return pl.pallas_call(
        kernel,
        out_shape=tuple(s for s, _ in outs),
        in_specs=ins,
        out_specs=tuple(m for _, m in outs),
        scratch_shapes=scratch,
        compiler_params=pltpu.CompilerParams(vmem_limit_bytes=room * 1024 * 1024),
        cost_estimate=pl.CostEstimate(flops=8 * flops, bytes_accessed=8000000, transcendentals=0),
    )(*args)


def shard_permute(x, k):
    return lax.ppermute(x, "shard", [(i, i ^ k) for i in range(16)])


def core_permute(x):
    return shard_permute(x, 1)


def y_permute(x):
    return shard_permute(x, 2)


def y_shift(x, by):
    pairs = []
    for z in range(4):
        for y in range(4):
            to = (y + by) % 4
            for rest in range(8):
                place = rest // 2 * 4 + rest % 2
                pairs.append(
                    (
                        (2 * z + y // 2) * 16 + place + 2 * (y % 2),
                        (2 * z + to // 2) * 16 + place + 2 * (to % 2),
                    )
                )
    return lax.ppermute(x, ("seq", "shard"), pairs)


def x_permutes(pieces):
    return [shard_permute(p, 4 * k) for k, p in enumerate(pieces, 1)]


def seq_permute(x, k):
    return lax.ppermute(x, "seq", [(i, i ^ k) for i in range(8)])


def z_permutes(pieces):
    return [seq_permute(p, 2 * k) for k, p in enumerate(pieces, 1)]


def passed_along(x, by):
    return lax.ppermute(x, "seq", [(i, (i + by) % 8) for i in range(8)])


def gather_x(block):
    return [block] + x_permutes([block] * 3)


def joined(blocks):
    widths = [SPLIT, SPLIT, SMALL][: -(-blocks[0].shape[1] // SPLIT)]
    return call(
        join_kernel, [VM] * 4, [(sds((128, w), BF), VM) for w in widths], [], tuple(blocks)
    )


def gather_y(left, right):
    return [left, y_shift(left, 1)], [right, y_shift(right, -1)]


def with_other_core(blocks):
    return blocks + [core_permute(b) for b in blocks]


def pair_sums(shares):
    return call(
        pair_kernel,
        [VM] * len(shares),
        [(sds((128, 2 * SHARE), BF), VM)] + [(sds((128, SHARE), BF), VM)] * 2,
        [],
        shares,
    )


def scatter_y(pieces):
    own, left, right = pieces
    return own, y_shift(left, 1), y_shift(right, -1)


def middle_sums(arrived):
    return call(middle_kernel, [VM] * 3, [(sds((32, 2 * SHARE), BF), VM)] * 4, [], arrived)


def end_sums(pieces):
    return call(
        split_kernel,
        [VM] * 4,
        [(sds((32, QUARTER), BF), HB)] * 4,
        [pltpu.VMEM((32, TOTAL), BF), pltpu.SemaphoreType.DMA((4,))],
        (pieces[0], *x_permutes(pieces[1:])),
    )


def total_of(parts):
    return functools.reduce(jnp.add, [p.astype(F32) for p in parts]).astype(BF)


def seq_sum(pieces):
    own = total_of([pieces[0]] + z_permutes(pieces[1:]))
    own = total_of([own, seq_permute(own, 1)])
    return [own] + z_permutes([own] * 3)


def on_device(
    images,
    norm_gain,
    norm_shift,
    qkv_weight,
    qkv_bias,
    rel_table,
    proj_weight,
    out_bias,
    fc1_weight,
    fc1_bias,
    fc2_weight,
    cotangent,
):
    def natural(x):
        return jnp.pad(x, ((0, 0), (0, 0), (0, 2), (0, 0))).reshape(-1, C)

    block_one, block_two = call(
        pack_kernel,
        [FAR] * 4 + [VM] * 6,
        [(sds((32, 2 * SPLIT + SMALL), BF), VM), (sds((32, 2 * SPLIT), BF), VM)],
        [pltpu.VMEM((SMALL, SMALL), F32), pltpu.SemaphoreType.DMA((2, 7))],
        (
            qkv_weight,
            proj_weight,
            fc1_weight,
            fc2_weight,
            norm_gain,
            norm_shift,
            qkv_bias,
            out_bias,
            fc1_bias,
            rel_table.reshape(2, 169),
        ),
        room=60,
    )
    cot_halo = passed_along(natural(cotangent[:, :SHIFT]), -1)
    cot_halo, block_two = lax.optimization_barrier((cot_halo, block_two))
    row_one, cot_halo = lax.optimization_barrier((gather_x(block_one), cot_halo))
    left_one, right_one, small = joined(row_one)
    left_one, right_one = gather_y(left_one, right_one)
    for permute in (y_permute, core_permute):
        small = jnp.concatenate([small, permute(small)], axis=0)
    row_two, _, _ = lax.optimization_barrier((gather_x(block_two), left_one, right_one))
    left_two, right_two = gather_y(*joined(row_two))

    img = natural(images)
    cot = natural(cotangent)

    (params,) = call(params_kernel, [VM], [(sds((SMALL, C), F32), VM)], [pltpu.VMEM((C, SMALL), F32)], (small,))
    tables = params[24:36].reshape(2, 6, HEADS, 32).transpose(0, 2, 1, 3).reshape(32, 192)
    bias_all = lax.dot_general(
        tables.astype(BF),
        const(REL_HOT),
        (((1,), (0,)), ((), ())),
        preferred_element_type=F32,
    )
    bias_all = bias_all.reshape(2, GROUPS, 4, SPOT, SPOT).transpose(0, 1, 3, 2, 4)
    bias_all = bias_all.reshape(2, GROUPS, SPOT, 256) + jnp.asarray(EDGE)
    fc1_b = params[16:24].reshape(2, 4, 16, 32).transpose(0, 2, 1, 3).reshape(2, 1, MLP)

    lanes = const(HEAD_LANES)
    seg = const(SEGMENT)
    tokens = sds((TOK, C), F32)
    tokens_low = sds((TOK, C), BF)
    hidden_low = sds((TOK, MLP), BF)
    halo_low = sds((HALO, C), BF)

    def attn_forward(level, lead, blocks):
        outs = [
            (tokens, VM),
            (tokens, VM),
            (tokens_low, VM),
            (sds((TOK, 3 * C), BF), VM),
            (sds((16, SPOT, 256), F32), VM),
            (tokens_low, VM),
        ]
        return call(
            functools.partial(attn_forward_kernel, level),
            [VM] * (len(lead) + 4) + [HB] * len(blocks),
            outs,
            [pltpu.VMEM((C, ATTN), BF), pltpu.SemaphoreType.DMA((16,))],
            tuple(lead) + (params, bias_all[level], lanes, seg) + tuple(blocks),
            flops=2 * TOK * C * ATTN,
        )

    def ff_scratch():
        return [pltpu.VMEM((C, MLP), BF), pltpu.VMEM((MLP, C), BF)]

    def ff_forward(level, x1, blocks):
        lead = (x1, params, fc1_b[level])
        if level == 0:
            lead += (const(FIRST_ROWS), const(ROLL))
            out = tokens
        else:
            lead += (const(LAST_ROWS), const(ROLLED.T))
            out = sds((NAT, C), F32)
        return call(
            functools.partial(ff_forward_kernel, level),
            [VM] * len(lead) + [HB] * len(blocks),
            [(out, VM), (halo_low, VM), (tokens_low, VM), (hidden_low, VM), (hidden_low, VM)],
            ff_scratch() + [pltpu.SemaphoreType.DMA((16, 6))],
            lead + tuple(blocks),
            flops=4 * TOK * C * MLP,
        )

    def ff_backward(level, lead, saved, blocks):
        shares = sds((256, FF), BF)
        return call(
            functools.partial(ff_backward_kernel, level),
            [VM] * (len(lead) + 6) + [HB] * len(blocks),
            [
                (tokens, VM),
                (sds((8, C), F32), VM),
                (sds((C, SMALL), F32), VM),
                (shares, HB),
                (shares, HB),
            ],
            ff_scratch()
            + [
                pltpu.VMEM((C, FF), BF),
                pltpu.SemaphoreType.DMA((16, 6)),
                pltpu.SemaphoreType.DMA((8, 2)),
            ],
            tuple(lead) + tuple(saved) + (params, lanes) + tuple(blocks),
            flops=8 * TOK * C * MLP,
        )

    def attn_backward(level, g1, saved, rows, cols, hots, blocks):
        shares = sds((256, ATTN_OUT), BF)
        outs = [(halo_low, VM)] if level == 1 else []
        outs.append((tokens if level == 1 else sds((NAT, C), F32), VM))
        return call(
            functools.partial(attn_backward_kernel, level),
            [VM] * (11 + len(hots)) + [HB] * len(blocks),
            outs + [(shares, HB), (shares, HB)],
            [
                pltpu.VMEM((C, ATTN), BF),
                pltpu.VMEM((C, ATTN_OUT), BF),
                pltpu.VMEM((TOK, 3 * C), BF),
                pltpu.VMEM((SMALL, C), F32),
                pltpu.VMEM((GROUPS, SPOT, 256), F32),
                pltpu.SemaphoreType.DMA((16,)),
                pltpu.SemaphoreType.DMA((8, 2)),
            ],
            (g1,) + tuple(saved) + (params, rows, cols, lanes, seg) + tuple(hots) + tuple(blocks),
            flops=4 * TOK * C * ATTN,
        )

    left_one, right_one, bias_all, fc1_b, img = lax.optimization_barrier(
        (left_one, right_one, bias_all, fc1_b, img)
    )
    all_one = with_other_core(left_one) + with_other_core(right_one)
    x_one, x1_one, *attn_saved_one = attn_forward(0, (img, const(PLAIN)), all_one)
    mid, send, *ff_saved_one = ff_forward(0, x1_one, all_one)
    halo, left_two[1], right_two[1] = lax.optimization_barrier(
        (passed_along(send, -1), left_two[1], right_two[1])
    )
    all_two = with_other_core(left_two) + with_other_core(right_two)
    lead = (
        mid,
        halo,
        const(ROLLED_HALO),
        jnp.asarray(MASK_ROWS),
        jnp.asarray(MASK_COLS),
    )
    x_two, x1_two, *attn_saved_two = attn_forward(1, lead, all_two)
    own_rows, send, *ff_saved_two = ff_forward(1, x1_two, all_two)
    returned = passed_along(send, 1).astype(F32).reshape(2, SHIFT, 16, C)
    outputs = jnp.concatenate(
        [returned, own_rows.reshape(2, 7, 16, C)[:, SHIFT:]], axis=1
    )[:, :, :14]

    g1, rows, cols, mine, theirs = ff_backward(
        1,
        (cot, cot_halo, const(ROLLED), const(ROLLED_HALO)),
        (x1_two, *ff_saved_two),
        all_two,
    )
    shares_two = (mine, core_permute(theirs))
    g1, outputs = lax.optimization_barrier((g1, outputs))
    send, own, mine, theirs = attn_backward(
        1,
        g1,
        (x_two, *attn_saved_two),
        rows,
        cols,
        (const(ROLL.T), const(LAST_ROWS)),
        all_two,
    )
    pieces_two = pair_sums(shares_two + (mine, core_permute(theirs)))
    own, pieces_two = lax.optimization_barrier((own, pieces_two))
    g1, rows, cols, mine, theirs = ff_backward(
        0,
        (own, passed_along(send, 1), const(PLAIN_HALO)),
        (x1_one, *ff_saved_one),
        all_one,
    )
    ff_shares = (mine, theirs)
    input_grad, mine, theirs = attn_backward(
        0, g1, (x_one, *attn_saved_one), rows, cols, (const(PLAIN.T),), all_one
    )
    arrived, ff_shares, attn_shares = lax.optimization_barrier(
        (scatter_y(pieces_two), ff_shares, (mine, theirs))
    )
    shares_one = [
        part for mine, theirs in (ff_shares, attn_shares) for part in (mine, core_permute(theirs))
    ]
    pieces_two, shares_one = lax.optimization_barrier((middle_sums(arrived), shares_one))
    pieces_one = scatter_y(pair_sums(shares_one))
    pieces_one, pieces_two = lax.optimization_barrier(
        (pieces_one, end_sums(pieces_two))
    )
    pieces_one = end_sums(middle_sums(pieces_one))
    sums_two = seq_sum(pieces_two)
    sums_one = seq_sum(pieces_one)
    shapes = [
        (2, 2, 32),
        (2, 2, 32),
        (2, 32, 3 * C),
        (2, 2, 32),
        (2, 1, 169),
        (2, 32, C),
        (2, 2, 32),
        (2, 32, MLP),
        (2, 128),
        (2, 128, C),
    ]
    grads = call(
        finish_kernel,
        [HB] * 8 + [VM],
        [(sds(shape, F32), VM) for shape in shapes],
        [pltpu.VMEM((2, 32, TOTAL), BF), pltpu.SemaphoreType.DMA((2, 4))],
        tuple(sums_one) + tuple(sums_two) + (const(PACKED_HOT),),
    )
    input_grad = input_grad.reshape(2, 7, 16, C)[:, :, :14]
    return (outputs, input_grad) + tuple(grads)


def solution(mesh):
    return jax.shard_map(
        on_device,
        mesh=mesh,
        in_specs=(
            P("shard", "seq", None, None),
            P(None, None, "shard"),
            P(None, None, "shard"),
            P(None, "shard", None),
            P(None, None, "shard"),
            P(None, "shard", None),
            P(None, "shard", None),
            P(None, None, "shard"),
            P(None, "shard", None),
            P(None, "shard"),
            P(None, "shard", None),
            P("shard", "seq", None, None),
        ),
        out_specs=(
            P("shard", "seq", None, None),
            P("shard", "seq", None, None),
            P(None, None, "shard"),
            P(None, None, "shard"),
            P(None, "shard", None),
            P(None, None, "shard"),
            P(None, "shard", None),
            P(None, "shard", None),
            P(None, None, "shard"),
            P(None, "shard", None),
            P(None, "shard"),
            P(None, "shard", None),
        ),
        check_vma=False,
    )
```

```python
import functools

import jax
import jax.numpy as jnp
import numpy as np
from jax import lax
from jax.experimental import pallas as pl
from jax.experimental.pallas import tpu as pltpu
from jax.sharding import PartitionSpec as P

C = 512
HEADS = 16
HD = 32
MLP = 2048
WIN = 7
SHIFT = 3
SPOT = 64
WINDOWS = 4
TOK = WINDOWS * SPOT
GROUPS = 4
NAT = 2 * 7 * 16
HALO = 2 * 3 * 16
SMALL = 128
ATTN = 2048
SPLIT = 3072
SHARE = 3200
ATTN_IN = ATTN + SMALL
ATTN_OUT = ATTN + 2 * SMALL
FF = 4096
TOTAL = 6656
QUARTER = TOTAL // 4
SCALE = HD ** (-0.5)
EPS = 1e-05
BF = jnp.bfloat16
F32 = jnp.float32
VM = pl.BlockSpec(memory_space=pltpu.VMEM)
HB = pl.BlockSpec(memory_space=pl.ANY)
FAR = pl.BlockSpec(memory_space=pltpu.HBM)


def _places():
    nat = lambda m, r, c: (m * 7 + r) * 16 + c
    halo = lambda m, r, c: (m * 3 + r) * 16 + c
    plain = np.zeros((TOK, NAT), np.float32)
    rolled = np.zeros((TOK, NAT), np.float32)
    rolled_halo = np.zeros((TOK, HALO), np.float32)
    first_rows = np.zeros((HALO, TOK), np.float32)
    last_rows = np.zeros((HALO, TOK), np.float32)
    for m in range(2):
        for w in range(2):
            for y in range(7):
                for x in range(7):
                    t = (m * 2 + w) * SPOT + y * 7 + x
                    col = w * 7 + x
                    plain[t, nat(m, y, col)] = 1
                    if y < SHIFT:
                        first_rows[halo(m, y, col), t] = 1
                    col = (col + SHIFT) % 14
                    if y + SHIFT < 7:
                        rolled[t, nat(m, y + SHIFT, col)] = 1
                    else:
                        rolled_halo[t, halo(m, y + SHIFT - 7, col)] = 1
                        last_rows[halo(m, y + SHIFT - 7, col), t] = 1
    return plain, rolled, rolled_halo, first_rows, last_rows


PLAIN, ROLLED, ROLLED_HALO, FIRST_ROWS, LAST_ROWS = _places()
ROLL = ROLLED @ PLAIN.T
PLAIN_HALO = np.zeros((TOK, HALO), np.float32)
for _r, _t in zip(*np.nonzero(FIRST_ROWS)):
    PLAIN_HALO[_t, _r] = 1


def _pairs():
    rel = np.full((SPOT, SPOT), -1)
    rows = np.zeros((SPOT, GROUPS * SPOT), np.float32)
    cols = np.zeros((SPOT, GROUPS * SPOT), np.float32)
    for a in range(49):
        for b in range(49):
            rel[a, b] = (a // 7 - b // 7 + 6) * 13 + a % 7 - b % 7 + 6
            for h in range(GROUPS):
                if (a // 7 >= 4) != (b // 7 >= 4):
                    rows[a, h * SPOT + b] = -100.0
                if (a % 7 >= 4) != (b % 7 >= 4):
                    cols[a, h * SPOT + b] = -100.0
    return rel, rows, cols


REL, MASK_ROWS, MASK_COLS = _pairs()
REL_HOT = (REL[None] == np.arange(192)[:, None, None]).astype(np.float32)
PACKED_REL = np.concatenate([REL[:32], REL[32:]], axis=1)
PACKED_HOT = (PACKED_REL.reshape(-1, 1) == np.arange(256)[None]).astype(np.float32)
EDGE = np.where(np.tile(np.arange(SPOT), GROUPS) < 49, 0.0, -1e30).astype(np.float32)
HEAD_LANES = np.repeat(np.kron(np.eye(GROUPS), np.ones((1, HD))), SPOT, axis=0).astype(np.float32)
SEGMENT = np.kron(np.eye(2), np.ones((SPOT, SPOT))).astype(np.float32)


def const(x):
    return jnp.asarray(x, BF)


def dot(a, b):
    return lax.dot_general(a, b, (((1,), (0,)), ((), ())), preferred_element_type=F32)


def dot_nt(a, b):
    return lax.dot_general(a, b, (((1,), (1,)), ((), ())), preferred_element_type=F32)


def dot_tn(a, b):
    return lax.dot_general(a, b, (((0,), (0,)), ((), ())), preferred_element_type=F32)


def halves(x):
    high = x.astype(BF)
    return high, (x - high.astype(F32)).astype(BF)


def place(hot, x):
    high = x.astype(BF)
    rest = x - high.astype(F32)
    mid = rest.astype(BF)
    low = (rest - mid.astype(F32)).astype(BF)
    return dot(hot, high) + dot(hot, mid) + dot(hot, low)


def segment_sum(x, seg):
    high, low = halves(x)
    parts = [
        dot(high[:, k : k + 128], seg) + dot(low[:, k : k + 128], seg) for k in (0, 128)
    ]
    return jnp.concatenate(parts, axis=1)


def segment_max(s):
    lane = lax.broadcasted_iota(jnp.int32, (SPOT, 128), 1)
    left = lane < SPOT
    parts = []
    for k in (0, 128):
        part = s[:, k : k + 128]
        one = jnp.max(jnp.where(left, part, -3e38), axis=1, keepdims=True)
        two = jnp.max(jnp.where(left, -3e38, part), axis=1, keepdims=True)
        parts.append(jnp.where(left, one, two))
    return jnp.concatenate(parts, axis=1)


def norm_parts(x):
    center = x - jnp.mean(x, axis=-1, keepdims=True)
    r = lax.rsqrt(jnp.mean(center * center, axis=-1, keepdims=True) + EPS)
    return center * r, r


def norm_back(dh, xhat, r, gain):
    e = dh * gain
    return r * (
        e
        - jnp.mean(e, axis=-1, keepdims=True)
        - xhat * jnp.mean(e * xhat, axis=-1, keepdims=True)
    )


def four(x, lanes):
    return jnp.concatenate([x] * GROUPS, axis=0) * lanes


def fold(x, lanes):
    x = x * lanes
    return x[:64] + x[64:128] + x[128:192] + x[192:]


def column_sum(x):
    return jnp.sum(x, axis=0, keepdims=True)


def me_shard():
    return lax.axis_index("shard")


def row_at(i, rows):
    return pl.ds(pl.multiple_of(i * rows, 32), 32)


def gathered(blocks):
    return [
        [
            (half[2 * core + y], 32 * m, 4 * m + 2 * y + core)
            for core in range(2)
            for y in range(2)
            for m in range(4)
        ]
        for half in (blocks[:4], blocks[4:])
    ]


def attn_copies(blocks, w, sem):
    me = me_shard()
    return [
        pltpu.make_async_copy(
            ref.at[row : row + 32, :ATTN],
            w.at[row_at(lax.bitwise_xor(me, whose), 32), :],
            sem.at[n],
        )
        for n, (ref, row, whose) in enumerate(gathered(blocks)[0])
    ]


def ff_copies(blocks, w, sem):
    out = []
    me = me_shard()
    first = SPLIT - ATTN
    for part, half in enumerate(gathered(blocks)):
        for n, (ref, row, whose) in enumerate(half):
            rows = row_at(lax.bitwise_xor(me, whose), 32)
            source, to = (ref.at[row : row + 32, ATTN:], w.at[rows, :first])
            if part == 1:
                source, to = ref.at[row : row + 32, :], w.at[rows, first:]
            out.append(pltpu.make_async_copy(source, to, sem.at[n, part]))
    return out


def regrouped(values, back):
    lane = lax.broadcasted_iota(jnp.int32, (32, 128), 1)
    out = []
    for group in range(16):
        total = None
        for part in range(4):
            if back:
                source, shift = 4 * part + group // 4, 32 * part - 32 * (group % 4)
            else:
                source, shift = 4 * (group % 4) + part, 32 * part - 32 * (group // 4)
            piece = values[:, 128 * source : 128 * source + 128]
            if shift % 128:
                piece = pltpu.roll(piece, shift % 128, 1)
            total = piece if part == 0 else jnp.where(lane < 32 * part, total, piece)
        out.append(total)
    return out


def share_copies(grads, mine, theirs, sem):
    core = lax.rem(me_shard(), 2)
    out = []
    for q in range(8):
        for n, (target, bit) in enumerate(((mine, core), (theirs, 1 - core))):
            at = pl.multiple_of((2 * q + bit) * 32, 32)
            out.append(
                pltpu.make_async_copy(
                    grads.at[pl.ds(at, 32), :],
                    target.at[32 * q : 32 * q + 32, :],
                    sem.at[q, n],
                )
            )
    return out


def pack_kernel(*refs):
    qkv_w, proj, fc1, fc2, gain, shift, qkv_b, out_b, fc1_b, table = refs[:10]
    outs, stack, wide, sem = refs[10:12], refs[12], refs[13], refs[14]
    copies = []
    for level in range(2):
        out = outs[level]
        pairs = [
            (qkv_w.at[level], out.at[:, : 3 * C]),
            (proj.at[level], out.at[:, 3 * C : ATTN]),
            (fc1.at[level], wide.at[level]),
        ]
        for j in range(4):
            at = ATTN + MLP + 512 * j
            pairs.append((fc2.at[level, 32 * j : 32 * j + 32, :], out.at[:, at : at + 512]))
        copies += [
            pltpu.make_async_copy(a, b, sem.at[level, n]) for n, (a, b) in enumerate(pairs)
        ]
    for c in copies:
        c.start()
    stack[...] = jnp.zeros((SMALL, SMALL), F32)
    for level in range(2):
        for n, ref in enumerate((gain, shift, qkv_b, out_b)):
            at = 8 * level + 2 * n
            stack[at : at + 2, :32] = ref[level].astype(F32)
        for j in range(4):
            at = 16 + 4 * level + j
            stack[at : at + 1, :32] = fc1_b[level : level + 1, 32 * j : 32 * j + 32].astype(F32)
        for j in range(6):
            at = 24 + 6 * level + j
            width = min(32, 169 - 32 * j)
            stack[at : at + 1, :width] = table[level : level + 1, 32 * j : 32 * j + width].astype(F32)
    outs[0][:, 2 * SPLIT :] = stack[...].T[:32, :].astype(BF)
    for c in copies:
        c.wait()
    for level in range(2):
        for n, group in enumerate(regrouped(wide[level].astype(F32), False)):
            at = ATTN + 128 * n
            outs[level][:, at : at + 128] = group.astype(BF)


def join_kernel(*refs):
    blocks, outs = refs[:4], refs[4:]
    for m in range(4):
        for n, out in enumerate(outs):
            cols = slice(SPLIT * n, SPLIT * n + out.shape[1])
            out[32 * m : 32 * m + 32, :] = blocks[m][:, cols]


def params_kernel(small, out, scratch):
    me = me_shard()
    for t in range(16):
        at = 128 * (t // 2 % 2) + 256 * (t % 2) + 32 * (t // 4)
        scratch[row_at(lax.bitwise_xor(me, t), 32), :] = small[at : at + 32, :].astype(F32)
    out[...] = scratch[...].T


def attn_forward_kernel(level, *refs):
    if level == 0:
        img, spread = refs[:2]
        refs = refs[2:]
    else:
        own, halo, spread_halo, mask_rows, mask_cols = refs[:5]
        refs = refs[5:]
    params, bias, lanes_ref, seg_ref = refs[:4]
    blocks, refs = refs[4:-8], refs[-8:]
    x_out, x1_out, h_out, qkv, a_out, o_out, w, sem = refs
    copies = attn_copies(blocks, w, sem)
    for c in copies:
        c.start()
    if level == 0:
        x = dot(spread[...], img[...])
    else:
        x = own[...] + dot(spread_halo[...], halo[...])
    x_out[...] = x
    row = 8 * level
    xhat, _ = norm_parts(x)
    h = (xhat * params[row : row + 1, :] + params[row + 2 : row + 3, :]).astype(BF)
    h_out[...] = h
    for c in copies:
        c.wait()
    qkv[:, :C] = (dot(h, w[:, :C]) + params[row + 4 : row + 5, :]).astype(BF)
    qkv[:, C : 2 * C] = dot(h, w[:, C : 2 * C]).astype(BF)
    qkv[:, 2 * C :] = (dot(h, w[:, 2 * C : 3 * C]) + params[row + 5 : row + 6, :]).astype(BF)
    lanes = lanes_ref[...]
    seg = seg_ref[...]
    if level == 1:
        last = (lax.axis_index("seq") == 7).astype(F32)
        row_mask = mask_rows[...] * last
        both_mask = jnp.minimum(row_mask, mask_cols[...])
    groups = range(GROUPS)
    for window in range(WINDOWS):
        rows = slice(window * SPOT, (window + 1) * SPOT)
        q, k, v = (
            [qkv[rows, C * n + 128 * g : C * n + 128 * g + 128] for g in groups] for n in range(3)
        )
        s = [dot_nt(q[g], four(k[g], lanes)) * SCALE + bias[g] for g in groups]
        if level == 1:
            mask = both_mask if window % 2 else row_mask
            s = [t + mask for t in s]
        top = [segment_max(t) for t in s]
        e = [jnp.exp(s[g] - top[g]) for g in groups]
        total = [segment_sum(t, seg) for t in e]
        a = [e[g] / total[g] for g in groups]
        o = [dot(a[g].astype(BF), four(v[g], lanes)).astype(BF) for g in groups]
        for g in groups:
            a_out[window * GROUPS + g] = a[g]
            o_out[rows, 128 * g : 128 * g + 128] = o[g]
    x1_out[...] = x + (dot(o_out[...], w[:, 3 * C :]) + params[row + 6 : row + 7, :])


def ff_forward_kernel(level, *refs):
    x1_ref, params, fc1_b, send_hot, out_hot = refs[:5]
    refs = refs[5:]
    blocks, refs = refs[:-7], refs[-7:]
    result, send, h2_out, g_out, gp_out, w, sem = refs
    copies = ff_copies(blocks, w, sem)
    for c in copies:
        c.start()
    row = 8 * level
    x1 = x1_ref[...]
    xhat, _ = norm_parts(x1)
    h2 = (xhat * params[row + 1 : row + 2, :] + params[row + 3 : row + 4, :]).astype(BF)
    h2_out[...] = h2
    for c in copies:
        c.wait()
    total = x1 + params[row + 7 : row + 8, :]
    for n in range(4):
        cols = slice(512 * n, 512 * n + 512)
        f = dot(h2, w[:, cols]) + fc1_b[:, cols]
        phi = 0.5 * (1.0 + lax.erf(f * (0.5**0.5)))
        g = (f * phi).astype(BF)
        g_out[:, cols] = g
        gp_out[:, cols] = (phi + f * (jnp.exp(f * f * -0.5) * 0.3989422804014327)).astype(BF)
        total = total + dot(g, w[:, MLP + 512 * n : MLP + 512 * n + 512])
    send[...] = dot(send_hot[...], total.astype(BF)).astype(BF)
    result[...] = place(out_hot[...], total)


def ff_backward_kernel(level, *refs):
    if level == 1:
        cot, halo, spread, spread_halo = refs[:4]
        refs = refs[4:]
    else:
        own, halo, spread_halo = refs[:3]
        refs = refs[3:]
    x1_ref, h2_ref, g_ref, gp_ref, params, pick = refs[:6]
    blocks, refs = refs[6:-9], refs[-9:]
    g1_out, rows_out, col_out, mine, theirs, w, grads, sem, share_sem = refs
    copies = ff_copies(blocks, w, sem)
    for c in copies:
        c.start()
    if level == 1:
        g2 = dot(spread[...], cot[...]) + dot(spread_halo[...], halo[...])
    else:
        g2 = own[...] + dot(spread_halo[...], halo[...])
    dz = g2.astype(BF)
    row = 8 * level
    xhat, r = norm_parts(x1_ref[...])
    h2 = h2_ref[...]
    ones = jnp.ones((TOK, 128), BF)
    for n in range(4):
        cols = slice(512 * n, 512 * n + 512)
        grads[:, MLP + 512 * n : MLP + 512 * n + 512] = dot_tn(g_ref[:, cols], dz).astype(BF)
    for c in copies:
        c.wait()
    dh2 = jnp.zeros((TOK, C), F32)
    bias = jnp.zeros((C, SMALL), F32)
    lane = lax.broadcasted_iota(jnp.int32, (C, SMALL), 1)
    for n in range(4):
        cols = slice(512 * n, 512 * n + 512)
        back = dot_nt(dz, w[:, MLP + 512 * n : MLP + 512 * n + 512])
        df = (back * gp_ref[:, cols].astype(F32)).astype(BF)
        grads[:, cols] = dot_tn(h2, df).astype(BF)
        bias = jnp.where(lane == 8 + n, dot_tn(df, ones), bias)
        dh2 = dh2 + dot_nt(df, w[:, cols])
    col_out[...] = bias
    shares = share_copies(grads, mine, theirs, share_sem)
    for c in shares:
        c.start()
    g1_out[...] = g2 + norm_back(dh2, xhat, r, params[row + 1 : row + 2, :])
    rows_out[...] = jnp.zeros((8, C), F32)
    rows_out[1:2, :] = column_sum(dh2 * xhat)
    rows_out[3:4, :] = column_sum(dh2)
    rows_out[7:8, :] = column_sum(dz.astype(F32))
    for c in shares:
        c.wait()


def attn_backward_kernel(level, *refs):
    g1_ref, x_ref, h_ref, qkv, a_ref, o_ref, params, rows_ref, col_ref = refs[:9]
    lanes_ref, seg_ref, back_hot = refs[9:12]
    refs = refs[12:]
    if level == 1:
        send_hot = refs[0]
        refs = refs[1:]
    blocks, refs = refs[:8], refs[8:]
    if level == 1:
        send = refs[0]
        refs = refs[1:]
    back, mine, theirs, w, grads, d_qkv, stack, ds_all, sem, share_sem = refs
    copies = attn_copies(blocks, w, sem)
    for c in copies:
        c.start()
    row = 8 * level
    g1 = g1_ref[...]
    dy = g1.astype(BF)
    grads[:, 3 * C : 4 * C] = dot_tn(o_ref[...], dy).astype(BF)
    stack[...] = jnp.zeros((SMALL, C), F32)
    stack[0:8, :] = rows_ref[...]
    stack[6:7, :] = column_sum(dy.astype(F32))
    xhat, r = norm_parts(x_ref[...])
    lanes = lanes_ref[...]
    lanes_f = lanes.astype(F32)
    seg = seg_ref[...]
    for c in copies:
        c.wait()
    do_all = dot_nt(dy, w[:, 3 * C :]).astype(BF)
    lane = lax.broadcasted_iota(jnp.int32, (32, 128), 1)
    groups = range(GROUPS)
    for window in range(WINDOWS):
        rows = slice(window * SPOT, (window + 1) * SPOT)
        q, k, v = (
            [qkv[rows, C * n + 128 * g : C * n + 128 * g + 128] for g in groups] for n in range(3)
        )
        do = [do_all[rows, 128 * g : 128 * g + 128] for g in groups]
        a = [a_ref[window * GROUPS + g] for g in groups]
        da = [dot_nt(do[g], four(v[g], lanes)) for g in groups]
        total = [segment_sum(a[g] * da[g], seg) for g in groups]
        dv = [fold(dot_tn(a[g].astype(BF), do[g]), lanes_f) for g in groups]
        ds = [(a[g] * (da[g] - total[g])).astype(BF) for g in groups]
        dq = [dot(ds[g], four(k[g], lanes)) * SCALE for g in groups]
        dk = [fold(dot_tn(ds[g], q[g]), lanes_f) * SCALE for g in groups]
        for g in groups:
            at = 128 * g
            d_qkv[rows, at : at + 128] = dq[g].astype(BF)
            d_qkv[rows, C + at : C + at + 128] = dk[g].astype(BF)
            d_qkv[rows, 2 * C + at : 2 * C + at + 128] = dv[g].astype(BF)
            if window == 0:
                ds_all[g] = ds[g].astype(F32)
            else:
                ds_all[g] = ds_all[g] + ds[g].astype(F32)
    for g in groups:
        ds_sum = ds_all[g]
        for pair in range(2):
            top = ds_sum[:32, 128 * pair : 128 * pair + 128]
            low = ds_sum[32:, 128 * pair : 128 * pair + 128]
            even = jnp.where(lane < 64, top, pltpu.roll(low, 64, 1))
            odd = jnp.where(lane < 64, pltpu.roll(top, 64, 1), low)
            head = 4 * g + 2 * pair
            grads[32 * head : 32 * head + 32, ATTN_IN:] = even.astype(BF)
            grads[32 * head + 32 : 32 * head + 64, ATTN_IN:] = odd.astype(BF)
    h = h_ref[...]
    for n in range(3):
        cols = slice(C * n, C * n + C)
        grads[:, cols] = dot_tn(h, d_qkv[:, cols]).astype(BF)
    stack[4:5, :] = column_sum(d_qkv[:, :C].astype(F32))
    stack[5:6, :] = column_sum(d_qkv[:, 2 * C :].astype(F32))
    dh = dot_nt(d_qkv[...], w[:, : 3 * C])
    stack[0:1, :] = column_sum(dh * xhat)
    stack[2:3, :] = column_sum(dh)
    grads[:, ATTN:ATTN_IN] = (stack[...].T + col_ref[...]).astype(BF)
    shares = share_copies(grads, mine, theirs, share_sem)
    for c in shares:
        c.start()
    total = g1 + norm_back(dh, xhat, r, params[row : row + 1, :])
    if level == 1:
        send[...] = dot(send_hot[...], total.astype(BF)).astype(BF)
    back[...] = place(back_hot[...], total)
    for c in shares:
        c.wait()


def pair_kernel(x_first, *refs):
    shares, outs = refs[:4], refs[4:]
    chip = lax.div(me_shard(), 2)
    for m in range(4):
        to = slice(32 * m, 32 * m + 32)
        for y in range(2):
            rows = row_at(lax.bitwise_xor(chip, 2 * m + y), 32)
            for mine, other, start, width in (
                (shares[0], shares[1], 0, FF),
                (shares[2], shares[3], FF, ATTN_OUT),
            ):
                total = (mine[rows, :].astype(F32) + other[rows, :].astype(F32)).astype(BF)
                if x_first:
                    outs[m][32 * y : 32 * y + 32, start : start + width] = total
                    continue
                if y == 0:
                    outs[0][to, start : start + width] = total
                    continue
                cut = max(0, min(width, SHARE - start))
                if cut:
                    outs[1][to, start : start + cut] = total[:, :cut]
                if cut < width:
                    at = start + cut - SHARE
                    outs[2][to, at : at + width - cut] = total[:, cut:]


def added(refs):
    return functools.reduce(jnp.add, [r[...].astype(F32) for r in refs])


def middle_x_kernel(*refs):
    pieces, (own, left, right) = refs[:4], refs[4:]
    total = added(pieces).astype(BF)
    own[...] = total[:32, :]
    left[...] = total[32:, :SHARE]
    right[...] = total[32:, SHARE:]


def middle_kernel(own, left, right, *outs):
    for m in range(4):
        rows = slice(32 * m, 32 * m + 32)
        for part, cols in ((left, slice(0, SHARE)), (right, slice(SHARE, 2 * SHARE))):
            total = own[rows, cols].astype(F32) + part[rows, :].astype(F32)
            outs[m][:, cols] = total.astype(BF)


def z_part(ref, k):
    p = lax.bitwise_xor(lax.div(lax.axis_index("seq"), 2), k)
    return ref.at[:, pl.ds(pl.multiple_of(p * QUARTER, 128), QUARTER)]


def split_kernel(*refs):
    pieces, outs, total, sem = refs[:-6], refs[-6:-2], refs[-2], refs[-1]
    if len(pieces) == 4:
        total[:, : 2 * SHARE] = added(pieces).astype(BF)
    else:
        own, left, right = pieces
        total[:, :SHARE] = (own[:, :SHARE].astype(F32) + left[...].astype(F32)).astype(BF)
        total[:, SHARE : 2 * SHARE] = (own[:, SHARE:].astype(F32) + right[...].astype(F32)).astype(BF)
    total[:, 2 * SHARE :] = jnp.zeros((32, TOTAL - 2 * SHARE), BF)
    copies = [pltpu.make_async_copy(z_part(total, k), outs[k], sem.at[k]) for k in range(4)]
    for c in copies:
        c.start()
    for c in copies:
        c.wait()


def finish_kernel(*refs):
    pieces, hot = refs[:8], refs[8]
    gain, shift, qkv_w, qkv_b, table, proj, out_b, fc1, fc1_b, fc2 = refs[9:19]
    scratch, sem = refs[19:]
    copies = [
        pltpu.make_async_copy(
            pieces[4 * level + k], z_part(scratch.at[level], k), sem.at[level, k]
        )
        for level in range(2)
        for k in range(4)
    ]
    for c in copies:
        c.start()
    for c in copies:
        c.wait()
    total = scratch[...]
    for level in range(2):
        for n, group in enumerate(regrouped(total[level, :, :MLP].astype(F32), True)):
            fc1[level, :, 128 * n : 128 * n + 128] = group
        for j in range(4):
            fc2[level, 32 * j : 32 * j + 32, :] = total[
                level, :, MLP + 512 * j : MLP + 512 * j + 512
            ].astype(F32)
        qkv_w[level] = total[level, :, FF : FF + 3 * C].astype(F32)
        proj[level] = total[level, :, FF + 3 * C : FF + 4 * C].astype(F32)
        small = total[level, :, FF + ATTN : FF + ATTN_IN].astype(F32).T
        gain[level] = small[0:2, :]
        shift[level] = small[2:4, :]
        qkv_b[level] = small[4:6, :]
        out_b[level] = small[6:8, :]
        fc1_b[level : level + 1, :] = jnp.concatenate(
            [small[8 + j : 9 + j, :] for j in range(4)], axis=1
        )
        ds = total[level, :, FF + ATTN_IN : FF + ATTN_OUT]
        flat = jnp.concatenate([ds[r : r + 1, :] for r in range(32)], axis=1)
        sums = dot(jnp.broadcast_to(flat.astype(F32), (16, 4096)).astype(BF), hot[...])
        table[level] = sums[0:1, :169]


def sds(shape, dtype):
    return jax.ShapeDtypeStruct(shape, dtype)


def call(kernel, ins, outs, scratch, args, flops=0, room=24):
    return pl.pallas_call(
        kernel,
        out_shape=tuple(s for s, _ in outs),
        in_specs=ins,
        out_specs=tuple(m for _, m in outs),
        scratch_shapes=scratch,
        compiler_params=pltpu.CompilerParams(vmem_limit_bytes=room * 1024 * 1024),
        cost_estimate=pl.CostEstimate(flops=8 * flops, bytes_accessed=8000000, transcendentals=0),
    )(*args)


def shard_permute(x, k):
    return lax.ppermute(x, "shard", [(i, i ^ k) for i in range(16)])


def core_permute(x):
    return shard_permute(x, 1)


def y_permute(x):
    return shard_permute(x, 2)


def y_shift(x, by):
    pairs = []
    for z in range(4):
        for y in range(4):
            to = (y + by) % 4
            for rest in range(8):
                place = rest // 2 * 4 + rest % 2
                pairs.append(
                    (
                        (2 * z + y // 2) * 16 + place + 2 * (y % 2),
                        (2 * z + to // 2) * 16 + place + 2 * (to % 2),
                    )
                )
    return lax.ppermute(x, ("seq", "shard"), pairs)


def x_permutes(pieces):
    return [shard_permute(p, 4 * k) for k, p in enumerate(pieces, 1)]


def seq_permute(x, k):
    return lax.ppermute(x, "seq", [(i, i ^ k) for i in range(8)])


def z_permutes(pieces):
    return [seq_permute(p, 2 * k) for k, p in enumerate(pieces, 1)]


def passed_along(x, by):
    return lax.ppermute(x, "seq", [(i, (i + by) % 8) for i in range(8)])


def gather_x(block):
    return [block] + x_permutes([block] * 3)


def joined(blocks):
    widths = [SPLIT, SPLIT, SMALL][: -(-blocks[0].shape[1] // SPLIT)]
    return call(
        join_kernel, [VM] * 4, [(sds((128, w), BF), VM) for w in widths], [], tuple(blocks)
    )


def gather_y(left, right):
    return [left, y_shift(left, 1)], [right, y_shift(right, -1)]


def with_other_core(blocks):
    return blocks + [core_permute(b) for b in blocks]


def pair_sums(shares, x_first):
    outs = [(sds((128, 2 * SHARE), BF), VM)] + [(sds((128, SHARE), BF), VM)] * 2
    if x_first:
        outs = [(sds((64, 2 * SHARE), BF), VM)] * 4
    return call(functools.partial(pair_kernel, x_first), [VM] * 4, outs, [], shares)


def scatter_x(pieces):
    return [pieces[0]] + x_permutes(pieces[1:])


def middle_x_sums(arrived):
    outs = [(sds((32, 2 * SHARE), BF), VM)] + [(sds((32, SHARE), BF), VM)] * 2
    return call(middle_x_kernel, [VM] * 4, outs, [], arrived)


def scatter_y(pieces):
    own, left, right = pieces
    return own, y_shift(left, 1), y_shift(right, -1)


def middle_sums(arrived):
    return call(middle_kernel, [VM] * 3, [(sds((32, 2 * SHARE), BF), VM)] * 4, [], arrived)


def end_sums(arrived):
    return call(
        split_kernel,
        [VM] * len(arrived),
        [(sds((32, QUARTER), BF), HB)] * 4,
        [pltpu.VMEM((32, TOTAL), BF), pltpu.SemaphoreType.DMA((4,))],
        arrived,
    )


def total_of(parts):
    return functools.reduce(jnp.add, [p.astype(F32) for p in parts]).astype(BF)


def seq_sum(pieces):
    own = total_of([pieces[0]] + z_permutes(pieces[1:]))
    own = total_of([own, seq_permute(own, 1)])
    return [own] + z_permutes([own] * 3)


def on_device(
    images,
    norm_gain,
    norm_shift,
    qkv_weight,
    qkv_bias,
    rel_table,
    proj_weight,
    out_bias,
    fc1_weight,
    fc1_bias,
    fc2_weight,
    cotangent,
):
    def natural(x):
        return jnp.pad(x, ((0, 0), (0, 0), (0, 2), (0, 0))).reshape(-1, C)

    block_one, block_two = call(
        pack_kernel,
        [FAR] * 4 + [VM] * 6,
        [(sds((32, 2 * SPLIT + SMALL), BF), VM), (sds((32, 2 * SPLIT), BF), VM)],
        [
            pltpu.VMEM((SMALL, SMALL), F32),
            pltpu.VMEM((2, 32, MLP), BF),
            pltpu.SemaphoreType.DMA((2, 7)),
        ],
        (
            qkv_weight,
            proj_weight,
            fc1_weight,
            fc2_weight,
            norm_gain,
            norm_shift,
            qkv_bias,
            out_bias,
            fc1_bias,
            rel_table.reshape(2, 169),
        ),
        room=60,
    )
    cot_halo = passed_along(natural(cotangent[:, :SHIFT]), -1)
    cot_halo, block_two = lax.optimization_barrier((cot_halo, block_two))
    row_one, cot_halo = lax.optimization_barrier((gather_x(block_one), cot_halo))
    left_one, right_one, small = joined(row_one)
    left_one, right_one = gather_y(left_one, right_one)
    for permute in (y_permute, core_permute):
        small = jnp.concatenate([small, permute(small)], axis=0)
    row_two, _, _ = lax.optimization_barrier((gather_x(block_two), left_one, right_one))
    left_two, right_two = gather_y(*joined(row_two))

    img = natural(images)
    cot = natural(cotangent)

    (params,) = call(params_kernel, [VM], [(sds((SMALL, C), F32), VM)], [pltpu.VMEM((C, SMALL), F32)], (small,))
    tables = params[24:36].reshape(2, 6, HEADS, 32).transpose(0, 2, 1, 3).reshape(32, 192)
    bias_all = lax.dot_general(
        tables.astype(BF),
        const(REL_HOT),
        (((1,), (0,)), ((), ())),
        preferred_element_type=F32,
    )
    bias_all = bias_all.reshape(2, GROUPS, 4, SPOT, SPOT).transpose(0, 1, 3, 2, 4)
    bias_all = bias_all.reshape(2, GROUPS, SPOT, 256) + jnp.asarray(EDGE)
    fc1_b = params[16:24].reshape(2, 1, MLP)

    lanes = const(HEAD_LANES)
    seg = const(SEGMENT)
    tokens = sds((TOK, C), F32)
    tokens_low = sds((TOK, C), BF)
    hidden_low = sds((TOK, MLP), BF)
    halo_low = sds((HALO, C), BF)

    def attn_forward(level, lead, blocks):
        outs = [
            (tokens, VM),
            (tokens, VM),
            (tokens_low, VM),
            (sds((TOK, 3 * C), BF), VM),
            (sds((16, SPOT, 256), F32), VM),
            (tokens_low, VM),
        ]
        return call(
            functools.partial(attn_forward_kernel, level),
            [VM] * (len(lead) + 4) + [HB] * len(blocks),
            outs,
            [pltpu.VMEM((C, ATTN), BF), pltpu.SemaphoreType.DMA((16,))],
            tuple(lead) + (params, bias_all[level], lanes, seg) + tuple(blocks),
            flops=2 * TOK * C * ATTN,
        )

    def ff_scratch():
        return [pltpu.VMEM((C, FF), BF)]

    def ff_forward(level, x1, blocks):
        lead = (x1, params, fc1_b[level])
        if level == 0:
            lead += (const(FIRST_ROWS), const(ROLL))
            out = tokens
        else:
            lead += (const(LAST_ROWS), const(ROLLED.T))
            out = sds((NAT, C), F32)
        return call(
            functools.partial(ff_forward_kernel, level),
            [VM] * len(lead) + [HB] * len(blocks),
            [(out, VM), (halo_low, VM), (tokens_low, VM), (hidden_low, VM), (hidden_low, VM)],
            ff_scratch() + [pltpu.SemaphoreType.DMA((16, 2))],
            lead + tuple(blocks),
            flops=4 * TOK * C * MLP,
        )

    def ff_backward(level, lead, saved, blocks):
        shares = sds((256, FF), BF)
        return call(
            functools.partial(ff_backward_kernel, level),
            [VM] * (len(lead) + 6) + [HB] * len(blocks),
            [
                (tokens, VM),
                (sds((8, C), F32), VM),
                (sds((C, SMALL), F32), VM),
                (shares, HB),
                (shares, HB),
            ],
            ff_scratch()
            + [
                pltpu.VMEM((C, FF), BF),
                pltpu.SemaphoreType.DMA((16, 2)),
                pltpu.SemaphoreType.DMA((8, 2)),
            ],
            tuple(lead) + tuple(saved) + (params, lanes) + tuple(blocks),
            flops=8 * TOK * C * MLP,
        )

    def attn_backward(level, g1, saved, rows, cols, hots, blocks):
        shares = sds((256, ATTN_OUT), BF)
        outs = [(halo_low, VM)] if level == 1 else []
        outs.append((tokens if level == 1 else sds((NAT, C), F32), VM))
        return call(
            functools.partial(attn_backward_kernel, level),
            [VM] * (11 + len(hots)) + [HB] * len(blocks),
            outs + [(shares, HB), (shares, HB)],
            [
                pltpu.VMEM((C, ATTN), BF),
                pltpu.VMEM((C, ATTN_OUT), BF),
                pltpu.VMEM((TOK, 3 * C), BF),
                pltpu.VMEM((SMALL, C), F32),
                pltpu.VMEM((GROUPS, SPOT, 256), F32),
                pltpu.SemaphoreType.DMA((16,)),
                pltpu.SemaphoreType.DMA((8, 2)),
            ],
            (g1,) + tuple(saved) + (params, rows, cols, lanes, seg) + tuple(hots) + tuple(blocks),
            flops=4 * TOK * C * ATTN,
        )

    left_one, right_one, bias_all, fc1_b, img = lax.optimization_barrier(
        (left_one, right_one, bias_all, fc1_b, img)
    )
    all_one = with_other_core(left_one) + with_other_core(right_one)
    x_one, x1_one, *attn_saved_one = attn_forward(0, (img, const(PLAIN)), all_one)
    mid, send, *ff_saved_one = ff_forward(0, x1_one, all_one)
    halo, left_two[1], right_two[1] = lax.optimization_barrier(
        (passed_along(send, -1), left_two[1], right_two[1])
    )
    all_two = with_other_core(left_two) + with_other_core(right_two)
    lead = (
        mid,
        halo,
        const(ROLLED_HALO),
        jnp.asarray(MASK_ROWS),
        jnp.asarray(MASK_COLS),
    )
    x_two, x1_two, *attn_saved_two = attn_forward(1, lead, all_two)
    own_rows, send, *ff_saved_two = ff_forward(1, x1_two, all_two)
    returned = passed_along(send, 1)

    g1, rows, cols, mine, theirs = ff_backward(
        1,
        (cot, cot_halo, const(ROLLED), const(ROLLED_HALO)),
        (x1_two, *ff_saved_two),
        all_two,
    )
    g1, mine, theirs, returned = lax.optimization_barrier((g1, mine, theirs, returned))
    shares_two = (mine, core_permute(theirs))
    outputs = jnp.concatenate(
        [
            returned.astype(F32).reshape(2, SHIFT, 16, C),
            own_rows.reshape(2, 7, 16, C)[:, SHIFT:],
        ],
        axis=1,
    )[:, :, :14]
    send, own, mine, theirs = attn_backward(
        1,
        g1,
        (x_two, *attn_saved_two),
        rows,
        cols,
        (const(ROLL.T), const(LAST_ROWS)),
        all_two,
    )
    pieces_two = pair_sums(shares_two + (mine, core_permute(theirs)), True)
    own, pieces_two = lax.optimization_barrier((own, pieces_two))
    g1, rows, cols, mine, theirs = ff_backward(
        0,
        (own, passed_along(send, 1), const(PLAIN_HALO)),
        (x1_one, *ff_saved_one),
        all_one,
    )
    ff_shares = (mine, theirs)
    input_grad, mine, theirs = attn_backward(
        0, g1, (x_one, *attn_saved_one), rows, cols, (const(PLAIN.T),), all_one
    )
    near = [shard_permute(pieces_two[k], 4 * k) for k in (1, 3)]
    near, far, ff_shares, attn_shares = lax.optimization_barrier(
        (near, pieces_two[2], ff_shares, (mine, theirs))
    )
    arrived = [pieces_two[0], near[0], shard_permute(far, 8), near[1]]
    shares_one = [
        part for mine, theirs in (ff_shares, attn_shares) for part in (mine, core_permute(theirs))
    ]
    pieces_one = scatter_y(pair_sums(shares_one, False))
    pieces_two = middle_x_sums(arrived)
    input_grad = input_grad.reshape(2, 7, 16, C)[:, :, :14]
    pieces_one, pieces_two, outputs, input_grad = lax.optimization_barrier(
        (pieces_one, pieces_two, outputs, input_grad)
    )
    pieces_two = end_sums(scatter_y(pieces_two))
    pieces_one = end_sums(scatter_x(middle_sums(pieces_one)))
    sums_two = seq_sum(pieces_two)
    sums_one = seq_sum(pieces_one)
    shapes = [
        (2, 2, 32),
        (2, 2, 32),
        (2, 32, 3 * C),
        (2, 2, 32),
        (2, 1, 169),
        (2, 32, C),
        (2, 2, 32),
        (2, 32, MLP),
        (2, 128),
        (2, 128, C),
    ]
    grads = call(
        finish_kernel,
        [HB] * 8 + [VM],
        [(sds(shape, F32), VM) for shape in shapes],
        [pltpu.VMEM((2, 32, TOTAL), BF), pltpu.SemaphoreType.DMA((2, 4))],
        tuple(sums_one) + tuple(sums_two) + (const(PACKED_HOT),),
    )
    return (outputs, input_grad) + tuple(grads)


def solution(mesh):
    return jax.shard_map(
        on_device,
        mesh=mesh,
        in_specs=(
            P("shard", "seq", None, None),
            P(None, None, "shard"),
            P(None, None, "shard"),
            P(None, "shard", None),
            P(None, None, "shard"),
            P(None, "shard", None),
            P(None, "shard", None),
            P(None, None, "shard"),
            P(None, "shard", None),
            P(None, "shard"),
            P(None, "shard", None),
            P("shard", "seq", None, None),
        ),
        out_specs=(
            P("shard", "seq", None, None),
            P("shard", "seq", None, None),
            P(None, None, "shard"),
            P(None, None, "shard"),
            P(None, "shard", None),
            P(None, None, "shard"),
            P(None, "shard", None),
            P(None, "shard", None),
            P(None, None, "shard"),
            P(None, "shard", None),
            P(None, "shard"),
            P(None, "shard", None),
        ),
        check_vma=False,
    )
```

```python
import functools

import jax
import jax.numpy as jnp
import numpy as np
from jax import lax
from jax.experimental import pallas as pl
from jax.experimental.pallas import tpu as pltpu
from jax.sharding import PartitionSpec as P

C = 512
HEADS = 16
HD = 32
MLP = 2048
WIN = 7
SHIFT = 3
SPOT = 64
WINDOWS = 4
TOK = WINDOWS * SPOT
GROUPS = 4
NAT = 2 * 7 * 16
HALO = 2 * 3 * 16
SMALL = 128
ATTN = 2048
SPLIT = 3072
SHARE = 3200
ATTN_IN = ATTN + SMALL
ATTN_OUT = ATTN + 2 * SMALL
FF = 4096
TOTAL = 6656
QUARTER = TOTAL // 4
SCALE = HD ** (-0.5)
EPS = 1e-05
BF = jnp.bfloat16
F32 = jnp.float32
VM = pl.BlockSpec(memory_space=pltpu.VMEM)
HB = pl.BlockSpec(memory_space=pl.ANY)
FAR = pl.BlockSpec(memory_space=pltpu.HBM)


def _places():
    nat = lambda m, r, c: (m * 7 + r) * 16 + c
    halo = lambda m, r, c: (m * 3 + r) * 16 + c
    plain = np.zeros((TOK, NAT), np.float32)
    rolled = np.zeros((TOK, NAT), np.float32)
    rolled_halo = np.zeros((TOK, HALO), np.float32)
    first_rows = np.zeros((HALO, TOK), np.float32)
    last_rows = np.zeros((HALO, TOK), np.float32)
    for m in range(2):
        for w in range(2):
            for y in range(7):
                for x in range(7):
                    t = (m * 2 + w) * SPOT + y * 7 + x
                    col = w * 7 + x
                    plain[t, nat(m, y, col)] = 1
                    if y < SHIFT:
                        first_rows[halo(m, y, col), t] = 1
                    col = (col + SHIFT) % 14
                    if y + SHIFT < 7:
                        rolled[t, nat(m, y + SHIFT, col)] = 1
                    else:
                        rolled_halo[t, halo(m, y + SHIFT - 7, col)] = 1
                        last_rows[halo(m, y + SHIFT - 7, col), t] = 1
    return plain, rolled, rolled_halo, first_rows, last_rows


PLAIN, ROLLED, ROLLED_HALO, FIRST_ROWS, LAST_ROWS = _places()
ROLL = ROLLED @ PLAIN.T
PLAIN_HALO = np.zeros((TOK, HALO), np.float32)
for _r, _t in zip(*np.nonzero(FIRST_ROWS)):
    PLAIN_HALO[_t, _r] = 1


def _pairs():
    rel = np.full((SPOT, SPOT), -1)
    rows = np.zeros((SPOT, GROUPS * SPOT), np.float32)
    cols = np.zeros((SPOT, GROUPS * SPOT), np.float32)
    for a in range(49):
        for b in range(49):
            rel[a, b] = (a // 7 - b // 7 + 6) * 13 + a % 7 - b % 7 + 6
            for h in range(GROUPS):
                if (a // 7 >= 4) != (b // 7 >= 4):
                    rows[a, h * SPOT + b] = -100.0
                if (a % 7 >= 4) != (b % 7 >= 4):
                    cols[a, h * SPOT + b] = -100.0
    return rel, rows, cols


REL, MASK_ROWS, MASK_COLS = _pairs()
REL_HOT = (REL[None] == np.arange(192)[:, None, None]).astype(np.float32)
PACKED_REL = np.concatenate([REL[:32], REL[32:]], axis=1)
PACKED_HOT = (PACKED_REL.reshape(-1, 1) == np.arange(256)[None]).astype(np.float32)
EDGE = np.where(np.tile(np.arange(SPOT), GROUPS) < 49, 0.0, -1e30).astype(np.float32)
HEAD_LANES = np.repeat(np.kron(np.eye(GROUPS), np.ones((1, HD))), SPOT, axis=0).astype(np.float32)
SEGMENT = np.kron(np.eye(2), np.ones((SPOT, SPOT))).astype(np.float32)


def const(x):
    return jnp.asarray(x, BF)


def dot(a, b):
    return lax.dot_general(a, b, (((1,), (0,)), ((), ())), preferred_element_type=F32)


def dot_nt(a, b):
    return lax.dot_general(a, b, (((1,), (1,)), ((), ())), preferred_element_type=F32)


def dot_tn(a, b):
    return lax.dot_general(a, b, (((0,), (0,)), ((), ())), preferred_element_type=F32)


def halves(x):
    high = x.astype(BF)
    return high, (x - high.astype(F32)).astype(BF)


def place(hot, x):
    high = x.astype(BF)
    rest = x - high.astype(F32)
    mid = rest.astype(BF)
    low = (rest - mid.astype(F32)).astype(BF)
    return dot(hot, high) + dot(hot, mid) + dot(hot, low)


def segment_sum(x, seg):
    high, low = halves(x)
    parts = [
        dot(high[:, k : k + 128], seg) + dot(low[:, k : k + 128], seg) for k in (0, 128)
    ]
    return jnp.concatenate(parts, axis=1)


def segment_max(s):
    lane = lax.broadcasted_iota(jnp.int32, (SPOT, 128), 1)
    left = lane < SPOT
    parts = []
    for k in (0, 128):
        part = s[:, k : k + 128]
        one = jnp.max(jnp.where(left, part, -3e38), axis=1, keepdims=True)
        two = jnp.max(jnp.where(left, -3e38, part), axis=1, keepdims=True)
        parts.append(jnp.where(left, one, two))
    return jnp.concatenate(parts, axis=1)


def norm_parts(x):
    center = x - jnp.mean(x, axis=-1, keepdims=True)
    r = lax.rsqrt(jnp.mean(center * center, axis=-1, keepdims=True) + EPS)
    return center * r, r


def norm_back(dh, xhat, r, gain):
    e = dh * gain
    return r * (
        e
        - jnp.mean(e, axis=-1, keepdims=True)
        - xhat * jnp.mean(e * xhat, axis=-1, keepdims=True)
    )


def four(x, lanes):
    return jnp.concatenate([x] * GROUPS, axis=0) * lanes


def fold(x, lanes):
    x = x * lanes
    return x[:64] + x[64:128] + x[128:192] + x[192:]


def column_sum(x):
    return jnp.sum(x, axis=0, keepdims=True)


def me_shard():
    return lax.axis_index("shard")


def row_at(i, rows):
    return pl.ds(pl.multiple_of(i * rows, 32), 32)


def gathered(blocks):
    return [
        [
            (half[2 * core + y], 32 * m, 4 * m + 2 * y + core)
            for core in range(2)
            for y in range(2)
            for m in range(4)
        ]
        for half in (blocks[:4], blocks[4:])
    ]


def attn_copies(blocks, w, sem):
    me = me_shard()
    return [
        pltpu.make_async_copy(
            ref.at[row : row + 32, :ATTN],
            w.at[row_at(lax.bitwise_xor(me, whose), 32), :],
            sem.at[n],
        )
        for n, (ref, row, whose) in enumerate(gathered(blocks)[0])
    ]


def ff_copies(blocks, w, sem):
    out = []
    me = me_shard()
    first = SPLIT - ATTN
    for part, half in enumerate(gathered(blocks)):
        for n, (ref, row, whose) in enumerate(half):
            rows = row_at(lax.bitwise_xor(me, whose), 32)
            source, to = (ref.at[row : row + 32, ATTN:], w.at[rows, :first])
            if part == 1:
                source, to = ref.at[row : row + 32, :], w.at[rows, first:]
            out.append(pltpu.make_async_copy(source, to, sem.at[n, part]))
    return out


def regrouped(values, back):
    lane = lax.broadcasted_iota(jnp.int32, (32, 128), 1)
    out = []
    for group in range(16):
        total = None
        for part in range(4):
            if back:
                source, shift = 4 * part + group // 4, 32 * part - 32 * (group % 4)
            else:
                source, shift = 4 * (group % 4) + part, 32 * part - 32 * (group // 4)
            piece = values[:, 128 * source : 128 * source + 128]
            if shift % 128:
                piece = pltpu.roll(piece, shift % 128, 1)
            total = piece if part == 0 else jnp.where(lane < 32 * part, total, piece)
        out.append(total)
    return out


def share_copies(grads, mine, theirs, sem):
    core = lax.rem(me_shard(), 2)
    out = []
    for q in range(8):
        for n, (target, bit) in enumerate(((mine, core), (theirs, 1 - core))):
            at = pl.multiple_of((2 * q + bit) * 32, 32)
            out.append(
                pltpu.make_async_copy(
                    grads.at[pl.ds(at, 32), :],
                    target.at[32 * q : 32 * q + 32, :],
                    sem.at[q, n],
                )
            )
    return out


def pack_kernel(*refs):
    qkv_w, proj, fc1, fc2, gain, shift, qkv_b, out_b, fc1_b, table = refs[:10]
    outs, stack, wide, sem = refs[10:12], refs[12], refs[13], refs[14]
    copies = []
    for level in range(2):
        out = outs[level]
        pairs = [
            (qkv_w.at[level], out.at[:, : 3 * C]),
            (proj.at[level], out.at[:, 3 * C : ATTN]),
            (fc1.at[level], wide.at[level]),
        ]
        for j in range(4):
            at = ATTN + MLP + 512 * j
            pairs.append((fc2.at[level, 32 * j : 32 * j + 32, :], out.at[:, at : at + 512]))
        copies += [
            pltpu.make_async_copy(a, b, sem.at[level, n]) for n, (a, b) in enumerate(pairs)
        ]
    for c in copies:
        c.start()
    stack[...] = jnp.zeros((SMALL, SMALL), F32)
    for level in range(2):
        for n, ref in enumerate((gain, shift, qkv_b, out_b)):
            at = 8 * level + 2 * n
            stack[at : at + 2, :32] = ref[level].astype(F32)
        for j in range(4):
            at = 16 + 4 * level + j
            stack[at : at + 1, :32] = fc1_b[level : level + 1, 32 * j : 32 * j + 32].astype(F32)
        for j in range(6):
            at = 24 + 6 * level + j
            width = min(32, 169 - 32 * j)
            stack[at : at + 1, :width] = table[level : level + 1, 32 * j : 32 * j + width].astype(F32)
    outs[0][:, 2 * SPLIT :] = stack[...].T[:32, :].astype(BF)
    for c in copies:
        c.wait()
    for level in range(2):
        for n, group in enumerate(regrouped(wide[level].astype(F32), False)):
            at = ATTN + 128 * n
            outs[level][:, at : at + 128] = group.astype(BF)


def join_kernel(*refs):
    blocks, outs = refs[:4], refs[4:]
    for m in range(4):
        for n, out in enumerate(outs):
            cols = slice(SPLIT * n, SPLIT * n + out.shape[1])
            out[32 * m : 32 * m + 32, :] = blocks[m][:, cols]


def params_kernel(small, out, scratch):
    me = me_shard()
    for t in range(16):
        at = 128 * (t // 2 % 2) + 256 * (t % 2) + 32 * (t // 4)
        scratch[row_at(lax.bitwise_xor(me, t), 32), :] = small[at : at + 32, :].astype(F32)
    out[...] = scratch[...].T


def attn_forward_kernel(level, *refs):
    if level == 0:
        img, spread = refs[:2]
        refs = refs[2:]
    else:
        own, halo, spread_halo, mask_rows, mask_cols = refs[:5]
        refs = refs[5:]
    params, bias, lanes_ref, seg_ref = refs[:4]
    blocks, refs = refs[4:-8], refs[-8:]
    x_out, x1_out, h_out, qkv, a_out, o_out, w, sem = refs
    copies = attn_copies(blocks, w, sem)
    for c in copies:
        c.start()
    if level == 0:
        x = dot(spread[...], img[...])
    else:
        x = own[...] + dot(spread_halo[...], halo[...])
    x_out[...] = x
    row = 8 * level
    xhat, _ = norm_parts(x)
    h = (xhat * params[row : row + 1, :] + params[row + 2 : row + 3, :]).astype(BF)
    h_out[...] = h
    for c in copies:
        c.wait()
    qkv[:, :C] = (dot(h, w[:, :C]) + params[row + 4 : row + 5, :]).astype(BF)
    qkv[:, C : 2 * C] = dot(h, w[:, C : 2 * C]).astype(BF)
    qkv[:, 2 * C :] = (dot(h, w[:, 2 * C : 3 * C]) + params[row + 5 : row + 6, :]).astype(BF)
    lanes = lanes_ref[...]
    seg = seg_ref[...]
    if level == 1:
        last = (lax.axis_index("seq") == 7).astype(F32)
        row_mask = mask_rows[...] * last
        both_mask = jnp.minimum(row_mask, mask_cols[...])
    groups = range(GROUPS)
    for window in range(WINDOWS):
        rows = slice(window * SPOT, (window + 1) * SPOT)
        q, k, v = (
            [qkv[rows, C * n + 128 * g : C * n + 128 * g + 128] for g in groups] for n in range(3)
        )
        s = [dot_nt(q[g], four(k[g], lanes)) * SCALE + bias[g] for g in groups]
        if level == 1:
            mask = both_mask if window % 2 else row_mask
            s = [t + mask for t in s]
        top = [segment_max(t) for t in s]
        e = [jnp.exp(s[g] - top[g]) for g in groups]
        total = [segment_sum(t, seg) for t in e]
        a = [e[g] / total[g] for g in groups]
        o = [dot(a[g].astype(BF), four(v[g], lanes)).astype(BF) for g in groups]
        for g in groups:
            a_out[window * GROUPS + g] = a[g]
            o_out[rows, 128 * g : 128 * g + 128] = o[g]
    x1_out[...] = x + (dot(o_out[...], w[:, 3 * C :]) + params[row + 6 : row + 7, :])


def ff_forward_kernel(level, *refs):
    x1_ref, params, fc1_b, send_hot, out_hot = refs[:5]
    refs = refs[5:]
    blocks, refs = refs[:-7], refs[-7:]
    result, send, h2_out, g_out, gp_out, w, sem = refs
    copies = ff_copies(blocks, w, sem)
    for c in copies:
        c.start()
    row = 8 * level
    x1 = x1_ref[...]
    xhat, _ = norm_parts(x1)
    h2 = (xhat * params[row + 1 : row + 2, :] + params[row + 3 : row + 4, :]).astype(BF)
    h2_out[...] = h2
    for c in copies:
        c.wait()
    total = x1 + params[row + 7 : row + 8, :]
    for n in range(4):
        cols = slice(512 * n, 512 * n + 512)
        f = dot(h2, w[:, cols]) + fc1_b[:, cols]
        phi = 0.5 * (1.0 + lax.erf(f * (0.5**0.5)))
        g = (f * phi).astype(BF)
        g_out[:, cols] = g
        gp_out[:, cols] = (phi + f * (jnp.exp(f * f * -0.5) * 0.3989422804014327)).astype(BF)
        total = total + dot(g, w[:, MLP + 512 * n : MLP + 512 * n + 512])
    send[...] = dot(send_hot[...], total.astype(BF)).astype(BF)
    result[...] = place(out_hot[...], total)


def ff_backward_kernel(level, *refs):
    if level == 1:
        cot, halo, spread, spread_halo = refs[:4]
        refs = refs[4:]
    else:
        own, halo, spread_halo = refs[:3]
        refs = refs[3:]
    x1_ref, h2_ref, g_ref, gp_ref, params, pick = refs[:6]
    blocks, refs = refs[6:-9], refs[-9:]
    g1_out, rows_out, col_out, mine, theirs, w, grads, sem, share_sem = refs
    copies = ff_copies(blocks, w, sem)
    for c in copies:
        c.start()
    if level == 1:
        g2 = dot(spread[...], cot[...]) + dot(spread_halo[...], halo[...])
    else:
        g2 = own[...] + dot(spread_halo[...], halo[...])
    dz = g2.astype(BF)
    row = 8 * level
    xhat, r = norm_parts(x1_ref[...])
    h2 = h2_ref[...]
    ones = jnp.ones((TOK, 128), BF)
    for n in range(4):
        cols = slice(512 * n, 512 * n + 512)
        grads[:, MLP + 512 * n : MLP + 512 * n + 512] = dot_tn(g_ref[:, cols], dz).astype(BF)
    for c in copies:
        c.wait()
    dh2 = jnp.zeros((TOK, C), F32)
    bias = jnp.zeros((C, SMALL), F32)
    lane = lax.broadcasted_iota(jnp.int32, (C, SMALL), 1)
    for n in range(4):
        cols = slice(512 * n, 512 * n + 512)
        back = dot_nt(dz, w[:, MLP + 512 * n : MLP + 512 * n + 512])
        df = (back * gp_ref[:, cols].astype(F32)).astype(BF)
        grads[:, cols] = dot_tn(h2, df).astype(BF)
        bias = jnp.where(lane == 8 + n, dot_tn(df, ones), bias)
        dh2 = dh2 + dot_nt(df, w[:, cols])
    col_out[...] = bias
    shares = share_copies(grads, mine, theirs, share_sem)
    for c in shares:
        c.start()
    g1_out[...] = g2 + norm_back(dh2, xhat, r, params[row + 1 : row + 2, :])
    rows_out[...] = jnp.zeros((8, C), F32)
    rows_out[1:2, :] = column_sum(dh2 * xhat)
    rows_out[3:4, :] = column_sum(dh2)
    rows_out[7:8, :] = column_sum(dz.astype(F32))
    for c in shares:
        c.wait()


def attn_backward_kernel(level, *refs):
    g1_ref, x_ref, h_ref, qkv, a_ref, o_ref, params, rows_ref, col_ref = refs[:9]
    lanes_ref, seg_ref, back_hot = refs[9:12]
    refs = refs[12:]
    if level == 1:
        send_hot = refs[0]
        refs = refs[1:]
    blocks, refs = refs[:8], refs[8:]
    if level == 1:
        send = refs[0]
        refs = refs[1:]
    back, mine, theirs, w, grads, d_qkv, stack, ds_all, sem, share_sem = refs
    copies = attn_copies(blocks, w, sem)
    for c in copies:
        c.start()
    row = 8 * level
    g1 = g1_ref[...]
    dy = g1.astype(BF)
    grads[:, 3 * C : 4 * C] = dot_tn(o_ref[...], dy).astype(BF)
    stack[...] = jnp.zeros((SMALL, C), F32)
    stack[0:8, :] = rows_ref[...]
    stack[6:7, :] = column_sum(dy.astype(F32))
    xhat, r = norm_parts(x_ref[...])
    lanes = lanes_ref[...]
    lanes_f = lanes.astype(F32)
    seg = seg_ref[...]
    for c in copies:
        c.wait()
    do_all = dot_nt(dy, w[:, 3 * C :]).astype(BF)
    lane = lax.broadcasted_iota(jnp.int32, (32, 128), 1)
    groups = range(GROUPS)
    for window in range(WINDOWS):
        rows = slice(window * SPOT, (window + 1) * SPOT)
        q, k, v = (
            [qkv[rows, C * n + 128 * g : C * n + 128 * g + 128] for g in groups] for n in range(3)
        )
        do = [do_all[rows, 128 * g : 128 * g + 128] for g in groups]
        a = [a_ref[window * GROUPS + g] for g in groups]
        da = [dot_nt(do[g], four(v[g], lanes)) for g in groups]
        o = [o_ref[rows, 128 * g : 128 * g + 128] for g in groups]
        parts = [halves(do[g].astype(F32) * o[g].astype(F32)) for g in groups]
        total = [dot_nt(high, lanes) + dot_nt(low, lanes) for high, low in parts]
        dv = [fold(dot_tn(a[g].astype(BF), do[g]), lanes_f) for g in groups]
        ds = [(a[g] * (da[g] - total[g])).astype(BF) for g in groups]
        dq = [dot(ds[g], four(k[g], lanes)) * SCALE for g in groups]
        dk = [fold(dot_tn(ds[g], q[g]), lanes_f) * SCALE for g in groups]
        for g in groups:
            at = 128 * g
            d_qkv[rows, at : at + 128] = dq[g].astype(BF)
            d_qkv[rows, C + at : C + at + 128] = dk[g].astype(BF)
            d_qkv[rows, 2 * C + at : 2 * C + at + 128] = dv[g].astype(BF)
            if window == 0:
                ds_all[g] = ds[g].astype(F32)
            else:
                ds_all[g] = ds_all[g] + ds[g].astype(F32)
    for g in groups:
        ds_sum = ds_all[g]
        for pair in range(2):
            top = ds_sum[:32, 128 * pair : 128 * pair + 128]
            low = ds_sum[32:, 128 * pair : 128 * pair + 128]
            even = jnp.where(lane < 64, top, pltpu.roll(low, 64, 1))
            odd = jnp.where(lane < 64, pltpu.roll(top, 64, 1), low)
            head = 4 * g + 2 * pair
            grads[32 * head : 32 * head + 32, ATTN_IN:] = even.astype(BF)
            grads[32 * head + 32 : 32 * head + 64, ATTN_IN:] = odd.astype(BF)
    h = h_ref[...]
    for n in range(3):
        cols = slice(C * n, C * n + C)
        grads[:, cols] = dot_tn(h, d_qkv[:, cols]).astype(BF)
    stack[4:5, :] = column_sum(d_qkv[:, :C].astype(F32))
    stack[5:6, :] = column_sum(d_qkv[:, 2 * C :].astype(F32))
    dh = dot_nt(d_qkv[...], w[:, : 3 * C])
    stack[0:1, :] = column_sum(dh * xhat)
    stack[2:3, :] = column_sum(dh)
    grads[:, ATTN:ATTN_IN] = (stack[...].T + col_ref[...]).astype(BF)
    shares = share_copies(grads, mine, theirs, share_sem)
    for c in shares:
        c.start()
    total = g1 + norm_back(dh, xhat, r, params[row : row + 1, :])
    if level == 1:
        send[...] = dot(send_hot[...], total.astype(BF)).astype(BF)
    back[...] = place(back_hot[...], total)
    for c in shares:
        c.wait()


def pair_kernel(x_first, *refs):
    shares, outs = refs[:4], refs[4:]
    chip = lax.div(me_shard(), 2)
    for m in range(4):
        to = slice(32 * m, 32 * m + 32)
        for y in range(2):
            rows = row_at(lax.bitwise_xor(chip, 2 * m + y), 32)
            for mine, other, start, width in (
                (shares[0], shares[1], 0, FF),
                (shares[2], shares[3], FF, ATTN_OUT),
            ):
                total = (mine[rows, :].astype(F32) + other[rows, :].astype(F32)).astype(BF)
                if x_first:
                    outs[m][32 * y : 32 * y + 32, start : start + width] = total
                    continue
                if y == 0:
                    outs[0][to, start : start + width] = total
                    continue
                cut = max(0, min(width, SHARE - start))
                if cut:
                    outs[1][to, start : start + cut] = total[:, :cut]
                if cut < width:
                    at = start + cut - SHARE
                    outs[2][to, at : at + width - cut] = total[:, cut:]


def added(refs):
    return functools.reduce(jnp.add, [r[...].astype(F32) for r in refs])


def middle_x_kernel(*refs):
    pieces, (own, left, right) = refs[:4], refs[4:]
    total = added(pieces).astype(BF)
    own[...] = total[:32, :]
    left[...] = total[32:, :SHARE]
    right[...] = total[32:, SHARE:]


def middle_kernel(own, left, right, *outs):
    for m in range(4):
        rows = slice(32 * m, 32 * m + 32)
        for part, cols in ((left, slice(0, SHARE)), (right, slice(SHARE, 2 * SHARE))):
            total = own[rows, cols].astype(F32) + part[rows, :].astype(F32)
            outs[m][:, cols] = total.astype(BF)


def z_part(ref, k):
    p = lax.bitwise_xor(lax.div(lax.axis_index("seq"), 2), k)
    return ref.at[:, pl.ds(pl.multiple_of(p * QUARTER, 128), QUARTER)]


def split_kernel(*refs):
    pieces, outs, total, sem = refs[:-6], refs[-6:-2], refs[-2], refs[-1]
    if len(pieces) == 4:
        total[:, : 2 * SHARE] = added(pieces).astype(BF)
    else:
        own, left, right = pieces
        total[:, :SHARE] = (own[:, :SHARE].astype(F32) + left[...].astype(F32)).astype(BF)
        total[:, SHARE : 2 * SHARE] = (own[:, SHARE:].astype(F32) + right[...].astype(F32)).astype(BF)
    total[:, 2 * SHARE :] = jnp.zeros((32, TOTAL - 2 * SHARE), BF)
    copies = [pltpu.make_async_copy(z_part(total, k), outs[k], sem.at[k]) for k in range(4)]
    for c in copies:
        c.start()
    for c in copies:
        c.wait()


def finish_kernel(*refs):
    pieces, hot = refs[:8], refs[8]
    gain, shift, qkv_w, qkv_b, table, proj, out_b, fc1, fc1_b, fc2 = refs[9:19]
    scratch, sem = refs[19:]
    copies = [
        pltpu.make_async_copy(
            pieces[4 * level + k], z_part(scratch.at[level], k), sem.at[level, k]
        )
        for level in range(2)
        for k in range(4)
    ]
    for c in copies:
        c.start()
    for c in copies:
        c.wait()
    total = scratch[...]
    for level in range(2):
        for n, group in enumerate(regrouped(total[level, :, :MLP].astype(F32), True)):
            fc1[level, :, 128 * n : 128 * n + 128] = group
        for j in range(4):
            fc2[level, 32 * j : 32 * j + 32, :] = total[
                level, :, MLP + 512 * j : MLP + 512 * j + 512
            ].astype(F32)
        qkv_w[level] = total[level, :, FF : FF + 3 * C].astype(F32)
        proj[level] = total[level, :, FF + 3 * C : FF + 4 * C].astype(F32)
        small = total[level, :, FF + ATTN : FF + ATTN_IN].astype(F32).T
        gain[level] = small[0:2, :]
        shift[level] = small[2:4, :]
        qkv_b[level] = small[4:6, :]
        out_b[level] = small[6:8, :]
        fc1_b[level : level + 1, :] = jnp.concatenate(
            [small[8 + j : 9 + j, :] for j in range(4)], axis=1
        )
        ds = total[level, :, FF + ATTN_IN : FF + ATTN_OUT]
        flat = jnp.concatenate([ds[r : r + 1, :] for r in range(32)], axis=1)
        sums = dot(jnp.broadcast_to(flat.astype(F32), (16, 4096)).astype(BF), hot[...])
        table[level] = sums[0:1, :169]


def sds(shape, dtype):
    return jax.ShapeDtypeStruct(shape, dtype)


def call(kernel, ins, outs, scratch, args, flops=0, room=24):
    return pl.pallas_call(
        kernel,
        out_shape=tuple(s for s, _ in outs),
        in_specs=ins,
        out_specs=tuple(m for _, m in outs),
        scratch_shapes=scratch,
        compiler_params=pltpu.CompilerParams(vmem_limit_bytes=room * 1024 * 1024),
        cost_estimate=pl.CostEstimate(flops=8 * flops, bytes_accessed=8000000, transcendentals=0),
    )(*args)


def shard_permute(x, k):
    return lax.ppermute(x, "shard", [(i, i ^ k) for i in range(16)])


def core_permute(x):
    return shard_permute(x, 1)


def y_permute(x):
    return shard_permute(x, 2)


def y_shift(x, by):
    pairs = []
    for z in range(4):
        for y in range(4):
            to = (y + by) % 4
            for rest in range(8):
                place = rest // 2 * 4 + rest % 2
                pairs.append(
                    (
                        (2 * z + y // 2) * 16 + place + 2 * (y % 2),
                        (2 * z + to // 2) * 16 + place + 2 * (to % 2),
                    )
                )
    return lax.ppermute(x, ("seq", "shard"), pairs)


def x_permutes(pieces):
    return [shard_permute(p, 4 * k) for k, p in enumerate(pieces, 1)]


def seq_permute(x, k):
    return lax.ppermute(x, "seq", [(i, i ^ k) for i in range(8)])


def z_permutes(pieces):
    return [seq_permute(p, 2 * k) for k, p in enumerate(pieces, 1)]


def passed_along(x, by):
    return lax.ppermute(x, "seq", [(i, (i + by) % 8) for i in range(8)])


def gather_x(block):
    return [block] + x_permutes([block] * 3)


def joined(blocks):
    widths = [SPLIT, SPLIT, SMALL][: -(-blocks[0].shape[1] // SPLIT)]
    return call(
        join_kernel, [VM] * 4, [(sds((128, w), BF), VM) for w in widths], [], tuple(blocks)
    )


def gather_y(left, right):
    return [left, y_shift(left, 1)], [right, y_shift(right, -1)]


def with_other_core(blocks):
    return blocks + [core_permute(b) for b in blocks]


def pair_sums(shares, x_first):
    outs = [(sds((128, 2 * SHARE), BF), VM)] + [(sds((128, SHARE), BF), VM)] * 2
    if x_first:
        outs = [(sds((64, 2 * SHARE), BF), VM)] * 4
    return call(functools.partial(pair_kernel, x_first), [VM] * 4, outs, [], shares)


def scatter_x(pieces):
    return [pieces[0]] + x_permutes(pieces[1:])


def middle_x_sums(arrived):
    outs = [(sds((32, 2 * SHARE), BF), VM)] + [(sds((32, SHARE), BF), VM)] * 2
    return call(middle_x_kernel, [VM] * 4, outs, [], arrived)


def scatter_y(pieces):
    own, left, right = pieces
    return own, y_shift(left, 1), y_shift(right, -1)


def middle_sums(arrived):
    return call(middle_kernel, [VM] * 3, [(sds((32, 2 * SHARE), BF), VM)] * 4, [], arrived)


def end_sums(arrived):
    return call(
        split_kernel,
        [VM] * len(arrived),
        [(sds((32, QUARTER), BF), HB)] * 4,
        [pltpu.VMEM((32, TOTAL), BF), pltpu.SemaphoreType.DMA((4,))],
        arrived,
    )


def total_of(parts):
    return functools.reduce(jnp.add, [p.astype(F32) for p in parts]).astype(BF)


def seq_sum(pieces):
    own = total_of([pieces[0]] + z_permutes(pieces[1:]))
    own = total_of([own, seq_permute(own, 1)])
    return [own] + z_permutes([own] * 3)


def on_device(
    images,
    norm_gain,
    norm_shift,
    qkv_weight,
    qkv_bias,
    rel_table,
    proj_weight,
    out_bias,
    fc1_weight,
    fc1_bias,
    fc2_weight,
    cotangent,
):
    def natural(x):
        return jnp.pad(x, ((0, 0), (0, 0), (0, 2), (0, 0))).reshape(-1, C)

    block_one, block_two = call(
        pack_kernel,
        [FAR] * 4 + [VM] * 6,
        [(sds((32, 2 * SPLIT + SMALL), BF), VM), (sds((32, 2 * SPLIT), BF), VM)],
        [
            pltpu.VMEM((SMALL, SMALL), F32),
            pltpu.VMEM((2, 32, MLP), BF),
            pltpu.SemaphoreType.DMA((2, 7)),
        ],
        (
            qkv_weight,
            proj_weight,
            fc1_weight,
            fc2_weight,
            norm_gain,
            norm_shift,
            qkv_bias,
            out_bias,
            fc1_bias,
            rel_table.reshape(2, 169),
        ),
        room=60,
    )
    cot_halo = passed_along(natural(cotangent[:, :SHIFT]), -1)
    cot_halo, block_two = lax.optimization_barrier((cot_halo, block_two))
    row_one, cot_halo = lax.optimization_barrier((gather_x(block_one), cot_halo))
    left_one, right_one, small = joined(row_one)
    left_one, right_one = gather_y(left_one, right_one)
    for permute in (y_permute, core_permute):
        small = jnp.concatenate([small, permute(small)], axis=0)
    row_two, _, _ = lax.optimization_barrier((gather_x(block_two), left_one, right_one))
    left_two, right_two = gather_y(*joined(row_two))

    img = natural(images)
    cot = natural(cotangent)

    (params,) = call(params_kernel, [VM], [(sds((SMALL, C), F32), VM)], [pltpu.VMEM((C, SMALL), F32)], (small,))
    tables = params[24:36].reshape(2, 6, HEADS, 32).transpose(0, 2, 1, 3).reshape(32, 192)
    bias_all = lax.dot_general(
        tables.astype(BF),
        const(REL_HOT),
        (((1,), (0,)), ((), ())),
        preferred_element_type=F32,
    )
    bias_all = bias_all.reshape(2, GROUPS, 4, SPOT, SPOT).transpose(0, 1, 3, 2, 4)
    bias_all = bias_all.reshape(2, GROUPS, SPOT, 256) + jnp.asarray(EDGE)
    fc1_b = params[16:24].reshape(2, 1, MLP)

    lanes = const(HEAD_LANES)
    seg = const(SEGMENT)
    tokens = sds((TOK, C), F32)
    tokens_low = sds((TOK, C), BF)
    hidden_low = sds((TOK, MLP), BF)
    halo_low = sds((HALO, C), BF)

    def attn_forward(level, lead, blocks):
        outs = [
            (tokens, VM),
            (tokens, VM),
            (tokens_low, VM),
            (sds((TOK, 3 * C), BF), VM),
            (sds((16, SPOT, 256), F32), VM),
            (tokens_low, VM),
        ]
        return call(
            functools.partial(attn_forward_kernel, level),
            [VM] * (len(lead) + 4) + [HB] * len(blocks),
            outs,
            [pltpu.VMEM((C, ATTN), BF), pltpu.SemaphoreType.DMA((16,))],
            tuple(lead) + (params, bias_all[level], lanes, seg) + tuple(blocks),
            flops=2 * TOK * C * ATTN,
        )

    def ff_scratch():
        return [pltpu.VMEM((C, FF), BF)]

    def ff_forward(level, x1, blocks):
        lead = (x1, params, fc1_b[level])
        if level == 0:
            lead += (const(FIRST_ROWS), const(ROLL))
            out = tokens
        else:
            lead += (const(LAST_ROWS), const(ROLLED.T))
            out = sds((NAT, C), F32)
        return call(
            functools.partial(ff_forward_kernel, level),
            [VM] * len(lead) + [HB] * len(blocks),
            [(out, VM), (halo_low, VM), (tokens_low, VM), (hidden_low, VM), (hidden_low, VM)],
            ff_scratch() + [pltpu.SemaphoreType.DMA((16, 2))],
            lead + tuple(blocks),
            flops=4 * TOK * C * MLP,
        )

    def ff_backward(level, lead, saved, blocks):
        shares = sds((256, FF), BF)
        return call(
            functools.partial(ff_backward_kernel, level),
            [VM] * (len(lead) + 6) + [HB] * len(blocks),
            [
                (tokens, VM),
                (sds((8, C), F32), VM),
                (sds((C, SMALL), F32), VM),
                (shares, HB),
                (shares, HB),
            ],
            ff_scratch()
            + [
                pltpu.VMEM((C, FF), BF),
                pltpu.SemaphoreType.DMA((16, 2)),
                pltpu.SemaphoreType.DMA((8, 2)),
            ],
            tuple(lead) + tuple(saved) + (params, lanes) + tuple(blocks),
            flops=8 * TOK * C * MLP,
        )

    def attn_backward(level, g1, saved, rows, cols, hots, blocks):
        shares = sds((256, ATTN_OUT), BF)
        outs = [(halo_low, VM)] if level == 1 else []
        outs.append((tokens if level == 1 else sds((NAT, C), F32), VM))
        return call(
            functools.partial(attn_backward_kernel, level),
            [VM] * (11 + len(hots)) + [HB] * len(blocks),
            outs + [(shares, HB), (shares, HB)],
            [
                pltpu.VMEM((C, ATTN), BF),
                pltpu.VMEM((C, ATTN_OUT), BF),
                pltpu.VMEM((TOK, 3 * C), BF),
                pltpu.VMEM((SMALL, C), F32),
                pltpu.VMEM((GROUPS, SPOT, 256), F32),
                pltpu.SemaphoreType.DMA((16,)),
                pltpu.SemaphoreType.DMA((8, 2)),
            ],
            (g1,) + tuple(saved) + (params, rows, cols, lanes, seg) + tuple(hots) + tuple(blocks),
            flops=4 * TOK * C * ATTN,
        )

    left_one, right_one, bias_all, fc1_b, img = lax.optimization_barrier(
        (left_one, right_one, bias_all, fc1_b, img)
    )
    all_one = with_other_core(left_one) + with_other_core(right_one)
    x_one, x1_one, *attn_saved_one = attn_forward(0, (img, const(PLAIN)), all_one)
    mid, send, *ff_saved_one = ff_forward(0, x1_one, all_one)
    halo, left_two[1], right_two[1] = lax.optimization_barrier(
        (passed_along(send, -1), left_two[1], right_two[1])
    )
    all_two = with_other_core(left_two) + with_other_core(right_two)
    lead = (
        mid,
        halo,
        const(ROLLED_HALO),
        jnp.asarray(MASK_ROWS),
        jnp.asarray(MASK_COLS),
    )
    x_two, x1_two, *attn_saved_two = attn_forward(1, lead, all_two)
    own_rows, send, *ff_saved_two = ff_forward(1, x1_two, all_two)
    returned = passed_along(send, 1)

    g1, rows, cols, mine, theirs = ff_backward(
        1,
        (cot, cot_halo, const(ROLLED), const(ROLLED_HALO)),
        (x1_two, *ff_saved_two),
        all_two,
    )
    g1, mine, theirs, returned = lax.optimization_barrier((g1, mine, theirs, returned))
    shares_two = (mine, core_permute(theirs))
    outputs = jnp.concatenate(
        [
            returned.astype(F32).reshape(2, SHIFT, 16, C),
            own_rows.reshape(2, 7, 16, C)[:, SHIFT:],
        ],
        axis=1,
    )[:, :, :14]
    send, own, mine, theirs = attn_backward(
        1,
        g1,
        (x_two, *attn_saved_two),
        rows,
        cols,
        (const(ROLL.T), const(LAST_ROWS)),
        all_two,
    )
    pieces_two = pair_sums(shares_two + (mine, core_permute(theirs)), True)
    own, pieces_two = lax.optimization_barrier((own, pieces_two))
    g1, rows, cols, mine, theirs = ff_backward(
        0,
        (own, passed_along(send, 1), const(PLAIN_HALO)),
        (x1_one, *ff_saved_one),
        all_one,
    )
    ff_shares = (mine, theirs)
    input_grad, mine, theirs = attn_backward(
        0, g1, (x_one, *attn_saved_one), rows, cols, (const(PLAIN.T),), all_one
    )
    near = [shard_permute(pieces_two[k], 4 * k) for k in (1, 3)]
    near, far, ff_shares, attn_shares = lax.optimization_barrier(
        (near, pieces_two[2], ff_shares, (mine, theirs))
    )
    arrived = [pieces_two[0], near[0], shard_permute(far, 8), near[1]]
    shares_one = [
        part for mine, theirs in (ff_shares, attn_shares) for part in (mine, core_permute(theirs))
    ]
    pieces_one = scatter_y(pair_sums(shares_one, False))
    pieces_two = middle_x_sums(arrived)
    input_grad = input_grad.reshape(2, 7, 16, C)[:, :, :14]
    pieces_one, pieces_two, outputs, input_grad = lax.optimization_barrier(
        (pieces_one, pieces_two, outputs, input_grad)
    )
    pieces_two = end_sums(scatter_y(pieces_two))
    pieces_one = end_sums(scatter_x(middle_sums(pieces_one)))
    sums_two = seq_sum(pieces_two)
    sums_one = seq_sum(pieces_one)
    shapes = [
        (2, 2, 32),
        (2, 2, 32),
        (2, 32, 3 * C),
        (2, 2, 32),
        (2, 1, 169),
        (2, 32, C),
        (2, 2, 32),
        (2, 32, MLP),
        (2, 128),
        (2, 128, C),
    ]
    grads = call(
        finish_kernel,
        [HB] * 8 + [VM],
        [(sds(shape, F32), VM) for shape in shapes],
        [pltpu.VMEM((2, 32, TOTAL), BF), pltpu.SemaphoreType.DMA((2, 4))],
        tuple(sums_one) + tuple(sums_two) + (const(PACKED_HOT),),
    )
    return (outputs, input_grad) + tuple(grads)


def solution(mesh):
    return jax.shard_map(
        on_device,
        mesh=mesh,
        in_specs=(
            P("shard", "seq", None, None),
            P(None, None, "shard"),
            P(None, None, "shard"),
            P(None, "shard", None),
            P(None, None, "shard"),
            P(None, "shard", None),
            P(None, "shard", None),
            P(None, None, "shard"),
            P(None, "shard", None),
            P(None, "shard"),
            P(None, "shard", None),
            P("shard", "seq", None, None),
        ),
        out_specs=(
            P("shard", "seq", None, None),
            P("shard", "seq", None, None),
            P(None, None, "shard"),
            P(None, None, "shard"),
            P(None, "shard", None),
            P(None, None, "shard"),
            P(None, "shard", None),
            P(None, "shard", None),
            P(None, None, "shard"),
            P(None, "shard", None),
            P(None, "shard"),
            P(None, "shard", None),
        ),
        check_vma=False,
    )
```
